32 devices in a mesh: dp: 4 (over y, core), seq: 8 (over z, x).
Axes of the slice: x: 2, y: 2, z: 4, core: 2. Of those that a mesh axis runs over, the one named last changes fastest.
Arguments:
- tokens: bfloat16 [32, 2048, 512], P('dp', 'seq'), may hold values from -6 to 6
- cotangent: bfloat16 [32, 2048, 512], P('dp', 'seq'), may hold values from -6 to 6
- lengths: int32 [32], P('dp'), may hold values from 512 to 2048, as said below
- w_qkv: float32 [512, 1536], P(('dp', 'seq')), may hold values from -0.25 to 0.25
- w_out: float32 [512, 512], P(('dp', 'seq')), may hold values from -0.375 to 0.375
- w_up: float32 [512, 2048], P(('dp', 'seq')), may hold values from -0.25 to 0.25
- w_down: float32 [2048, 512], P(('dp', 'seq')), may hold values from -0.125 to 0.125
- norm_params: float32 [4, 512], P(None, ('dp', 'seq')), may hold values from -1.5 to 2.5
- first_qkv: float32 [512, 1536], P(('dp', 'seq')), may hold values from -0.00036621094 to 0.00036621094
- first_out: float32 [512, 512], P(('dp', 'seq')), may hold values from -0.00036621094 to 0.00036621094
- first_up: float32 [512, 2048], P(('dp', 'seq')), may hold values from -0.00036621094 to 0.00036621094
- first_down: float32 [2048, 512], P(('dp', 'seq')), may hold values from -0.00036621094 to 0.00036621094
- first_norm: float32 [4, 512], P(None, ('dp', 'seq')), may hold values from -0.0009765625 to 0.0009765625
- second_qkv: float32 [512, 1536], P(('dp', 'seq')), may hold values from 3.1789144e-10 to 1.2715657e-09
- second_out: float32 [512, 512], P(('dp', 'seq')), may hold values from 3.1789144e-10 to 1.2715657e-09
- second_up: float32 [512, 2048], P(('dp', 'seq')), may hold values from 3.1789144e-10 to 1.2715657e-09
- second_down: float32 [2048, 512], P(('dp', 'seq')), may hold values from 3.1789144e-10 to 1.2715657e-09
- second_norm: float32 [4, 512], P(None, ('dp', 'seq')), may hold values from 2.861023e-09 to 1.1444092e-08
Outputs:
- activations: bfloat16 [32, 2048, 512], P('dp', 'seq')
- input_grad: float32 [32, 2048, 512], P('dp', 'seq')
- grad_norm: float32 [], replicated
- new_qkv: float32 [512, 1536], P(('dp', 'seq'))
- new_first_qkv: float32 [512, 1536], P(('dp', 'seq'))
- new_second_qkv: float32 [512, 1536], P(('dp', 'seq'))
- new_out: float32 [512, 512], P(('dp', 'seq'))
- new_first_out: float32 [512, 512], P(('dp', 'seq'))
- new_second_out: float32 [512, 512], P(('dp', 'seq'))
- new_up: float32 [512, 2048], P(('dp', 'seq'))
- new_first_up: float32 [512, 2048], P(('dp', 'seq'))
- new_second_up: float32 [512, 2048], P(('dp', 'seq'))
- new_down: float32 [2048, 512], P(('dp', 'seq'))
- new_first_down: float32 [2048, 512], P(('dp', 'seq'))
- new_second_down: float32 [2048, 512], P(('dp', 'seq'))
- new_norm: float32 [4, 512], P(None, ('dp', 'seq'))
- new_first_norm: float32 [4, 512], P(None, ('dp', 'seq'))
- new_second_norm: float32 [4, 512], P(None, ('dp', 'seq'))
The draws below stay inside these ranges and needn't reach their ends.
Inputs may be any that keep to these rules, and one draw needn't show every extreme that they name: `lengths`: in each group of 8 consecutive items one item has length 2048.
All inputs are finite; a program needn't handle non-finite values.
Results may differ from the reference program's by a relative error of at most 0.0086.
Values may be sent and summed in bfloat16 or wider, within the bound.
A program may use at most 192 MiB of HBM per device.

```python
import math
import jax
import jax.numpy as jnp
from jax import lax

D = 512
HEADS = 8
HEAD_DIM = 64
FF = 2048
SPAN = 128
ITEMS_DEV = 8
STEP = 10
SPANS = 16
SEQLEN = 2048
ITEMS = 32


def draw_tokens(key, part):
    key = jax.random.fold_in(key, 11)
    key_one, key_two = jax.random.split(key)
    rough_part = 0.6 * jax.random.normal(key_one, (ITEMS, SPANS, SPAN, D), jnp.float32)
    common = 0.8 * jax.random.normal(key_two, (ITEMS, SPANS, 1, D), jnp.float32)
    joined = jnp.clip(rough_part + common, -6.0, 6.0)
    return joined.reshape(ITEMS, SEQLEN, D).astype(jnp.bfloat16)


def draw_lengths(key, part):
    key = jax.random.fold_in(key, 5)
    key_one, key_two = jax.random.split(key)
    draw_len = jax.random.randint(key_one, (ITEMS,), SEQLEN // 4, SEQLEN + 1, dtype=jnp.int32)
    groups = ITEMS // ITEMS_DEV
    chosen = jax.random.randint(key_two, (groups,), 0, ITEMS_DEV, dtype=jnp.int32)
    index_all = jnp.arange(ITEMS, dtype=jnp.int32)
    is_full = index_all % ITEMS_DEV == jnp.repeat(chosen, ITEMS_DEV)
    return jnp.where(is_full, SEQLEN, draw_len).astype(jnp.int32)


def draw_norm_params(key, part):
    key = jax.random.fold_in(key, 13)
    key_one, key_two = jax.random.split(key)
    ramp_line = jnp.arange(D, dtype=jnp.float32) / D
    gain_rows = (0.5 + ramp_line) * jnp.exp(0.2 * jax.random.uniform(key_one, (2, D), jnp.float32, -1.0, 1.0))
    shifts = jnp.clip(0.3 * jax.random.normal(key_two, (2, D), jnp.float32), -1.5, 1.5)
    return jnp.stack([gain_rows[0], shifts[0], gain_rows[1], shifts[1]]).astype(jnp.float32)


def levels(own_key, dims, pieces, smallest, high):
    gain = 1.0
    for axis_at, shards_of in pieces:
        draws = jax.random.uniform(jax.random.fold_in(jax.random.fold_in(own_key, 6), axis_at), (shards_of,), jnp.float32, smallest / len(pieces), high / len(pieces))
        gain = gain * jnp.repeat(jnp.exp(draws), dims[axis_at] // shards_of).reshape((-1,) + (1,) * (len(dims) - 1 - axis_at))
    return gain


def normal_values(rng, dims, width, most, cuts=(), kind=jnp.bfloat16):
    level = levels(rng, dims, cuts, -0.22, 0.18) if cuts else 1.0
    drawn = jax.random.normal(rng, dims, jnp.float32) * width * level
    return jnp.minimum(jnp.maximum(drawn, -most), most).astype(kind)


def setup_inputs(seed: int = 0) -> dict:
    keys = jax.random.split(jax.random.key(seed), 19)
    tokens = draw_tokens(jax.random.fold_in(keys[18], 71), 0)
    cotangent = normal_values(keys[1], (ITEMS, SEQLEN, D), 1.0, 6.0, ((0, 4), (1, 8)))
    lengths = draw_lengths(jax.random.fold_in(keys[18], 71), 0)
    w_qkv = normal_values(keys[3], (D, 3 * D), D ** -0.5, 0.25, ((0, 32),), jnp.float32)
    w_out = normal_values(keys[4], (D, D), (D // 2) ** -0.5, 0.375, ((0, 32),), jnp.float32)
    w_up = normal_values(keys[5], (D, FF), D ** -0.5, 0.25, ((0, 32),), jnp.float32)
    w_down = normal_values(keys[6], (FF, D), FF ** -0.5, 0.125, ((0, 32),), jnp.float32)
    norm_params = draw_norm_params(jax.random.fold_in(keys[18], 71), 0)
    first_qkv = normal_values(keys[8], (D, 3 * D), (0.11 * (4 * D * D + 2 * D * FF) ** -0.5), 0.00036621094, ((0, 32),), jnp.float32)
    first_out = normal_values(keys[9], (D, D), (0.11 * (4 * D * D + 2 * D * FF) ** -0.5), 0.00036621094, ((0, 32),), jnp.float32)
    first_up = normal_values(keys[10], (D, FF), (0.11 * (4 * D * D + 2 * D * FF) ** -0.5), 0.00036621094, ((0, 32),), jnp.float32)
    first_down = normal_values(keys[11], (FF, D), (0.11 * (4 * D * D + 2 * D * FF) ** -0.5), 0.00036621094, ((0, 32),), jnp.float32)
    first_norm = normal_values(keys[12], (4, D), (0.33 * (4 * D * D + 2 * D * FF) ** -0.5), 0.0009765625, ((1, 32),), jnp.float32)
    second_qkv = jnp.clip(jnp.exp(math.log(1.2715657415895976e-09) - 1.3862944 * jax.random.uniform(keys[13], (D, 3 * D), jnp.float32) ** levels(keys[13], (D, 3 * D), ((0, 32),), -0.2, 0.2)), 3.178914353973994e-10, 1.2715657415895976e-09)
    second_out = jnp.clip(jnp.exp(math.log(1.2715657415895976e-09) - 1.3862944 * jax.random.uniform(keys[14], (D, D), jnp.float32) ** levels(keys[14], (D, D), ((0, 32),), -0.2, 0.2)), 3.178914353973994e-10, 1.2715657415895976e-09)
    second_up = jnp.clip(jnp.exp(math.log(1.2715657415895976e-09) - 1.3862944 * jax.random.uniform(keys[15], (D, FF), jnp.float32) ** levels(keys[15], (D, FF), ((0, 32),), -0.2, 0.2)), 3.178914353973994e-10, 1.2715657415895976e-09)
    second_down = jnp.clip(jnp.exp(math.log(1.2715657415895976e-09) - 1.3862944 * jax.random.uniform(keys[16], (FF, D), jnp.float32) ** levels(keys[16], (FF, D), ((0, 32),), -0.2, 0.2)), 3.178914353973994e-10, 1.2715657415895976e-09)
    second_norm = jnp.clip(jnp.exp(math.log(1.1444091896350983e-08) - 1.3862944 * jax.random.uniform(keys[17], (4, D), jnp.float32) ** levels(keys[17], (4, D), ((1, 32),), -0.2, 0.2)), 2.8610229740877458e-09, 1.1444091896350983e-08)
    return {"tokens": tokens, "cotangent": cotangent, "lengths": lengths, "w_qkv": w_qkv, "w_out": w_out, "w_up": w_up, "w_down": w_down, "norm_params": norm_params, "first_qkv": first_qkv, "first_out": first_out, "first_up": first_up, "first_down": first_down, "first_norm": first_norm, "second_qkv": second_qkv, "second_out": second_out, "second_up": second_up, "second_down": second_down, "second_norm": second_norm}


eps_norm = 1e-05
neg_fill = -1e+30
beta_one = 0.9
beta_two = 0.999
adam_eps = 1e-08
decay_coef = 0.1
rate_matrix = 0.05
rate_norm = 0.5
clip_bound = 1.0

@jax.custom_vjp
def low(v):
    return lax.optimization_barrier(v.astype(jnp.bfloat16)).astype(jnp.float32)

@jax.custom_vjp
def low_back(v):
    return v

def low_keep(v):
    return (low(v), None)

def low_pass(kept, grad):
    return (grad,)

def back_keep(v):
    return (v, None)

def back_low(kept, grad):
    return (low(grad),)
low.defvjp(low_keep, low_pass)
low_back.defvjp(back_keep, back_low)

def normalize(values_in, gain_row, shift_row):
    center = values_in - lax.optimization_barrier(jnp.mean(values_in, axis=-1, keepdims=True))
    spread = lax.optimization_barrier(jnp.mean(center * center, axis=-1, keepdims=True))
    return center * lax.rsqrt(spread + eps_norm) * gain_row + shift_row

def matmul_high(left, right):
    return jnp.dot(left, right, precision=lax.Precision.HIGHEST, preferred_element_type=jnp.float32)

def einsum_high(form, left, right):
    return jnp.einsum(form, left, right, precision=lax.Precision.HIGHEST, preferred_element_type=jnp.float32)

def item_forward(params, tokens_f, length):
    w_qkv, w_out, w_up, w_down, norm_rows = [low(weight) for weight in params]
    seq_len, model_width = tokens_f.shape
    span_count = seq_len // SPAN
    score_scale = HEAD_DIM ** (-0.5)
    normed = low(normalize(tokens_f, norm_rows[0], norm_rows[1]))
    qkv_rows = low(low_back(matmul_high(normed, w_qkv))).reshape(span_count, SPAN, 3, HEADS, HEAD_DIM)
    query_part = qkv_rows[:, :, 0]
    key_part = qkv_rows[:, :, 1]
    value_part = qkv_rows[:, :, 2]
    positions = jnp.arange(seq_len).reshape(span_count, SPAN)
    live_mask = (positions < length).astype(jnp.float32)
    counts = lax.optimization_barrier(jnp.sum(live_mask, axis=1))
    pooled = einsum_high('st,stchd->schd', live_mask, qkv_rows[:, :, 1:]) / jnp.maximum(counts, 1.0)[:, None, None, None]
    pooled = low(pooled)
    near_raw = einsum_high('sqhd,skhd->shqk', query_part, key_part) * score_scale
    far_raw = einsum_high('sqhd,rhd->shqr', query_part, pooled[:, 0]) * score_scale
    scores = low_back(jnp.concatenate([near_raw, far_raw], axis=-1))
    span_ids = jnp.arange(span_count)
    far_valid = (counts[None, :] > 0.0) & (span_ids[:, None] != span_ids[None, :])
    near_ok = jnp.broadcast_to((live_mask > 0.0)[:, None, None, :], (span_count, HEADS, SPAN, SPAN))
    far_ok = jnp.broadcast_to(far_valid[:, None, None, :], (span_count, HEADS, SPAN, span_count))
    masked = jnp.where(jnp.concatenate([near_ok, far_ok], axis=-1), scores, neg_fill)
    score_top = lax.optimization_barrier(jnp.max(masked, axis=-1, keepdims=True))
    log_total = score_top + jnp.log(lax.optimization_barrier(jnp.sum(jnp.exp(masked - score_top), axis=-1, keepdims=True)))
    attn_probs = low(jnp.exp(masked - log_total))
    mixed_rows = einsum_high('shqk,skhd->sqhd', attn_probs[..., :SPAN], value_part)
    mixed_rows = mixed_rows + einsum_high('shqr,rhd->sqhd', attn_probs[..., SPAN:], pooled[:, 1])
    mixed_rows = low(low_back(mixed_rows.reshape(seq_len, model_width)))
    residual = tokens_f + low_back(matmul_high(mixed_rows, w_out))
    normed_two = low(normalize(residual, norm_rows[2], norm_rows[3]))
    gated = low(jax.nn.gelu(low_back(matmul_high(normed_two, w_up))))
    return residual + matmul_high(gated, w_down)

def adamw_update(weight, grad_in, first_old, second_old, factor, step_rate, weight_decay):
    clipped = grad_in * factor
    first_new = beta_one * first_old + (1.0 - beta_one) * clipped
    second_new = beta_two * second_old + (1.0 - beta_two) * clipped * clipped
    first_hat = first_new / (1.0 - beta_one ** STEP)
    second_hat = second_new / (1.0 - beta_two ** STEP)
    weight_new = weight - step_rate * (first_hat / (jnp.sqrt(second_hat) + adam_eps) + weight_decay * weight)
    return (weight_new, first_new, second_new)

def reference(tokens, cotangent, lengths, w_qkv, w_out, w_up, w_down, norm_params, first_qkv, first_out, first_up, first_down, first_norm, second_qkv, second_out, second_up, second_down, second_norm):
    params = (w_qkv, w_out, w_up, w_down, norm_params)

    def one_item(totals, item_data):
        tokens_f, cot_f, length = item_data

        def forward_of(param_tree, tokens_in):
            return item_forward(param_tree, tokens_in, length)
        layer_out, back_fn = jax.vjp(forward_of, params, tokens_f)
        grad_tree, grad_tokens = back_fn(cot_f)
        totals = jax.tree.map(jnp.add, totals, grad_tree)
        return (totals, (layer_out.astype(jnp.bfloat16), grad_tokens))
    zero_tree = jax.tree.map(jnp.zeros_like, params)
    grad_tree, (activations, input_grad) = lax.scan(one_item, zero_tree, (tokens.astype(jnp.float32), cotangent.astype(jnp.float32), lengths))
    grad_qkv, grad_out, grad_up, grad_down, grad_norm_rows = grad_tree
    total_sq = jnp.sum(grad_qkv * grad_qkv) + jnp.sum(grad_out * grad_out) + jnp.sum(grad_up * grad_up)
    total_sq = total_sq + jnp.sum(grad_down * grad_down) + jnp.sum(grad_norm_rows * grad_norm_rows)
    grad_norm = jnp.sqrt(total_sq)
    factor = clip_bound / jnp.maximum(grad_norm, clip_bound)
    new_qkv, new_first_qkv, new_second_qkv = adamw_update(w_qkv, grad_qkv, first_qkv, second_qkv, factor, rate_matrix, decay_coef)
    new_out, new_first_out, new_second_out = adamw_update(w_out, grad_out, first_out, second_out, factor, rate_matrix, decay_coef)
    new_up, new_first_up, new_second_up = adamw_update(w_up, grad_up, first_up, second_up, factor, rate_matrix, decay_coef)
    new_down, new_first_down, new_second_down = adamw_update(w_down, grad_down, first_down, second_down, factor, rate_matrix, decay_coef)
    new_norm, new_first_norm, new_second_norm = adamw_update(norm_params, grad_norm_rows, first_norm, second_norm, factor, rate_norm, 0.0)
    return (activations, input_grad, grad_norm, new_qkv, new_first_qkv, new_second_qkv, new_out, new_first_out, new_second_out, new_up, new_first_up, new_second_up, new_down, new_first_down, new_second_down, new_norm, new_first_norm, new_second_norm)
```

```python
import functools
import math

import jax
import jax.numpy as jnp
from jax import lax
from jax.experimental import pallas as pl
from jax.experimental.pallas import tpu as pltpu
from jax.sharding import PartitionSpec as P

HEADS = 8
HEAD_DIM = 64
SPAN = 128
STEP = 10
WIDTH = 512


eps_norm = 1e-05
neg_fill = -1e30
beta_one = 0.9
beta_two = 0.999
adam_eps = 1e-08
decay_coef = 0.1
rate_matrix = 0.05
rate_norm = 0.5
clip_bound = 1.0


def normalize(values_in, gain_row, shift_row):
    center = values_in - jnp.mean(values_in, axis=-1, keepdims=True)
    spread = jnp.mean(center * center, axis=-1, keepdims=True)
    return center * lax.rsqrt(spread + eps_norm) * gain_row + shift_row


def adamw_update(weight, grad_in, first_old, second_old, factor, step_rate, weight_decay):
    clipped = grad_in * factor
    first_new = beta_one * first_old + (1.0 - beta_one) * clipped
    second_new = beta_two * second_old + (1.0 - beta_two) * clipped * clipped
    first_hat = first_new / (1.0 - beta_one**STEP)
    second_hat = second_new / (1.0 - beta_two**STEP)
    weight_new = weight - step_rate * (
        first_hat / (jnp.sqrt(second_hat) + adam_eps) + weight_decay * weight
    )
    return (weight_new, first_new, second_new)


def generic_device(
    tokens,
    cotangent,
    lengths,
    w_qkv,
    w_out,
    w_up,
    w_down,
    norm_params,
    first_qkv,
    first_out,
    first_up,
    first_down,
    first_norm,
    second_qkv,
    second_out,
    second_up,
    second_down,
    second_norm,
):
    item_count, local_len, model_width = tokens.shape
    row_count = item_count * local_len
    spans_here = local_len // SPAN
    spans_all = spans_here * lax.axis_size("seq")
    seq_rank = lax.axis_index("seq")
    score_scale = HEAD_DIM ** (-0.5)
    full_qkv, full_out, full_up, full_down, full_norm = (
        lax.all_gather(w_qkv.astype(jnp.bfloat16), ("dp", "seq"), axis=0, tiled=True),
        lax.all_gather(w_out.astype(jnp.bfloat16), ("dp", "seq"), axis=0, tiled=True),
        lax.all_gather(w_up.astype(jnp.bfloat16), ("dp", "seq"), axis=0, tiled=True),
        lax.all_gather(w_down.astype(jnp.bfloat16), ("dp", "seq"), axis=0, tiled=True),
        lax.all_gather(norm_params.astype(jnp.bfloat16), ("dp", "seq"), axis=1, tiled=True),
    )
    norm_rows = full_norm.astype(jnp.float32)
    tokens_f = tokens.reshape(row_count, model_width).astype(jnp.float32)
    normed, back_one = jax.vjp(normalize, tokens_f, norm_rows[0], norm_rows[1])
    normed_b = normed.astype(jnp.bfloat16)
    qkv_b = jnp.dot(normed_b, full_qkv, preferred_element_type=jnp.float32).astype(jnp.bfloat16)
    qkv_view = qkv_b.reshape(item_count, spans_here, SPAN, 3, HEADS, HEAD_DIM)
    query_part = qkv_view[:, :, :, 0]
    key_part = qkv_view[:, :, :, 1]
    value_part = qkv_view[:, :, :, 2]
    local_pos = seq_rank * local_len + jnp.arange(local_len, dtype=jnp.int32)
    live_mask = (local_pos[None, :] < lengths[:, None]).reshape(item_count, spans_here, SPAN)
    live_f = live_mask.astype(jnp.float32)
    counts_here = jnp.maximum(jnp.sum(live_f, axis=2), 1.0)
    pooled = jnp.einsum(
        "ist,istchd->ischd",
        live_mask.astype(jnp.bfloat16),
        qkv_view[:, :, :, 1:],
        preferred_element_type=jnp.float32,
    )
    pooled = (pooled / counts_here[:, :, None, None, None]).astype(jnp.bfloat16)
    pooled_all = lax.all_gather(pooled, "seq", axis=1, tiled=True)
    pooled_keys = pooled_all[:, :, 0]
    pooled_values = pooled_all[:, :, 1]
    all_pos = jnp.arange(spans_all * SPAN, dtype=jnp.int32).reshape(spans_all, SPAN)
    counts_all = jnp.sum((all_pos[None] < lengths[:, None, None]).astype(jnp.float32), axis=2)
    span_ids = seq_rank * spans_here + jnp.arange(spans_here, dtype=jnp.int32)
    far_valid = (counts_all[:, None, :] > 0.0) & (
        span_ids[None, :, None] != jnp.arange(spans_all, dtype=jnp.int32)[None, None, :]
    )
    near_mask = live_mask[:, :, None, None, :]
    far_mask = far_valid[:, :, None, None, :]

    def scores_of():
        near_raw = (
            jnp.einsum(
                "isqhd,iskhd->ishqk", query_part, key_part, preferred_element_type=jnp.float32
            )
            * score_scale
        )
        far_raw = (
            jnp.einsum(
                "isqhd,irhd->ishqr", query_part, pooled_keys, preferred_element_type=jnp.float32
            )
            * score_scale
        )
        return (jnp.where(near_mask, near_raw, neg_fill), jnp.where(far_mask, far_raw, neg_fill))

    near_s, far_s = scores_of()
    score_top = jnp.maximum(
        jnp.max(near_s, axis=-1, keepdims=True), jnp.max(far_s, axis=-1, keepdims=True)
    )
    exp_total = jnp.sum(jnp.exp(near_s - score_top), axis=-1, keepdims=True) + jnp.sum(
        jnp.exp(far_s - score_top), axis=-1, keepdims=True
    )
    log_total = score_top + jnp.log(exp_total)
    near_pb = jnp.exp(near_s - log_total).astype(jnp.bfloat16)
    far_pb = jnp.exp(far_s - log_total).astype(jnp.bfloat16)
    mixed_rows = jnp.einsum(
        "ishqk,iskhd->isqhd", near_pb, value_part, preferred_element_type=jnp.float32
    )
    mixed_rows = mixed_rows + jnp.einsum(
        "ishqr,irhd->isqhd", far_pb, pooled_values, preferred_element_type=jnp.float32
    )
    mixed_b = mixed_rows.reshape(row_count, model_width).astype(jnp.bfloat16)
    residual = tokens_f + jnp.dot(mixed_b, full_out, preferred_element_type=jnp.float32)
    normed_two, back_two = jax.vjp(normalize, residual, norm_rows[2], norm_rows[3])
    normed_two_b = normed_two.astype(jnp.bfloat16)
    up_pre = jnp.dot(normed_two_b, full_up, preferred_element_type=jnp.float32)
    gated, gelu_back = jax.vjp(jax.nn.gelu, up_pre)
    gated_b = gated.astype(jnp.bfloat16)
    layer_out = residual + jnp.dot(gated_b, full_down, preferred_element_type=jnp.float32)
    activations = layer_out.astype(jnp.bfloat16).reshape(item_count, local_len, model_width)
    grad_out_b = cotangent.reshape(row_count, model_width)
    grad_down = jnp.dot(gated_b.T, grad_out_b, preferred_element_type=jnp.float32)
    grad_gated = jnp.dot(grad_out_b, full_down.T, preferred_element_type=jnp.float32)
    grad_up_pre = gelu_back(grad_gated)[0].astype(jnp.bfloat16)
    grad_up = jnp.dot(normed_two_b.T, grad_up_pre, preferred_element_type=jnp.float32)
    grad_normed_two = jnp.dot(grad_up_pre, full_up.T, preferred_element_type=jnp.float32)
    grad_resid_ln, grad_gain_two, grad_shift_two = back_two(grad_normed_two)
    grad_resid = grad_out_b.astype(jnp.float32) + grad_resid_ln
    grad_attn_b = grad_resid.astype(jnp.bfloat16)
    grad_out_proj = jnp.dot(mixed_b.T, grad_attn_b, preferred_element_type=jnp.float32)
    grad_mixed = jnp.dot(grad_attn_b, full_out.T, preferred_element_type=jnp.float32).astype(
        jnp.bfloat16
    )
    grad_mixed = grad_mixed.reshape(item_count, spans_here, SPAN, HEADS, HEAD_DIM)
    near_s, far_s = scores_of()
    near_pf = jnp.exp(near_s - log_total)
    far_pf = jnp.exp(far_s - log_total)
    near_pb = near_pf.astype(jnp.bfloat16)
    far_pb = far_pf.astype(jnp.bfloat16)
    grad_near = jnp.einsum(
        "isqhd,iskhd->ishqk", grad_mixed, value_part, preferred_element_type=jnp.float32
    )
    grad_far = jnp.einsum(
        "isqhd,irhd->ishqr", grad_mixed, pooled_values, preferred_element_type=jnp.float32
    )
    row_delta = jnp.sum(near_pf * grad_near, axis=-1, keepdims=True) + jnp.sum(
        far_pf * grad_far, axis=-1, keepdims=True
    )
    dscore_near = (near_pf * (grad_near - row_delta)).astype(jnp.bfloat16)
    dscore_far = (far_pf * (grad_far - row_delta)).astype(jnp.bfloat16)
    grad_query = jnp.einsum(
        "ishqk,iskhd->isqhd", dscore_near, key_part, preferred_element_type=jnp.float32
    )
    grad_query = (
        grad_query
        + jnp.einsum(
            "ishqr,irhd->isqhd", dscore_far, pooled_keys, preferred_element_type=jnp.float32
        )
    ) * score_scale
    grad_keys = (
        jnp.einsum(
            "ishqk,isqhd->iskhd", dscore_near, query_part, preferred_element_type=jnp.float32
        )
        * score_scale
    )
    grad_values = jnp.einsum(
        "ishqk,isqhd->iskhd", near_pb, grad_mixed, preferred_element_type=jnp.float32
    )
    grad_pool_keys = (
        jnp.einsum("ishqr,isqhd->irhd", dscore_far, query_part, preferred_element_type=jnp.float32)
        * score_scale
    )
    grad_pool_values = jnp.einsum(
        "ishqr,isqhd->irhd", far_pb, grad_mixed, preferred_element_type=jnp.float32
    )
    pool_grads = jnp.stack([grad_pool_keys, grad_pool_values], axis=2)
    pool_mine = lax.psum_scatter(
        pool_grads.astype(jnp.bfloat16), "seq", scatter_dimension=1, tiled=True
    ).astype(jnp.float32)
    spread_back = pool_mine / counts_here[:, :, None, None, None]
    grad_kv = (
        jnp.stack([grad_keys, grad_values], axis=3)
        + live_f[:, :, :, None, None, None] * spread_back[:, :, None]
    )
    grad_qkv_rows = jnp.concatenate([grad_query[:, :, :, None], grad_kv], axis=3)
    grad_qkv_b = grad_qkv_rows.reshape(row_count, 3 * model_width).astype(jnp.bfloat16)
    grad_qkv = jnp.dot(normed_b.T, grad_qkv_b, preferred_element_type=jnp.float32)
    grad_normed = jnp.dot(grad_qkv_b, full_qkv.T, preferred_element_type=jnp.float32)
    grad_in_ln, grad_gain_one, grad_shift_one = back_one(grad_normed)
    input_grad = (grad_resid + grad_in_ln).reshape(item_count, local_len, model_width)
    grad_norm_rows = jnp.stack([grad_gain_one, grad_shift_one, grad_gain_two, grad_shift_two])
    red_qkv, red_out, red_up, red_down, red_norm = (
        lax.psum_scatter(grad_qkv, ("dp", "seq"), scatter_dimension=0, tiled=True),
        lax.psum_scatter(grad_out_proj, ("dp", "seq"), scatter_dimension=0, tiled=True),
        lax.psum_scatter(grad_up, ("dp", "seq"), scatter_dimension=0, tiled=True),
        lax.psum_scatter(grad_down, ("dp", "seq"), scatter_dimension=0, tiled=True),
        lax.psum_scatter(grad_norm_rows, ("dp", "seq"), scatter_dimension=1, tiled=True),
    )
    squares = jnp.sum(red_qkv * red_qkv) + jnp.sum(red_out * red_out) + jnp.sum(red_up * red_up)
    squares = squares + jnp.sum(red_down * red_down) + jnp.sum(red_norm * red_norm)
    total_sq = lax.psum(squares, ("dp", "seq"))
    grad_norm = jnp.sqrt(total_sq)
    factor = clip_bound / jnp.maximum(grad_norm, clip_bound)
    new_qkv, new_first_qkv, new_second_qkv = adamw_update(
        w_qkv, red_qkv, first_qkv, second_qkv, factor, rate_matrix, decay_coef
    )
    new_out, new_first_out, new_second_out = adamw_update(
        w_out, red_out, first_out, second_out, factor, rate_matrix, decay_coef
    )
    new_up, new_first_up, new_second_up = adamw_update(
        w_up, red_up, first_up, second_up, factor, rate_matrix, decay_coef
    )
    new_down, new_first_down, new_second_down = adamw_update(
        w_down, red_down, first_down, second_down, factor, rate_matrix, decay_coef
    )
    new_norm, new_first_norm, new_second_norm = adamw_update(
        norm_params, red_norm, first_norm, second_norm, factor, rate_norm, 0.0
    )
    return (
        activations,
        input_grad,
        grad_norm,
        new_qkv,
        new_first_qkv,
        new_second_qkv,
        new_out,
        new_first_out,
        new_second_out,
        new_up,
        new_first_up,
        new_second_up,
        new_down,
        new_first_down,
        new_second_down,
        new_norm,
        new_first_norm,
        new_second_norm,
    )


BF = jnp.bfloat16
F32 = jnp.float32
MESH = pl.DeviceIdType.MESH
LANES = 128
TILE = 512
NN = (((1,), (0,)), ((), ()))
NT = (((1,), (1,)), ((), ()))
TN = (((0,), (0,)), ((), ()))
GATHER, REDUCE, POOL, POOLBACK, SQUARES, COPIES = 0, 24, 48, 55, 62, 72


def mm(left, right, dims=NN):
    return lax.dot_general(left, right, dims, preferred_element_type=F32)


def centered(values_in):
    center = values_in - jnp.mean(values_in, axis=-1, keepdims=True)
    scale = lax.rsqrt(jnp.mean(center * center, axis=-1, keepdims=True) + eps_norm)
    return center * scale, scale


def norm_back(grad_hat, hat, scale):
    mean_grad = jnp.mean(grad_hat, axis=-1, keepdims=True)
    mean_both = jnp.mean(grad_hat * hat, axis=-1, keepdims=True)
    return scale * (grad_hat - mean_grad - hat * mean_both)


def fold_rows(values_in):
    rows, width = values_in.shape
    return jnp.sum(values_in.reshape(rows // 8, 8, width), axis=0)


def layer_kernel(
    len_ref, x_any, dy_any, wq_ref, wo_ref, wu_ref, wd_ref, nrm_ref,
    fq_ref, fo_ref, fu_ref, fd_ref, sq_ref, so_ref, su_ref, sd_ref,
    act_any, dx_any, gn_ref,
    nq_ref, nfq_ref, nsq_ref, no_ref, nfo_ref, nso_ref,
    nu_ref, nfu_ref, nsu_ref, nd_ref, nfd_ref, nsd_ref, nnrm_ref,
    bq, bu, bd, qkv, mix, prob, gq, gu, gdt, gd,
    r1q, r2aq, r2bq, r3aq, r3bq, r4q,
    r1u, s2au, s2bu, r2au, r2bu, r3au, r3bu, s3u, r4u,
    r1d, s2ad, s2bd, r2ad, r2bd, r3ad, r3bd, s3d, r4d,
    pool_all, pool_far, pool_grad, pool_send, pool_recv, spread,
    nrow, nacc, act_s, dup_s, h_s, ht_s, dyt_s, dh_s, fin_q, fin_u, fin_d,
    psq, psd, x_ref, dy_ref, dx_ref, send_sem, recv_sem, local_sem,
):
    ny, nc, nz, nx, blk, _ = bq.shape
    dblk = bd.shape[4]
    rows_all, width = x_ref.shape
    width3 = 3 * width
    ff = wu_ref.shape[1]
    seq_n = nz * nx
    dp_n = ny * nc
    local_len = rows_all // len_ref.shape[0]
    spans_here = local_len // SPAN
    blocks = rows_all // SPAN
    spans_all = spans_here * seq_n
    tiles = rows_all // TILE
    per_tile = TILE // SPAN
    pairs = width // LANES
    dp_i = lax.axis_index("dp")
    sq_i = lax.axis_index("seq")
    y, c = dp_i // nc, dp_i % nc
    z, x = sq_i // nx, sq_i % nx

    def dev(yy, cc, zz, xx):
        return (yy * nc + cc, zz * nx + xx)

    twin = dev(y, 1 - c, z, x)
    over_x = dev(y, c, z, 1 - x)
    over_y = dev(1 - y, c, z, x)

    def hop(src, dst, index, target):
        return pltpu.make_async_remote_copy(
            src_ref=src, dst_ref=dst, send_sem=send_sem.at[index],
            recv_sem=recv_sem.at[index], device_id=target, device_id_type=MESH,
        )

    load_x = pltpu.make_async_copy(x_any, x_ref, local_sem.at[0])
    load_dy = pltpu.make_async_copy(dy_any, dy_ref, local_sem.at[1])
    keep_act = pltpu.make_async_copy(dy_ref, act_any, local_sem.at[2])
    keep_dx = pltpu.make_async_copy(dx_ref, dx_any, local_sem.at[3])
    load_x.start()
    load_dy.start()

    barrier = pltpu.get_barrier_semaphore()
    for step in range(1, seq_n):
        pl.semaphore_signal(
            barrier, inc=1, device_id=(dp_i, lax.rem(sq_i + step, seq_n)), device_id_type=MESH
        )
    for step in range(1, dp_n):
        pl.semaphore_signal(
            barrier, inc=1, device_id=(lax.rem(dp_i + step, dp_n), sq_i), device_id_type=MESH
        )
    pl.semaphore_wait(barrier, seq_n + dp_n - 2)

    bq[y, c, z, x, :, 0:width3] = wq_ref[...].astype(BF)
    bq[y, c, z, x, :, width3:] = nrm_ref[0:blk, :].astype(BF)
    bu[y, c, z, x, :, 0:ff] = wu_ref[...].astype(BF)
    bu[y, c, z, x, :, ff:] = wo_ref[...].astype(BF)
    bd[y, c, z, x] = wd_ref[...].astype(BF)

    def gather_hops(full, base):
        cut = (full.shape[5] // 2) // LANES * LANES
        one, two = pl.ds(0, cut), pl.ds(cut, full.shape[5] - cut)

        def same(part, index, target):
            return hop(part, part, base + index, target)

        first = [
            same(full.at[y, c, z, x], step - 1, dev(y, c, lax.rem(z + step, nz), x))
            for step in range(1, nz)
        ]
        second = [
            same(full.at[y, c, :, x, :, one], 3, over_x),
            same(full.at[y, c, :, x, :, two], 4, over_y),
        ]
        third = [
            same(full.at[y, c, :, :, :, one], 5, over_y),
            same(full.at[:, c, :, x, :, two], 6, over_x),
        ]
        last = [same(full.at[:, c], 7, twin)]
        return first, second, third, last

    def start(hops):
        for one in hops:
            one.start()

    def arrived(hops):
        for one in hops:
            one.wait_recv()

    def sent(hops):
        for one in hops:
            one.wait_send()

    hops_q = gather_hops(bq, GATHER)
    hops_u = gather_hops(bu, GATHER + 8)
    hops_d = gather_hops(bd, GATHER + 16)
    start(hops_q[0])
    start(hops_u[0])
    start(hops_d[0])

    def clear(index, carry):
        gq[...] = jnp.zeros_like(gq)
        gu[...] = jnp.zeros_like(gu)
        gdt[...] = jnp.zeros_like(gdt)
        return carry

    lax.fori_loop(0, 1, clear, 0)
    nacc[...] = jnp.zeros_like(nacc)
    pool_grad[...] = jnp.zeros_like(pool_grad)

    load_x.wait()
    arrived(hops_q[0])
    start(hops_q[1])
    arrived(hops_q[1])
    start(hops_q[2])
    arrived(hops_q[2])
    start(hops_q[3])
    arrived(hops_u[0])
    start(hops_u[1])
    arrived(hops_d[0])
    start(hops_d[1])
    arrived(hops_q[3])

    norm_cols = bq[:, :, :, :, :, width3:].reshape(width, LANES).astype(F32)
    nrow[...] = norm_cols.T[0:8]

    def w_qkv(lo, hi):
        return bq[:, :, :, :, :, lo:hi].reshape(width, hi - lo)

    def qkv_tile(tile, pooled):
        rows = pl.ds(pl.multiple_of(tile * TILE, TILE), TILE)
        hat, _ = centered(x_ref[rows, :].astype(F32))
        h1 = (hat * nrow[0:1, :] + nrow[1:2, :]).astype(BF)
        for part in range(3):
            cols = pl.ds(part * width, width)
            qkv[rows, cols] = mm(h1, w_qkv(part * width, (part + 1) * width)).astype(BF)
        block_at = lax.broadcasted_iota(jnp.int32, (blocks, TILE), 0)
        row_at = lax.broadcasted_iota(jnp.int32, (blocks, TILE), 1) + tile * TILE
        pos = sq_i * local_len + lax.rem(row_at, local_len)
        item = row_at // local_len
        length = jnp.zeros((blocks, TILE), jnp.int32)
        for i in range(TILE // local_len):
            at = tile * (TILE // local_len) + i
            length = jnp.where(item == at, len_ref[at], length)
        pick = jnp.where((row_at // SPAN == block_at) & (pos < length), 1.0, 0.0).astype(BF)

        @pl.when(tile == 1)
        def _():
            arrived(hops_u[1])
            start(hops_u[2])

        @pl.when(tile == 2)
        def _():
            arrived(hops_d[1])
            start(hops_d[2])

        return pooled + mm(pick, qkv[rows, width:])

    pooled = lax.fori_loop(0, tiles, qkv_tile, jnp.zeros((blocks, 2 * width), F32))
    block_col = lax.broadcasted_iota(jnp.int32, (blocks, 1), 0)
    length_col = jnp.zeros((blocks, 1), jnp.int32)
    for i in range(blocks // spans_here):
        length_col = jnp.where(block_col // spans_here == i, len_ref[i], length_col)
    first_pos = sq_i * local_len + lax.rem(block_col, spans_here) * SPAN
    count_col = jnp.clip(length_col - first_pos, 1, SPAN).astype(F32)
    pool_all[sq_i] = (pooled / count_col).astype(BF)
    pool_hops = [
        hop(
            pool_all.at[sq_i], pool_all.at[sq_i], POOL + step - 1,
            (dp_i, lax.rem(sq_i + step, seq_n)),
        )
        for step in range(1, seq_n)
    ]
    start(pool_hops)
    arrived(hops_u[2])
    start(hops_u[3])
    arrived(hops_d[2])
    start(hops_d[3])
    arrived(pool_hops)

    far_n = seq_n * blocks
    to_row = lax.broadcasted_iota(jnp.int32, (far_n, far_n), 0)
    to_col = lax.broadcasted_iota(jnp.int32, (far_n, far_n), 1)
    item_row, span_row = to_row // spans_all, to_row % spans_all
    wanted = (span_row // spans_here) * blocks + item_row * spans_here + span_row % spans_here
    order = jnp.where(wanted == to_col, 1.0, 0.0).astype(BF)
    pool_far[...] = mm(order, pool_all[...].reshape(far_n, 2 * width)).astype(BF)

    keys_n = SPAN + spans_all
    lane = lax.broadcasted_iota(jnp.int32, (1, LANES), 1)
    score_scale = HEAD_DIM ** (-0.5)
    half_a = jnp.where(lane < HEAD_DIM, 1.0, 0.0)
    half_b = jnp.where(lane >= HEAD_DIM, 1.0, 0.0)
    query_a, query_b = (half_a * score_scale).astype(BF), (half_b * score_scale).astype(BF)
    grad_a, grad_b = half_a.astype(BF), half_b.astype(BF)

    def both(near_rows, far_rows, cols):
        return jnp.concatenate([qkv[near_rows, cols], pool_far[far_rows, cols_far(cols)]], axis=0)

    def cols_far(cols):
        return pl.ds(cols.start - width, cols.size)

    def diagonal(stacked):
        return jnp.concatenate(
            [stacked[0:HEAD_DIM, 0:SPAN], stacked[HEAD_DIM:, SPAN:]], axis=0
        ).T

    def attend(block, carry):
        item = block // spans_here
        sub = lax.rem(block, spans_here)
        rows = pl.ds(pl.multiple_of(block * SPAN, SPAN), SPAN)
        far_rows = pl.ds(pl.multiple_of(item * spans_all, spans_all), spans_all)
        length = len_ref[item]
        key_at = lax.broadcasted_iota(jnp.int32, (keys_n, 2 * SPAN), 0)
        span_at = key_at - SPAN
        mine = sq_i * spans_here + sub
        near_ok = (key_at < SPAN) & (mine * SPAN + key_at < length)
        far_ok = (key_at >= SPAN) & (span_at * SPAN < length) & (span_at != mine)
        seen = near_ok | far_ok
        for pair in range(pairs):
            q2 = qkv[rows, pl.ds(pair * LANES, LANES)]
            kk = both(rows, far_rows, pl.ds(width + pair * LANES, LANES))
            vv = both(rows, far_rows, pl.ds(2 * width + pair * LANES, LANES))
            qq = jnp.concatenate([q2 * query_a, q2 * query_b], axis=0)
            score = jnp.where(seen, mm(kk, qq, NT), neg_fill)
            top = jnp.max(score, axis=0, keepdims=True)
            raised = jnp.exp(score - top)
            share = (raised * (1.0 / jnp.sum(raised, axis=0, keepdims=True))).astype(BF)
            prob[block, pair] = share
            mixed = diagonal(mm(vv, share, TN))
            mix[rows, pl.ds(pair * LANES, LANES)] = mixed.astype(BF)
        return carry

    lax.fori_loop(0, blocks, attend, 0)
    arrived(hops_u[3])
    arrived(hops_d[3])
    for hops in (hops_q, hops_u, hops_d):
        for group in hops:
            sent(group)
    sent(pool_hops)

    load_dy.wait()
    w_out = bu[:, :, :, :, :, ff:].reshape(width, width)
    gelu_in = math.sqrt(2.0 / math.pi)
    gelu_cube = 0.044715

    tall_tile = (nz, nx, dblk, width)
    half_tile = TILE // 2

    def ffn_tile(tile, carry):
        rows = pl.ds(pl.multiple_of(tile * TILE, TILE), TILE)
        x1 = x_ref[rows, :].astype(F32) + mm(mix[rows, :], w_out)
        hat, scale = centered(x1)
        gd[0] = x1.reshape(tall_tile)
        gd[1] = hat.reshape(tall_tile)
        h2 = hat * nrow[2:3, :] + nrow[3:4, :]
        h_s[...] = h2.astype(BF)
        ht_s[...] = h2.T.astype(BF)
        dyt_s[...] = dy_ref[rows, :].astype(F32).T.astype(BF)
        dh_s[...] = jnp.zeros_like(dh_s)

        def ffn_part(part, inner):
            cols = pl.ds(pl.multiple_of(part * TILE, TILE), TILE)
            w_up = bu[:, :, :, :, :, cols].reshape(width, TILE)
            w_down = bd[part // nc, part % nc].reshape(TILE, width)
            for part_rows in range(2):
                some = pl.ds(part_rows * half_tile, half_tile)
                up = mm(h_s[some, :], w_up)
                square = up * up
                bent = jnp.tanh(up * (gelu_in + (gelu_in * gelu_cube) * square))
                half = 0.5 + 0.5 * bent
                act_s[some, :] = (up * half).astype(BF)
                rate = half + (up * (1.0 - bent * bent)) * (
                    0.5 * gelu_in + (1.5 * gelu_in * gelu_cube) * square
                )
                near = pl.ds(pl.multiple_of(tile * TILE + part_rows * half_tile, half_tile), half_tile)
                dup_s[some, :] = (mm(dy_ref[near, :], w_down, NT) * rate).astype(BF)
            gd[0] += mm(act_s[...], w_down).reshape(tall_tile)
            gdt[:, cols] += mm(dyt_s[...], act_s[...])
            gu[:, :, :, :, :, cols] += mm(ht_s[...], dup_s[...]).reshape(
                ny, nc, nz, nx, blk, TILE
            )
            dh_s[...] += mm(dup_s[...], w_up, NT)
            return inner

        lax.fori_loop(0, ff // TILE, ffn_part, 0)
        dh2 = dh_s[...]
        hat = gd[1].reshape(TILE, width)
        nacc[2] += fold_rows(dh2 * hat)
        nacc[3] += fold_rows(dh2)
        dx1 = dy_ref[rows, :].astype(F32) + norm_back(dh2 * nrow[2:3, :], hat, scale)
        dy_ref[rows, :] = gd[0].reshape(TILE, width).astype(BF)
        dx_ref[rows, :] = dx1
        dz = dx1.astype(BF)
        gu[:, :, :, :, :, ff:] += mm(mix[rows, :], dz, TN).reshape(ny, nc, nz, nx, blk, width)
        mix[rows, :] = mm(dz, w_out, NT).astype(BF)
        return carry

    lax.fori_loop(0, tiles, ffn_tile, 0)
    keep_act.start()

    def each(count, body):
        def step(index, carry):
            body(index)
            return carry

        lax.fori_loop(0, count, step, 0)

    def reduce_steps(own, load_other, s1, r1, s2a, s2b, r2a, r2b, r3a, r3b, s3, r4, fin, base):
        n = s1.shape[4]
        cut = (n // 2) // LANES * LANES
        one, two = pl.ds(0, cut), pl.ds(cut, n - cut)
        hop1 = [hop(s1, r1, base, twin)]
        hop2 = [
            hop(s1.at[1 - y, :, :, :, one], r2a, base + 1, over_y),
            hop(s1.at[:, :, 1 - x, :, two], r2b, base + 2, over_x),
        ]
        hop3 = [
            hop(s2a.at[:, 1 - x], r3a, base + 3, over_x),
            hop(s2b.at[1 - y], r3b, base + 4, over_y),
        ]
        hop4 = [
            hop(
                s3.at[lax.rem(z + step, nz)], r4.at[step - 1], base + 4 + step,
                dev(y, c, lax.rem(z + step, nz), x),
            )
            for step in range(1, nz)
        ]

        def stage1():
            load_other()
            start(hop1)

        def stage2():
            arrived(hop1)
            sent(hop1)

            def add(index):
                yy, zz, xx = index // (nz * nx), (index // nx) % nz, index % nx
                total = own[yy, zz, xx] + r1[yy, zz, xx].astype(F32)
                own[yy, zz, xx] = total
                s1[yy, zz, xx] = total.astype(BF)

            each(ny * nz * nx, add)
            start(hop2)

        def stage3():
            arrived(hop2)
            for zz in range(nz):
                for xx in range(nx):
                    total = own[y, zz, xx, :, one] + r2a[zz, xx].astype(F32)
                    own[y, zz, xx, :, one] = total
                    s2a[zz, xx] = total.astype(BF)
            hop3[0].start()
            for yy in range(ny):
                for zz in range(nz):
                    total = own[yy, zz, x, :, two] + r2b[yy, zz].astype(F32)
                    own[yy, zz, x, :, two] = total
                    s2b[yy, zz] = total.astype(BF)
            hop3[1].start()

        def stage4():
            arrived(hop3)
            for zz in range(nz):
                total = own[y, zz, x, :, one] + r3a[zz].astype(F32)
                own[y, zz, x, :, one] = total
                s3[zz, :, one] = total.astype(BF)
                total = own[y, zz, x, :, two] + r3b[zz].astype(F32)
                own[y, zz, x, :, two] = total
                s3[zz, :, two] = total.astype(BF)
            start(hop4)

        def stage5():
            arrived(hop4)
            total = own[y, z, x]
            for step in range(nz - 1):
                total = total + r4[step].astype(F32)
            fin[...] = total
            sent(hop2)
            sent(hop3)
            sent(hop4)

        return stage1, stage2, stage3, stage4, stage5

    def plain_own(full):
        return full.at[:, c]

    def plain_other(full, s1):
        def load():
            def one(index):
                yy, zz, xx = index // (nz * nx), (index // nx) % nz, index % nx
                s1[yy, zz, xx] = full[yy, 1 - c, zz, xx].astype(BF)

            each(ny * nz * nx, one)

        return load

    def down_other():
        group = nz * nx * dblk
        for yy in range(ny):
            for cc, is_own in ((c, True), (1 - c, False)):
                for part in range(group // LANES):
                    at = pl.multiple_of((yy * nc + cc) * group + part * LANES, LANES)
                    piece = gdt[:, pl.ds(at, LANES)].T.reshape(LANES // dblk, dblk, width)
                    for inner in range(LANES // dblk):
                        where = part * (LANES // dblk) + inner
                        if is_own:
                            gd[yy, where // nx, where % nx] = piece[inner]
                        else:
                            s1d[yy, where // nx, where % nx] = piece[inner].astype(BF)

    s1u, s1d = bu.at[:, 0], bd.at[:, 0]
    cols_q = r1q.shape[4]
    cut_q = r3aq.shape[2]
    s1q = bu.at[:, 1, :, :, :, pl.ds(0, cols_q)]
    s2aq = s2au.at[:, :, :, pl.ds(0, cut_q)]
    s2bq = s2bu.at[:, :, :, pl.ds(0, cols_q - cut_q)]
    s3q = s3u.at[:, :, pl.ds(0, cols_q)]
    red_d = reduce_steps(
        gd, down_other, s1d, r1d, s2ad, s2bd, r2ad, r2bd, r3ad, r3bd, s3d, r4d, fin_d, REDUCE
    )
    red_u = reduce_steps(
        plain_own(gu), plain_other(gu, s1u), s1u, r1u, s2au, s2bu, r2au, r2bu, r3au, r3bu,
        s3u, r4u, fin_u, REDUCE + 8,
    )
    red_q = reduce_steps(
        plain_own(gq), plain_other(gq, s1q), s1q, r1q, s2aq, s2bq, r2aq, r2bq, r3aq, r3bq,
        s3q, r4q, fin_q, REDUCE + 16,
    )
    red_d[0]()
    red_u[0]()

    def attend_back(block, carry):
        for at, steps in ((1, 1), (5, 2), (10, 3)):

            @pl.when(block == at)
            def _(steps=steps):
                red_d[steps]()
                red_u[steps]()

        item = block // spans_here
        rows = pl.ds(pl.multiple_of(block * SPAN, SPAN), SPAN)
        far_rows = pl.ds(pl.multiple_of(item * spans_all, spans_all), spans_all)
        for pair in range(pairs):
            q_cols = pl.ds(pair * LANES, LANES)
            k_cols = pl.ds(width + pair * LANES, LANES)
            v_cols = pl.ds(2 * width + pair * LANES, LANES)
            q2 = qkv[rows, q_cols]
            do2 = mix[rows, q_cols]
            kk = both(rows, far_rows, k_cols)
            vv = both(rows, far_rows, v_cols)
            qq = jnp.concatenate([q2 * query_a, q2 * query_b], axis=0)
            dd = jnp.concatenate([do2 * grad_a, do2 * grad_b], axis=0)
            share = prob[block, pair]
            share_f = share.astype(F32)
            dshare = mm(vv, dd, NT)
            inner = jnp.sum(share_f * dshare, axis=0, keepdims=True)
            dscore = (share_f * (dshare - inner)).astype(BF)
            dq = diagonal(mm(kk, dscore, TN)) * score_scale
            dk = mm(dscore, qq)
            dv = mm(share, dd)
            qkv[rows, q_cols] = dq.astype(BF)
            qkv[rows, k_cols] = dk[0:SPAN].astype(BF)
            qkv[rows, v_cols] = dv[0:SPAN].astype(BF)
            pool_grad[far_rows, q_cols] += dk[SPAN:]
            pool_grad[far_rows, pl.ds(width + pair * LANES, LANES)] += dv[SPAN:]
        return carry

    lax.fori_loop(0, blocks, attend_back, 0)

    back_row = lax.broadcasted_iota(jnp.int32, (far_n, far_n), 0)
    back_col = lax.broadcasted_iota(jnp.int32, (far_n, far_n), 1)
    owner, place = back_row // blocks, back_row % blocks
    source = (place // spans_here) * spans_all + owner * spans_here + place % spans_here
    reorder = jnp.where(source == back_col, 1.0, 0.0).astype(BF)
    pool_send[...] = (
        mm(reorder, pool_grad[...].astype(BF)).astype(BF).reshape(seq_n, blocks, 2 * width)
    )
    back_hops = [
        hop(
            pool_send.at[lax.rem(sq_i + step, seq_n)], pool_recv.at[step - 1],
            POOLBACK + step - 1, (dp_i, lax.rem(sq_i + step, seq_n)),
        )
        for step in range(1, seq_n)
    ]
    start(back_hops)
    arrived(back_hops)
    pool_total = pool_send[sq_i].astype(F32)
    for step in range(seq_n - 1):
        pool_total = pool_total + pool_recv[step].astype(F32)
    spread[...] = pool_total / count_col

    def last_tile(tile, carry):
        rows = pl.ds(pl.multiple_of(tile * TILE, TILE), TILE)
        hat, scale = centered(x_ref[rows, :].astype(F32))
        h1 = (hat * nrow[0:1, :] + nrow[1:2, :]).astype(BF)
        for part in range(per_tile):
            block = tile * per_tile + part
            own_rows = pl.ds(pl.multiple_of(block * SPAN, SPAN), SPAN)
            pos = (
                sq_i * local_len
                + lax.rem(block, spans_here) * SPAN
                + lax.broadcasted_iota(jnp.int32, (SPAN, 1), 0)
            )
            live = jnp.where(pos < len_ref[block // spans_here], 1.0, 0.0)
            far = live * spread[pl.ds(block, 1), :]
            qkv[own_rows, width:] = (qkv[own_rows, width:].astype(F32) + far).astype(BF)
        ht_s[...] = h1.astype(F32).T.astype(BF)
        dh_s[...] = jnp.zeros_like(dh_s)
        for part in range(3):
            cols = pl.ds(part * width, width)
            gq[:, :, :, :, :, cols] += mm(ht_s[...], qkv[rows, cols]).reshape(
                ny, nc, nz, nx, blk, width
            )
            dh_s[...] += mm(qkv[rows, cols], w_qkv(part * width, (part + 1) * width), NT)
        dh1 = dh_s[...]
        nacc[0] += fold_rows(dh1 * hat)
        nacc[1] += fold_rows(dh1)
        dx_ref[rows, :] += norm_back(dh1 * nrow[0:1, :], hat, scale)
        return carry

    lax.fori_loop(0, tiles, last_tile, 0)
    keep_dx.start()
    norm_rows = [jnp.sum(nacc[k], axis=0, keepdims=True) for k in range(4)]
    norm_rows.append(jnp.zeros((LANES - 4, width), F32))
    gq[:, :, :, :, :, width3:] = (
        jnp.concatenate(norm_rows, axis=0).T.reshape(ny, nc, nz, nx, blk, LANES)
    )
    red_q[0]()
    red_d[4]()
    red_u[4]()
    red_q[1]()
    red_q[2]()
    red_q[3]()
    sent(back_hops)
    red_q[4]()

    def partial(ref):
        values_in = ref[...]
        squares = fold_rows(values_in * values_in)
        return sum(
            squares[:, k * LANES : (k + 1) * LANES] for k in range(squares.shape[1] // LANES)
        )

    psq[sq_i] = partial(fin_q) + partial(fin_u) + partial(fin_d)
    seq_hops = [
        hop(
            psq.at[sq_i], psq.at[sq_i], SQUARES + step - 1,
            (dp_i, lax.rem(sq_i + step, seq_n)),
        )
        for step in range(1, seq_n)
    ]
    start(seq_hops)
    arrived(seq_hops)
    total = psq[0]
    for k in range(1, seq_n):
        total = total + psq[k]
    psd[dp_i] = total
    dp_hops = [
        hop(
            psd.at[dp_i], psd.at[dp_i], SQUARES + seq_n - 2 + step,
            (lax.rem(dp_i + step, dp_n), sq_i),
        )
        for step in range(1, dp_n)
    ]
    start(dp_hops)
    arrived(dp_hops)
    total = psd[0]
    for k in range(1, dp_n):
        total = total + psd[k]
    grad_norm = jnp.sqrt(jnp.sum(jnp.sum(total, axis=1, keepdims=True), axis=0, keepdims=True))
    factor = clip_bound / jnp.maximum(grad_norm, clip_bound)
    gn_ref[...] = jnp.broadcast_to(grad_norm, gn_ref.shape)

    def update(weight, grad_in, first, second, outs, rate, decay):
        new = adamw_update(weight, grad_in, first, second, factor, rate, decay)
        for out, value in zip(outs, new):
            out[...] = value

    update(
        wq_ref[...], fin_q[:, 0:width3], fq_ref[...], sq_ref[...],
        (nq_ref, nfq_ref, nsq_ref), rate_matrix, decay_coef,
    )
    update(
        wo_ref[...], fin_u[:, ff:], fo_ref[...], so_ref[...],
        (no_ref, nfo_ref, nso_ref), rate_matrix, decay_coef,
    )
    update(
        wu_ref[...], fin_u[:, 0:ff], fu_ref[...], su_ref[...],
        (nu_ref, nfu_ref, nsu_ref), rate_matrix, decay_coef,
    )
    update(
        wd_ref[...], fin_d[...], fd_ref[...], sd_ref[...],
        (nd_ref, nfd_ref, nsd_ref), rate_matrix, decay_coef,
    )
    update(
        nrm_ref[0:blk, :], fin_q[:, width3:], nrm_ref[blk : 2 * blk, :],
        nrm_ref[2 * blk :, :],
        (
            nnrm_ref.at[pl.ds(0, blk)],
            nnrm_ref.at[pl.ds(blk, blk)],
            nnrm_ref.at[pl.ds(2 * blk, blk)],
        ),
        rate_norm, 0.0,
    )
    sent(seq_hops)
    sent(dp_hops)
    keep_act.wait()
    keep_dx.wait()


def fused_device(
    tokens, cotangent, lengths, w_qkv, w_out, w_up, w_down, norm_params,
    first_qkv, first_out, first_up, first_down, first_norm,
    second_qkv, second_out, second_up, second_down, second_norm,
):
    item_count, local_len, width = tokens.shape
    rows_all = item_count * local_len
    dp_n, seq_n = lax.axis_size("dp"), lax.axis_size("seq")
    nc = 2
    ny = dp_n // nc
    nx = ny
    nz = seq_n // nx
    blk, width3 = w_qkv.shape
    ff = w_up.shape[1]
    dblk = w_down.shape[0]
    blocks = rows_all // SPAN
    far_n = seq_n * blocks
    keys_n = SPAN + local_len // SPAN * seq_n

    def tall(rows_in):
        return jnp.pad(rows_in.T, ((0, 0), (0, LANES - rows_in.shape[0])))

    norm_pack = jnp.concatenate([tall(norm_params), tall(first_norm), tall(second_norm)], axis=0)
    matrices = (w_qkv, w_out, w_up, w_down)
    triples = [jax.ShapeDtypeStruct(w.shape, F32) for w in matrices for _ in range(3)]
    nq, nu, nd = width3 + LANES, ff + width, width

    def bufs(b, n, sends):
        cut = (n // 2) // LANES * LANES
        rest = n - cut
        taken = [pltpu.VMEM((nz, nx, b, cut), BF), pltpu.VMEM((ny, nz, b, rest), BF)]
        return [
            pltpu.VMEM((ny, nz, nx, b, n), BF),
            *(taken if sends else []),
            *taken,
            pltpu.VMEM((nz, b, cut), BF),
            pltpu.VMEM((nz, b, rest), BF),
            *([pltpu.VMEM((nz, b, n), BF)] if sends else []),
            pltpu.VMEM((nz - 1, b, n), BF),
        ]

    whole = pl.BlockSpec(memory_space=pltpu.VMEM)
    outside = pl.BlockSpec(memory_space=pl.ANY)
    outs = pl.pallas_call(
        layer_kernel,
        out_shape=[
            jax.ShapeDtypeStruct((rows_all, width), BF),
            jax.ShapeDtypeStruct((rows_all, width), F32),
            jax.ShapeDtypeStruct((8, LANES), F32),
            *triples,
            jax.ShapeDtypeStruct(norm_pack.shape, F32),
        ],
        in_specs=[pl.BlockSpec(memory_space=pltpu.SMEM), outside, outside] + [whole] * 13,
        out_specs=[outside, outside] + [whole] * 14,
        scratch_shapes=[
            pltpu.VMEM((ny, nc, nz, nx, blk, nq), BF),
            pltpu.VMEM((ny, nc, nz, nx, blk, nu), BF),
            pltpu.VMEM((ny, nc, nz, nx, dblk, nd), BF),
            pltpu.VMEM((rows_all, width3), BF),
            pltpu.VMEM((rows_all, width), BF),
            pltpu.VMEM((blocks, width // LANES, keys_n, 2 * SPAN), BF),
            pltpu.VMEM((ny, nc, nz, nx, blk, nq), F32),
            pltpu.VMEM((ny, nc, nz, nx, blk, nu), F32),
            pltpu.VMEM((width, ff), F32),
            pltpu.VMEM((ny, nz, nx, dblk, nd), F32),
            *bufs(blk, nq, False),
            *bufs(blk, nu, True),
            *bufs(dblk, nd, True),
            pltpu.VMEM((seq_n, blocks, 2 * width), BF),
            pltpu.VMEM((far_n, 2 * width), BF),
            pltpu.VMEM((far_n, 2 * width), F32),
            pltpu.VMEM((seq_n, blocks, 2 * width), BF),
            pltpu.VMEM((seq_n - 1, blocks, 2 * width), BF),
            pltpu.VMEM((blocks, 2 * width), F32),
            pltpu.VMEM((8, width), F32),
            pltpu.VMEM((4, 8, width), F32),
            pltpu.VMEM((TILE, TILE), BF),
            pltpu.VMEM((TILE, TILE), BF),
            pltpu.VMEM((TILE, width), BF),
            pltpu.VMEM((width, TILE), BF),
            pltpu.VMEM((width, TILE), BF),
            pltpu.VMEM((TILE, width), F32),
            pltpu.VMEM((blk, nq), F32),
            pltpu.VMEM((blk, nu), F32),
            pltpu.VMEM((dblk, nd), F32),
            pltpu.VMEM((seq_n, 8, LANES), F32),
            pltpu.VMEM((dp_n, 8, LANES), F32),
            pltpu.VMEM((rows_all, width), BF),
            pltpu.VMEM((rows_all, width), BF),
            pltpu.VMEM((rows_all, width), F32),
            pltpu.SemaphoreType.DMA((COPIES,)),
            pltpu.SemaphoreType.DMA((COPIES,)),
            pltpu.SemaphoreType.DMA((4,)),
        ],
        compiler_params=pltpu.CompilerParams(
            collective_id=0, has_side_effects=True, vmem_limit_bytes=64 * 1024 * 1024 - 65536
        ),
    )(
        lengths,
        tokens.reshape(rows_all, width),
        cotangent.reshape(rows_all, width),
        w_qkv, w_out, w_up, w_down, norm_pack,
        first_qkv, first_out, first_up, first_down,
        second_qkv, second_out, second_up, second_down,
    )
    act, grad, gnorm = outs[:3]
    new_pack = outs[15]
    count = norm_params.shape[0]
    norms = [new_pack[k * blk : (k + 1) * blk, 0:count].T for k in range(3)]
    return (
        act.reshape(tokens.shape), grad.reshape(tokens.shape), gnorm[0, 0],
        *outs[3:15], *norms,
    )


def solution(mesh):
    placed = (
        P("dp", "seq", None),
        P("dp", "seq", None),
        P("dp"),
        P(("dp", "seq"), None),
        P(("dp", "seq"), None),
        P(("dp", "seq"), None),
        P(("dp", "seq"), None),
        P(None, ("dp", "seq")),
        P(("dp", "seq"), None),
        P(("dp", "seq"), None),
        P(("dp", "seq"), None),
        P(("dp", "seq"), None),
        P(None, ("dp", "seq")),
        P(("dp", "seq"), None),
        P(("dp", "seq"), None),
        P(("dp", "seq"), None),
        P(("dp", "seq"), None),
        P(None, ("dp", "seq")),
    )
    dp_n, seq_n = mesh.shape["dp"], mesh.shape["seq"]
    fits = dp_n == 4 and seq_n % 2 == 0 and WIDTH // (dp_n * seq_n) == 16
    return jax.shard_map(
        fused_device if fits else generic_device,
        mesh=mesh,
        in_specs=placed,
        out_specs=(
            P("dp", "seq", None),
            P("dp", "seq", None),
            P(),
            P(("dp", "seq"), None),
            P(("dp", "seq"), None),
            P(("dp", "seq"), None),
            P(("dp", "seq"), None),
            P(("dp", "seq"), None),
            P(("dp", "seq"), None),
            P(("dp", "seq"), None),
            P(("dp", "seq"), None),
            P(("dp", "seq"), None),
            P(("dp", "seq"), None),
            P(("dp", "seq"), None),
            P(("dp", "seq"), None),
            P(None, ("dp", "seq")),
            P(None, ("dp", "seq")),
            P(None, ("dp", "seq")),
        ),
        check_vma=False,
    )
```

```python
import functools
import math

import jax
import jax.numpy as jnp
from jax import lax
from jax.experimental import pallas as pl
from jax.experimental.pallas import tpu as pltpu
from jax.sharding import PartitionSpec as P

HEADS = 8
HEAD_DIM = 64
SPAN = 128
STEP = 10
WIDTH = 512


eps_norm = 1e-05
neg_fill = -1e30
beta_one = 0.9
beta_two = 0.999
adam_eps = 1e-08
decay_coef = 0.1
rate_matrix = 0.05
rate_norm = 0.5
clip_bound = 1.0


def normalize(values_in, gain_row, shift_row):
    center = values_in - jnp.mean(values_in, axis=-1, keepdims=True)
    spread = jnp.mean(center * center, axis=-1, keepdims=True)
    return center * lax.rsqrt(spread + eps_norm) * gain_row + shift_row


def adamw_update(weight, grad_in, first_old, second_old, factor, step_rate, weight_decay):
    clipped = grad_in * factor
    first_new = beta_one * first_old + (1.0 - beta_one) * clipped
    second_new = beta_two * second_old + (1.0 - beta_two) * clipped * clipped
    first_hat = first_new / (1.0 - beta_one**STEP)
    second_hat = second_new / (1.0 - beta_two**STEP)
    weight_new = weight - step_rate * (
        first_hat / (jnp.sqrt(second_hat) + adam_eps) + weight_decay * weight
    )
    return (weight_new, first_new, second_new)


def generic_device(
    tokens,
    cotangent,
    lengths,
    w_qkv,
    w_out,
    w_up,
    w_down,
    norm_params,
    first_qkv,
    first_out,
    first_up,
    first_down,
    first_norm,
    second_qkv,
    second_out,
    second_up,
    second_down,
    second_norm,
):
    item_count, local_len, model_width = tokens.shape
    row_count = item_count * local_len
    spans_here = local_len // SPAN
    spans_all = spans_here * lax.axis_size("seq")
    seq_rank = lax.axis_index("seq")
    score_scale = HEAD_DIM ** (-0.5)
    full_qkv, full_out, full_up, full_down, full_norm = (
        lax.all_gather(w_qkv.astype(jnp.bfloat16), ("dp", "seq"), axis=0, tiled=True),
        lax.all_gather(w_out.astype(jnp.bfloat16), ("dp", "seq"), axis=0, tiled=True),
        lax.all_gather(w_up.astype(jnp.bfloat16), ("dp", "seq"), axis=0, tiled=True),
        lax.all_gather(w_down.astype(jnp.bfloat16), ("dp", "seq"), axis=0, tiled=True),
        lax.all_gather(norm_params.astype(jnp.bfloat16), ("dp", "seq"), axis=1, tiled=True),
    )
    norm_rows = full_norm.astype(jnp.float32)
    tokens_f = tokens.reshape(row_count, model_width).astype(jnp.float32)
    normed, back_one = jax.vjp(normalize, tokens_f, norm_rows[0], norm_rows[1])
    normed_b = normed.astype(jnp.bfloat16)
    qkv_b = jnp.dot(normed_b, full_qkv, preferred_element_type=jnp.float32).astype(jnp.bfloat16)
    qkv_view = qkv_b.reshape(item_count, spans_here, SPAN, 3, HEADS, HEAD_DIM)
    query_part = qkv_view[:, :, :, 0]
    key_part = qkv_view[:, :, :, 1]
    value_part = qkv_view[:, :, :, 2]
    local_pos = seq_rank * local_len + jnp.arange(local_len, dtype=jnp.int32)
    live_mask = (local_pos[None, :] < lengths[:, None]).reshape(item_count, spans_here, SPAN)
    live_f = live_mask.astype(jnp.float32)
    counts_here = jnp.maximum(jnp.sum(live_f, axis=2), 1.0)
    pooled = jnp.einsum(
        "ist,istchd->ischd",
        live_mask.astype(jnp.bfloat16),
        qkv_view[:, :, :, 1:],
        preferred_element_type=jnp.float32,
    )
    pooled = (pooled / counts_here[:, :, None, None, None]).astype(jnp.bfloat16)
    pooled_all = lax.all_gather(pooled, "seq", axis=1, tiled=True)
    pooled_keys = pooled_all[:, :, 0]
    pooled_values = pooled_all[:, :, 1]
    all_pos = jnp.arange(spans_all * SPAN, dtype=jnp.int32).reshape(spans_all, SPAN)
    counts_all = jnp.sum((all_pos[None] < lengths[:, None, None]).astype(jnp.float32), axis=2)
    span_ids = seq_rank * spans_here + jnp.arange(spans_here, dtype=jnp.int32)
    far_valid = (counts_all[:, None, :] > 0.0) & (
        span_ids[None, :, None] != jnp.arange(spans_all, dtype=jnp.int32)[None, None, :]
    )
    near_mask = live_mask[:, :, None, None, :]
    far_mask = far_valid[:, :, None, None, :]

    def scores_of():
        near_raw = (
            jnp.einsum(
                "isqhd,iskhd->ishqk", query_part, key_part, preferred_element_type=jnp.float32
            )
            * score_scale
        )
        far_raw = (
            jnp.einsum(
                "isqhd,irhd->ishqr", query_part, pooled_keys, preferred_element_type=jnp.float32
            )
            * score_scale
        )
        return (jnp.where(near_mask, near_raw, neg_fill), jnp.where(far_mask, far_raw, neg_fill))

    near_s, far_s = scores_of()
    score_top = jnp.maximum(
        jnp.max(near_s, axis=-1, keepdims=True), jnp.max(far_s, axis=-1, keepdims=True)
    )
    exp_total = jnp.sum(jnp.exp(near_s - score_top), axis=-1, keepdims=True) + jnp.sum(
        jnp.exp(far_s - score_top), axis=-1, keepdims=True
    )
    log_total = score_top + jnp.log(exp_total)
    near_pb = jnp.exp(near_s - log_total).astype(jnp.bfloat16)
    far_pb = jnp.exp(far_s - log_total).astype(jnp.bfloat16)
    mixed_rows = jnp.einsum(
        "ishqk,iskhd->isqhd", near_pb, value_part, preferred_element_type=jnp.float32
    )
    mixed_rows = mixed_rows + jnp.einsum(
        "ishqr,irhd->isqhd", far_pb, pooled_values, preferred_element_type=jnp.float32
    )
    mixed_b = mixed_rows.reshape(row_count, model_width).astype(jnp.bfloat16)
    residual = tokens_f + jnp.dot(mixed_b, full_out, preferred_element_type=jnp.float32)
    normed_two, back_two = jax.vjp(normalize, residual, norm_rows[2], norm_rows[3])
    normed_two_b = normed_two.astype(jnp.bfloat16)
    up_pre = jnp.dot(normed_two_b, full_up, preferred_element_type=jnp.float32)
    gated, gelu_back = jax.vjp(jax.nn.gelu, up_pre)
    gated_b = gated.astype(jnp.bfloat16)
    layer_out = residual + jnp.dot(gated_b, full_down, preferred_element_type=jnp.float32)
    activations = layer_out.astype(jnp.bfloat16).reshape(item_count, local_len, model_width)
    grad_out_b = cotangent.reshape(row_count, model_width)
    grad_down = jnp.dot(gated_b.T, grad_out_b, preferred_element_type=jnp.float32)
    grad_gated = jnp.dot(grad_out_b, full_down.T, preferred_element_type=jnp.float32)
    grad_up_pre = gelu_back(grad_gated)[0].astype(jnp.bfloat16)
    grad_up = jnp.dot(normed_two_b.T, grad_up_pre, preferred_element_type=jnp.float32)
    grad_normed_two = jnp.dot(grad_up_pre, full_up.T, preferred_element_type=jnp.float32)
    grad_resid_ln, grad_gain_two, grad_shift_two = back_two(grad_normed_two)
    grad_resid = grad_out_b.astype(jnp.float32) + grad_resid_ln
    grad_attn_b = grad_resid.astype(jnp.bfloat16)
    grad_out_proj = jnp.dot(mixed_b.T, grad_attn_b, preferred_element_type=jnp.float32)
    grad_mixed = jnp.dot(grad_attn_b, full_out.T, preferred_element_type=jnp.float32).astype(
        jnp.bfloat16
    )
    grad_mixed = grad_mixed.reshape(item_count, spans_here, SPAN, HEADS, HEAD_DIM)
    near_s, far_s = scores_of()
    near_pf = jnp.exp(near_s - log_total)
    far_pf = jnp.exp(far_s - log_total)
    near_pb = near_pf.astype(jnp.bfloat16)
    far_pb = far_pf.astype(jnp.bfloat16)
    grad_near = jnp.einsum(
        "isqhd,iskhd->ishqk", grad_mixed, value_part, preferred_element_type=jnp.float32
    )
    grad_far = jnp.einsum(
        "isqhd,irhd->ishqr", grad_mixed, pooled_values, preferred_element_type=jnp.float32
    )
    row_delta = jnp.sum(near_pf * grad_near, axis=-1, keepdims=True) + jnp.sum(
        far_pf * grad_far, axis=-1, keepdims=True
    )
    dscore_near = (near_pf * (grad_near - row_delta)).astype(jnp.bfloat16)
    dscore_far = (far_pf * (grad_far - row_delta)).astype(jnp.bfloat16)
    grad_query = jnp.einsum(
        "ishqk,iskhd->isqhd", dscore_near, key_part, preferred_element_type=jnp.float32
    )
    grad_query = (
        grad_query
        + jnp.einsum(
            "ishqr,irhd->isqhd", dscore_far, pooled_keys, preferred_element_type=jnp.float32
        )
    ) * score_scale
    grad_keys = (
        jnp.einsum(
            "ishqk,isqhd->iskhd", dscore_near, query_part, preferred_element_type=jnp.float32
        )
        * score_scale
    )
    grad_values = jnp.einsum(
        "ishqk,isqhd->iskhd", near_pb, grad_mixed, preferred_element_type=jnp.float32
    )
    grad_pool_keys = (
        jnp.einsum("ishqr,isqhd->irhd", dscore_far, query_part, preferred_element_type=jnp.float32)
        * score_scale
    )
    grad_pool_values = jnp.einsum(
        "ishqr,isqhd->irhd", far_pb, grad_mixed, preferred_element_type=jnp.float32
    )
    pool_grads = jnp.stack([grad_pool_keys, grad_pool_values], axis=2)
    pool_mine = lax.psum_scatter(
        pool_grads.astype(jnp.bfloat16), "seq", scatter_dimension=1, tiled=True
    ).astype(jnp.float32)
    spread_back = pool_mine / counts_here[:, :, None, None, None]
    grad_kv = (
        jnp.stack([grad_keys, grad_values], axis=3)
        + live_f[:, :, :, None, None, None] * spread_back[:, :, None]
    )
    grad_qkv_rows = jnp.concatenate([grad_query[:, :, :, None], grad_kv], axis=3)
    grad_qkv_b = grad_qkv_rows.reshape(row_count, 3 * model_width).astype(jnp.bfloat16)
    grad_qkv = jnp.dot(normed_b.T, grad_qkv_b, preferred_element_type=jnp.float32)
    grad_normed = jnp.dot(grad_qkv_b, full_qkv.T, preferred_element_type=jnp.float32)
    grad_in_ln, grad_gain_one, grad_shift_one = back_one(grad_normed)
    input_grad = (grad_resid + grad_in_ln).reshape(item_count, local_len, model_width)
    grad_norm_rows = jnp.stack([grad_gain_one, grad_shift_one, grad_gain_two, grad_shift_two])
    red_qkv, red_out, red_up, red_down, red_norm = (
        lax.psum_scatter(grad_qkv, ("dp", "seq"), scatter_dimension=0, tiled=True),
        lax.psum_scatter(grad_out_proj, ("dp", "seq"), scatter_dimension=0, tiled=True),
        lax.psum_scatter(grad_up, ("dp", "seq"), scatter_dimension=0, tiled=True),
        lax.psum_scatter(grad_down, ("dp", "seq"), scatter_dimension=0, tiled=True),
        lax.psum_scatter(grad_norm_rows, ("dp", "seq"), scatter_dimension=1, tiled=True),
    )
    squares = jnp.sum(red_qkv * red_qkv) + jnp.sum(red_out * red_out) + jnp.sum(red_up * red_up)
    squares = squares + jnp.sum(red_down * red_down) + jnp.sum(red_norm * red_norm)
    total_sq = lax.psum(squares, ("dp", "seq"))
    grad_norm = jnp.sqrt(total_sq)
    factor = clip_bound / jnp.maximum(grad_norm, clip_bound)
    new_qkv, new_first_qkv, new_second_qkv = adamw_update(
        w_qkv, red_qkv, first_qkv, second_qkv, factor, rate_matrix, decay_coef
    )
    new_out, new_first_out, new_second_out = adamw_update(
        w_out, red_out, first_out, second_out, factor, rate_matrix, decay_coef
    )
    new_up, new_first_up, new_second_up = adamw_update(
        w_up, red_up, first_up, second_up, factor, rate_matrix, decay_coef
    )
    new_down, new_first_down, new_second_down = adamw_update(
        w_down, red_down, first_down, second_down, factor, rate_matrix, decay_coef
    )
    new_norm, new_first_norm, new_second_norm = adamw_update(
        norm_params, red_norm, first_norm, second_norm, factor, rate_norm, 0.0
    )
    return (
        activations,
        input_grad,
        grad_norm,
        new_qkv,
        new_first_qkv,
        new_second_qkv,
        new_out,
        new_first_out,
        new_second_out,
        new_up,
        new_first_up,
        new_second_up,
        new_down,
        new_first_down,
        new_second_down,
        new_norm,
        new_first_norm,
        new_second_norm,
    )


BF = jnp.bfloat16
F32 = jnp.float32
MESH = pl.DeviceIdType.MESH
LANES = 128
TILE = 512
NN = (((1,), (0,)), ((), ()))
NT = (((1,), (1,)), ((), ()))
TN = (((0,), (0,)), ((), ()))
GATHER, SPREAD, PARTS, DOWN, OUTER, INNER, POOL, POOLBACK = 0, 22, 62, 94, 97, 105, 113, 120
NORM_SEQ, NORM_DP, SQUARE_SEQ, SQUARE_DP, COPIES = 127, 134, 137, 144, 147


def mm(left, right, dims=NN):
    return lax.dot_general(left, right, dims, preferred_element_type=F32)


def centered(values_in):
    center = values_in - jnp.mean(values_in, axis=-1, keepdims=True)
    scale = lax.rsqrt(jnp.mean(center * center, axis=-1, keepdims=True) + eps_norm)
    return center * scale, scale


def norm_back(grad_hat, hat, scale):
    mean_grad = jnp.mean(grad_hat, axis=-1, keepdims=True)
    mean_both = jnp.mean(grad_hat * hat, axis=-1, keepdims=True)
    return scale * (grad_hat - mean_grad - hat * mean_both)


def fold_rows(values_in):
    rows, width = values_in.shape
    return jnp.sum(values_in.reshape(rows // 8, 8, width), axis=0)


def layer_kernel(
    len_ref, x_any, dy_any, wq_ref, wo_ref, wu_ref, wd_ref, nrm_ref,
    act_any, dx_any, fin_q, fin_o, fin_u, fin_d, norm_sum, total_ref,
    bkv, bqo, bu, bd, qkv, mix, prob, gq, go, yacc, h2_s, ht_s, dyt_s, act_s, dup_s,
    own_p, s1p, r1p, s2ap, s2bp, r2ap, r2bp, r3ap, r3bp, s4p, r4p, fin_p, keep_d, s5d, r5d,
    s2aq, s2bq, s3q, r1q, r2aq, r2bq, r3aq, r3bq, r4q,
    s2ao, s2bo, s3o, r1o, r2ao, r2bo, r3ao, r3bo, r4o,
    pool_all, pool_far, pool_grad, pool_send, pool_recv, live_sum, spread_w,
    nrow, nacc, ntall, norm_seq, norm_dp, psq, psd, x_ref, dy_ref, dx_ref,
    send_sem, recv_sem, local_sem,
):
    ny, nc, nz, nx, blk, _ = bu.shape
    dblk = bd.shape[4]
    rows_all, width = x_ref.shape
    width3 = 3 * width
    ff = wu_ref.shape[1]
    seq_n = nz * nx
    dp_n = ny * nc
    local_len = rows_all // len_ref.shape[0]
    spans_here = local_len // SPAN
    blocks = rows_all // SPAN
    spans_all = spans_here * seq_n
    tiles = rows_all // TILE
    per_tile = TILE // SPAN
    pairs = width // LANES
    part_n = ff // nz
    half_tile = TILE // 2
    dp_i = lax.axis_index("dp")
    sq_i = lax.axis_index("seq")
    y, c = dp_i // nc, dp_i % nc
    z, x = sq_i // nx, sq_i % nx

    def dev(yy, cc, zz, xx):
        return (yy * nc + cc, zz * nx + xx)

    twin = dev(y, 1 - c, z, x)
    over_x = dev(y, c, z, 1 - x)
    over_y = dev(1 - y, c, z, x)

    def seq_peer(step):
        return lax.rem(sq_i + step, seq_n)

    def dp_peer(step):
        return lax.rem(dp_i + step, dp_n)

    def z_peer(step):
        return lax.rem(z + step, nz)

    def hop(src, dst, index, target):
        return pltpu.make_async_remote_copy(
            src_ref=src, dst_ref=dst, send_sem=send_sem.at[index],
            recv_sem=recv_sem.at[index], device_id=target, device_id_type=MESH,
        )

    def start(hops):
        for one in hops:
            one.start()

    def arrived(hops):
        for one in hops:
            one.wait_recv()

    def sent(hops):
        for one in hops:
            one.wait_send()

    def each(count, body):
        def step(index, carry):
            body(index)
            return carry

        lax.fori_loop(0, count, step, 0)

    def tile_rows(tile):
        return pl.ds(pl.multiple_of(tile * TILE, TILE), TILE)

    load_x = pltpu.make_async_copy(x_any, x_ref, local_sem.at[0])
    load_dy = pltpu.make_async_copy(dy_any, dy_ref, local_sem.at[1])
    keep_act = pltpu.make_async_copy(dy_ref, act_any, local_sem.at[2])
    keep_dx = pltpu.make_async_copy(dx_ref, dx_any, local_sem.at[3])
    load_dy.start()
    load_x.start()

    barrier = pltpu.get_barrier_semaphore()
    for step in range(1, seq_n):
        pl.semaphore_signal(
            barrier, inc=1, device_id=(dp_i, seq_peer(step)), device_id_type=MESH
        )
    for step in range(1, dp_n):
        pl.semaphore_signal(
            barrier, inc=1, device_id=(dp_peer(step), sq_i), device_id_type=MESH
        )

    bkv[y, c, z, x, :, 0 : 2 * width] = wq_ref[:, width:].astype(BF)
    bqo[y, c, z, x, :, 0:width] = wq_ref[:, 0:width].astype(BF)
    bqo[y, c, z, x, :, width:] = wo_ref[...].astype(BF)
    count = nrm_ref.shape[0]
    ntall[...] = jnp.zeros_like(ntall)
    ntall[0:count, 0:blk] = nrm_ref[...]
    bkv[y, c, z, x, :, 2 * width :] = ntall[...].T[0:blk].astype(BF)
    for part in range(nz):
        for group in range(dp_n):
            lo, at = part * part_n + group * LANES, (group * nz + part) * LANES
            bu[y, c, z, x, :, lo : lo + LANES] = wu_ref[:, at : at + LANES].astype(BF)
    bd[y, c, z, x] = wd_ref[...].astype(BF)
    pl.semaphore_wait(barrier, seq_n + dp_n - 2)

    def gather_hops(full, base):
        cut = (full.shape[5] // 2) // LANES * LANES
        one, two = pl.ds(0, cut), pl.ds(cut, full.shape[5] - cut)

        def same(part, index, target):
            return hop(part, part, base + index, target)

        first = [
            same(full.at[y, c, z, x], step - 1, dev(y, c, z_peer(step), x))
            for step in range(1, nz)
        ]
        second = [
            same(full.at[y, c, :, x, :, one], 3, over_x),
            same(full.at[y, c, :, x, :, two], 4, over_y),
        ]
        third = [
            same(full.at[y, c, :, :, :, one], 5, over_y),
            same(full.at[:, c, :, x, :, two], 6, over_x),
        ]
        last = [same(full.at[:, c], 7, twin)]
        return first, second, third, last

    def direct(full, base):
        mine = full.at[y, c, z, x]
        return [
            hop(mine, mine, base + step - 1, dev(y, c, z_peer(step), x)) for step in range(1, nz)
        ]

    def spread_hops(part):
        base = SPREAD + part * 10
        cols = pl.ds(pl.multiple_of(part * part_n, part_n), part_n)
        one = pl.ds(pl.multiple_of(part * part_n, LANES), part_n // 2)
        two = pl.ds(pl.multiple_of(part * part_n + part_n // 2, LANES), part_n // 2)
        d_one, d_two = pl.ds(0, width // 2), pl.ds(width // 2, width // 2)

        def same(place, index, target):
            return hop(place, place, base + index, target)

        return (
            [
                same(bu.at[y, c, :, x, :, one], 0, over_x),
                same(bu.at[y, c, :, x, :, two], 1, over_y),
                same(bd.at[y, c, part, x, :, d_one], 2, over_x),
                same(bd.at[y, c, part, x, :, d_two], 3, over_y),
            ],
            [
                same(bu.at[y, c, :, :, :, one], 4, over_y),
                same(bu.at[:, c, :, x, :, two], 5, over_x),
                same(bd.at[y, c, part, :, :, d_one], 6, over_y),
                same(bd.at[:, c, part, x, :, d_two], 7, over_x),
            ],
            [
                same(bu.at[:, c, :, :, :, cols], 8, twin),
                same(bd.at[:, c, part], 9, twin),
            ],
        )

    def pass_on(part, stage):
        hops = spread_hops(part)
        arrived(hops[stage])
        start(hops[stage + 1])

    hops_kv = gather_hops(bkv, GATHER)
    hops_qo = gather_hops(bqo, GATHER + 8)
    direct_u = direct(bu, GATHER + 16)
    direct_d = direct(bd, GATHER + 19)
    start(hops_kv[0])
    start(hops_qo[0])
    start(direct_u)
    start(direct_d)
    nacc[...] = jnp.zeros_like(nacc)
    pool_grad[...] = jnp.zeros_like(pool_grad)
    arrived(hops_kv[0])
    start(hops_kv[1])
    load_dy.wait()

    def turn_dy(tile):
        rows = tile_rows(tile)
        dyt_s[:, rows] = dy_ref[rows, :].astype(F32).T.astype(BF)

    each(tiles // 2, turn_dy)
    arrived(hops_kv[1])
    start(hops_kv[2])
    arrived(hops_qo[0])
    start(hops_qo[1])
    load_x.wait()
    each(tiles // 2, lambda tile: turn_dy(tile + tiles // 2))
    arrived(hops_kv[2])
    start(hops_kv[3])
    arrived(hops_qo[1])
    start(hops_qo[2])
    arrived(direct_u)
    arrived(direct_d)
    for part in range(nz):
        start(spread_hops(part)[0])
    arrived(hops_kv[3])

    norm_cols = bkv[:, :, :, :, :, 2 * width :].reshape(width, LANES).astype(F32)
    nrow[...] = norm_cols.T[0:8]

    def w_qkv(part):
        if part == 0:
            return bqo[:, :, :, :, :, 0:width].reshape(width, width)
        return bkv[:, :, :, :, :, (part - 1) * width : part * width].reshape(width, width)

    def first_norm(rows):
        hat, scale = centered(x_ref[rows, :].astype(F32))
        return hat, scale, (hat * nrow[0:1, :] + nrow[1:2, :]).astype(BF)

    def live_pick(tile):
        block_at = lax.broadcasted_iota(jnp.int32, (blocks, TILE), 0)
        row_at = lax.broadcasted_iota(jnp.int32, (blocks, TILE), 1) + tile * TILE
        pos = sq_i * local_len + lax.rem(row_at, local_len)
        item = row_at // local_len
        length = jnp.zeros((blocks, TILE), jnp.int32)
        for i in range(TILE // local_len):
            at = tile * (TILE // local_len) + i
            length = jnp.where(item == at, len_ref[at], length)
        return jnp.where((row_at // SPAN == block_at) & (pos < length), 1.0, 0.0).astype(BF)

    def kv_tile(tile, pooled):
        rows = tile_rows(tile)
        _, _, h1 = first_norm(rows)
        h2_s[rows, :] = h1
        for part in (1, 2):
            qkv[rows, pl.ds(part * width, width)] = mm(h1, w_qkv(part)).astype(BF)

        @pl.when(tile == 3)
        def _():
            arrived(hops_qo[2])
            start(hops_qo[3])

        return pooled + mm(live_pick(tile), qkv[rows, width:])

    pooled = lax.fori_loop(0, tiles, kv_tile, jnp.zeros((blocks, 2 * width), F32))
    block_col = lax.broadcasted_iota(jnp.int32, (blocks, 1), 0)
    length_col = jnp.zeros((blocks, 1), jnp.int32)
    for i in range(blocks // spans_here):
        length_col = jnp.where(block_col // spans_here == i, len_ref[i], length_col)
    first_pos = sq_i * local_len + lax.rem(block_col, spans_here) * SPAN
    count_col = jnp.clip(length_col - first_pos, 1, SPAN).astype(F32)
    pool_all[sq_i] = (pooled / count_col).astype(BF)
    pool_hops = [
        hop(pool_all.at[sq_i], pool_all.at[sq_i], POOL + step - 1, (dp_i, seq_peer(step)))
        for step in range(1, seq_n)
    ]
    start(pool_hops)
    pass_on(0, 0)
    arrived(hops_qo[3])

    def q_tile(tile):
        rows = tile_rows(tile)
        qkv[rows, 0:width] = mm(h2_s[rows, :], w_qkv(0)).astype(BF)

    each(tiles, q_tile)
    arrived(pool_hops)

    far_n = seq_n * blocks
    to_row = lax.broadcasted_iota(jnp.int32, (far_n, far_n), 0)
    to_col = lax.broadcasted_iota(jnp.int32, (far_n, far_n), 1)
    item_row, span_row = to_row // spans_all, to_row % spans_all
    wanted = (span_row // spans_here) * blocks + item_row * spans_here + span_row % spans_here
    order = jnp.where(wanted == to_col, 1.0, 0.0).astype(BF)
    pool_far[...] = mm(order, pool_all[...].reshape(far_n, 2 * width)).astype(BF)

    keys_n = SPAN + spans_all
    lane = lax.broadcasted_iota(jnp.int32, (1, LANES), 1)
    score_scale = HEAD_DIM ** (-0.5)
    half_a = jnp.where(lane < HEAD_DIM, 1.0, 0.0)
    half_b = jnp.where(lane >= HEAD_DIM, 1.0, 0.0)
    query_a, query_b = (half_a * score_scale).astype(BF), (half_b * score_scale).astype(BF)
    grad_a, grad_b = half_a.astype(BF), half_b.astype(BF)

    def both(near_rows, far_rows, cols):
        far_cols = pl.ds(cols.start - width, cols.size)
        return jnp.concatenate([qkv[near_rows, cols], pool_far[far_rows, far_cols]], axis=0)

    def diagonal(stacked):
        return jnp.concatenate(
            [stacked[0:HEAD_DIM, 0:SPAN], stacked[HEAD_DIM:, SPAN:]], axis=0
        ).T

    def attend(block, carry):
        for at, part, stage in (
            (0, 1, 0), (3, 0, 1), (4, 2, 0), (7, 1, 1), (8, 3, 0), (12, 2, 1), (15, 3, 1)
        ):

            @pl.when(block == at)
            def _(part=part, stage=stage):
                pass_on(part, stage)

        item = block // spans_here
        sub = lax.rem(block, spans_here)
        rows = pl.ds(pl.multiple_of(block * SPAN, SPAN), SPAN)
        far_rows = pl.ds(pl.multiple_of(item * spans_all, spans_all), spans_all)
        length = len_ref[item]
        key_at = lax.broadcasted_iota(jnp.int32, (keys_n, 2 * SPAN), 0)
        span_at = key_at - SPAN
        mine = sq_i * spans_here + sub
        near_ok = (key_at < SPAN) & (mine * SPAN + key_at < length)
        far_ok = (key_at >= SPAN) & (span_at * SPAN < length) & (span_at != mine)
        seen = near_ok | far_ok
        for pair in range(pairs):
            q2 = qkv[rows, pl.ds(pair * LANES, LANES)]
            kk = both(rows, far_rows, pl.ds(width + pair * LANES, LANES))
            vv = both(rows, far_rows, pl.ds(2 * width + pair * LANES, LANES))
            qq = jnp.concatenate([q2 * query_a, q2 * query_b], axis=0)
            score = jnp.where(seen, mm(kk, qq, NT), neg_fill)
            top = jnp.max(score, axis=0, keepdims=True)
            raised = jnp.exp(score - top)
            share = (raised * (1.0 / jnp.sum(raised, axis=0, keepdims=True))).astype(BF)
            prob[block, pair] = share
            mixed = diagonal(mm(vv, share, TN))
            mix[rows, pl.ds(pair * LANES, LANES)] = mixed.astype(BF)
        return carry

    lax.fori_loop(0, blocks, attend, 0)
    for group in (*hops_kv, *hops_qo, direct_u, direct_d, pool_hops):
        sent(group)

    w_out = bqo[:, :, :, :, :, width:].reshape(width, width)
    gelu_in = math.sqrt(2.0 / math.pi)
    gelu_cube = 0.044715

    def second_norm(rows):
        x1 = x_ref[rows, :].astype(F32) + mm(mix[rows, :], w_out)
        hat, scale = centered(x1)
        return x1, hat, scale

    def ffn_open(tile):
        rows = tile_rows(tile)
        x1, hat, _ = second_norm(rows)
        yacc[rows, :] = x1
        dx_ref[rows, :] = jnp.zeros((TILE, width), F32)
        h2 = hat * nrow[2:3, :] + nrow[3:4, :]
        h2_s[rows, :] = h2.astype(BF)
        ht_s[:, rows] = h2.T.astype(BF)

    each(tiles, ffn_open)

    half_cols = width // 2
    one_p, two_p = pl.ds(0, half_cols), pl.ds(half_cols, half_cols)
    up_rows = nz * blk

    def part_hops(part):
        base = PARTS + part * 8
        return (
            [hop(s1p, r1p.at[part], base, twin)],
            [
                hop(s1p.at[1 - y, :, :, one_p], r2ap.at[part], base + 1, over_y),
                hop(s1p.at[:, 1 - x, :, two_p], r2bp.at[part], base + 2, over_x),
            ],
            [
                hop(s2ap.at[1 - x], r3ap.at[part], base + 3, over_x),
                hop(s2bp.at[1 - y], r3bp.at[part], base + 4, over_y),
            ],
            [
                hop(
                    s4p.at[part, z_peer(step)], r4p.at[step - 1, part], base + 4 + step,
                    dev(y, c, z_peer(step), x),
                )
                for step in range(1, nz)
            ],
        )

    def down_cols(group):
        cols = pl.ds(pl.multiple_of(group * LANES, LANES), LANES)
        return gq[:, :, :, :, :, cols].reshape(width, LANES)

    def part_first(part):
        for yy in range(ny):
            for xx in range(nx):
                for zz in range(nz):
                    at = pl.ds(zz * blk, blk)
                    own_p[yy, xx, at] = go[yy, c, zz, xx]
                    s1p[yy, xx, at] = go[yy, 1 - c, zz, xx].astype(BF)
            mine = down_cols(yy * nc + c).T
            other = down_cols(yy * nc + 1 - c).T
            for xx in range(nx):
                own_p[yy, xx, up_rows:] = mine[xx * dblk : (xx + 1) * dblk]
                s1p[yy, xx, up_rows:] = other[xx * dblk : (xx + 1) * dblk].astype(BF)
        start(part_hops(part)[0])

    def part_second(part):
        hops = part_hops(part)
        arrived(hops[0])
        sent(hops[0])

        def add(index):
            yy, xx = index // nx, index % nx
            total = own_p[yy, xx] + r1p[part, yy, xx].astype(F32)
            own_p[yy, xx] = total
            s1p[yy, xx] = total.astype(BF)

        each(ny * nx, add)
        start(hops[1])

    def part_third(part):
        hops = part_hops(part)
        arrived(hops[1])
        sent(hops[1])
        for xx in range(nx):
            total = own_p[y, xx, :, one_p] + r2ap[part, xx].astype(F32)
            own_p[y, xx, :, one_p] = total
            s2ap[xx] = total.astype(BF)
        for yy in range(ny):
            total = own_p[yy, x, :, two_p] + r2bp[part, yy].astype(F32)
            own_p[yy, x, :, two_p] = total
            s2bp[yy] = total.astype(BF)
        start(hops[2])

    def part_fourth(part):
        hops = part_hops(part)
        arrived(hops[2])
        sent(hops[2])
        own_p[y, x, :, one_p] += r3ap[part].astype(F32)
        own_p[y, x, :, two_p] += r3bp[part].astype(F32)
        for zz in range(nz):
            s4p[part, zz] = own_p[y, x, zz * blk : (zz + 1) * blk].astype(BF)
        fin_p[part] = own_p[y, x, pl.ds(pl.multiple_of(z * blk, blk), blk)]
        down = own_p[y, x, up_rows:]
        keep_d[part] = down
        s5d[part] = down.astype(BF)
        start(hops[3])

    down_hops = [
        hop(
            s5d.at[z_peer(step)], r5d.at[step - 1], DOWN + step - 1, dev(y, c, z_peer(step), x)
        )
        for step in range(1, nz)
    ]

    def ffn_part(part, carry):
        cols = pl.ds(pl.multiple_of(part * part_n, part_n), part_n)
        arrived(spread_hops(part)[2])
        w_up = bu[:, :, :, :, :, cols].reshape(width, part_n)
        w_down = bd[:, :, part].reshape(part_n, width)

        def ffn_tile(tile):
            @pl.when((part > 0) & (tile == 1))
            def _():
                part_second(part - 1)

            rows = tile_rows(tile)
            for piece in range(2):
                lo = tile * TILE + piece * half_tile
                some = pl.ds(pl.multiple_of(lo, half_tile), half_tile)
                up = mm(h2_s[some, :], w_up)
                square = up * up
                bent = jnp.tanh(up * (gelu_in + (gelu_in * gelu_cube) * square))
                half = 0.5 + 0.5 * bent
                act_s[some, :] = (up * half).astype(BF)
                rate = half + (up * (1.0 - bent * bent)) * (
                    0.5 * gelu_in + (1.5 * gelu_in * gelu_cube) * square
                )
                dup_s[some, :] = (mm(dy_ref[some, :], w_down, NT) * rate).astype(BF)
            yacc[rows, :] += mm(act_s[rows, :], w_down)
            dx_ref[rows, :] += mm(dup_s[rows, :], w_up, NT)

        each(tiles, ffn_tile)

        @pl.when(part > 0)
        def _():
            part_third(part - 1)

        gq[:, :, :, :, :, 0:part_n] = mm(dyt_s[...], act_s[...]).reshape(go.shape)
        go[...] = mm(ht_s[...], dup_s[...]).reshape(go.shape)

        @pl.when(part > 0)
        def _():
            part_fourth(part - 1)

        part_first(part)
        return carry

    lax.fori_loop(0, nz, ffn_part, 0)

    def ffn_close(tile):
        @pl.when(tile == 1)
        def _():
            part_second(nz - 1)

        rows = tile_rows(tile)
        _, hat, scale = second_norm(rows)
        dh2 = dx_ref[rows, :]
        nacc[2] += fold_rows(dh2 * hat)
        nacc[3] += fold_rows(dh2)
        dx1 = dy_ref[rows, :].astype(F32) + norm_back(dh2 * nrow[2:3, :], hat, scale)
        dy_ref[rows, :] = yacc[rows, :].astype(BF)
        dx_ref[rows, :] = dx1
        dz = dx1.astype(BF)
        act_s[rows, :] = dz
        ht_s[:, rows] = mix[rows, :].astype(F32).T.astype(BF)
        mix[rows, :] = mm(dz, w_out, NT).astype(BF)

    each(tiles, ffn_close)
    keep_act.start()
    for part in range(nz):
        for group in spread_hops(part):
            sent(group)
    go[...] = mm(ht_s[...], act_s[...]).reshape(go.shape)

    def reduce_steps(full, s1, r1, s2a, s2b, r2a, r2b, r3a, r3b, s3, r4, fin, base):
        own = full.at[:, c]
        n = s1.shape[4]
        cut = (n // 2) // LANES * LANES
        one, two = pl.ds(0, cut), pl.ds(cut, n - cut)
        hop1 = [hop(s1, r1, base, twin)]
        hop2 = [
            hop(s1.at[1 - y, :, :, :, one], r2a, base + 1, over_y),
            hop(s1.at[:, :, 1 - x, :, two], r2b, base + 2, over_x),
        ]
        hop3 = [
            hop(s2a.at[:, 1 - x], r3a, base + 3, over_x),
            hop(s2b.at[1 - y], r3b, base + 4, over_y),
        ]
        hop4 = [
            hop(
                s3.at[z_peer(step)], r4.at[step - 1], base + 4 + step,
                dev(y, c, z_peer(step), x),
            )
            for step in range(1, nz)
        ]

        def places(index):
            return index // (nz * nx), (index // nx) % nz, index % nx

        def stage1():
            def load(index):
                yy, zz, xx = places(index)
                s1[yy, zz, xx] = full[yy, 1 - c, zz, xx].astype(BF)

            each(ny * nz * nx, load)
            start(hop1)

        def stage2():
            arrived(hop1)
            sent(hop1)

            def add(index):
                yy, zz, xx = places(index)
                total = own[yy, zz, xx] + r1[yy, zz, xx].astype(F32)
                own[yy, zz, xx] = total
                s1[yy, zz, xx] = total.astype(BF)

            each(ny * nz * nx, add)
            start(hop2)

        def stage3():
            arrived(hop2)
            for zz in range(nz):
                for xx in range(nx):
                    total = own[y, zz, xx, :, one] + r2a[zz, xx].astype(F32)
                    own[y, zz, xx, :, one] = total
                    s2a[zz, xx] = total.astype(BF)
            start(hop3[0:1])
            for yy in range(ny):
                for zz in range(nz):
                    total = own[yy, zz, x, :, two] + r2b[yy, zz].astype(F32)
                    own[yy, zz, x, :, two] = total
                    s2b[yy, zz] = total.astype(BF)
            start(hop3[1:2])

        def stage4():
            arrived(hop3)
            for zz in range(nz):
                total = own[y, zz, x, :, one] + r3a[zz].astype(F32)
                own[y, zz, x, :, one] = total
                s3[zz, :, one] = total.astype(BF)
                total = own[y, zz, x, :, two] + r3b[zz].astype(F32)
                own[y, zz, x, :, two] = total
                s3[zz, :, two] = total.astype(BF)
            start(hop4)

        def stage5():
            arrived(hop4)
            total = own[y, z, x]
            for step in range(nz - 1):
                total = total + r4[step].astype(F32)
            fin[...] = total
            sent(hop2)
            sent(hop3)
            sent(hop4)

        return stage1, stage2, stage3, stage4, stage5

    red_o = reduce_steps(
        go, bu.at[:, 0, :, :, :, pl.ds(0, width)], r1o, s2ao, s2bo, r2ao, r2bo, r3ao, r3bo, s3o,
        r4o, fin_o, OUTER,
    )
    red_q = reduce_steps(
        gq, bu.at[:, 1, :, :, :, pl.ds(0, width3)], r1q, s2aq, s2bq, r2aq, r2bq, r3aq, r3bq,
        s3q, r4q, fin_q, INNER,
    )
    red_o[0]()

    def last_third():
        part_third(nz - 1)

    def fourth_and_down():
        part_fourth(nz - 1)
        start(down_hops)

    def attend_back(block, carry):
        for at, step in (
            (0, last_third), (5, fourth_and_down), (6, red_o[1]), (10, red_o[2]), (14, red_o[3])
        ):

            @pl.when(block == at)
            def _(step=step):
                step()

        item = block // spans_here
        rows = pl.ds(pl.multiple_of(block * SPAN, SPAN), SPAN)
        far_rows = pl.ds(pl.multiple_of(item * spans_all, spans_all), spans_all)
        for pair in range(pairs):
            q_cols = pl.ds(pair * LANES, LANES)
            k_cols = pl.ds(width + pair * LANES, LANES)
            v_cols = pl.ds(2 * width + pair * LANES, LANES)
            q2 = qkv[rows, q_cols]
            do2 = mix[rows, q_cols]
            kk = both(rows, far_rows, k_cols)
            vv = both(rows, far_rows, v_cols)
            qq = jnp.concatenate([q2 * query_a, q2 * query_b], axis=0)
            dd = jnp.concatenate([do2 * grad_a, do2 * grad_b], axis=0)
            share = prob[block, pair]
            share_f = share.astype(F32)
            dshare = mm(vv, dd, NT)
            inner = jnp.sum(share_f * dshare, axis=0, keepdims=True)
            dscore = (share_f * (dshare - inner)).astype(BF)
            dq = diagonal(mm(kk, dscore, TN)) * score_scale
            dk = mm(dscore, qq)
            dv = mm(share, dd)
            qkv[rows, q_cols] = dq.astype(BF)
            qkv[rows, k_cols] = dk[0:SPAN].astype(BF)
            qkv[rows, v_cols] = dv[0:SPAN].astype(BF)
            pool_grad[far_rows, q_cols] += dk[SPAN:]
            pool_grad[far_rows, pl.ds(width + pair * LANES, LANES)] += dv[SPAN:]
        return carry

    lax.fori_loop(0, blocks, attend_back, 0)

    back_row = lax.broadcasted_iota(jnp.int32, (far_n, far_n), 0)
    back_col = lax.broadcasted_iota(jnp.int32, (far_n, far_n), 1)
    owner, place = back_row // blocks, back_row % blocks
    source = (place // spans_here) * spans_all + owner * spans_here + place % spans_here
    reorder = jnp.where(source == back_col, 1.0, 0.0).astype(BF)
    pool_send[...] = (
        mm(reorder, pool_grad[...].astype(BF)).astype(BF).reshape(seq_n, blocks, 2 * width)
    )
    back_hops = [
        hop(
            pool_send.at[seq_peer(step)], pool_recv.at[step - 1], POOLBACK + step - 1,
            (dp_i, seq_peer(step)),
        )
        for step in range(1, seq_n)
    ]
    start(back_hops)

    live_sum[...] = jnp.zeros_like(live_sum)

    def turn_h1(tile):
        rows = tile_rows(tile)
        _, _, h1 = first_norm(rows)
        ht_s[:, rows] = h1.astype(F32).T.astype(BF)
        live_sum[...] += mm(live_pick(tile), h1)

    each(tiles, turn_h1)
    for part in range(3):
        cols = pl.ds(part * width, width)
        gq[:, :, :, :, :, cols] = mm(ht_s[...], qkv[:, cols]).reshape(
            ny, nc, nz, nx, blk, width
        )
    for part in range(nz):
        arrived(part_hops(part)[3])
        total = fin_p[part]
        for step in range(nz - 1):
            total = total + r4p[step, part].astype(F32)
        for group in range(dp_n):
            at = (group * nz + part) * LANES
            fin_u[:, at : at + LANES] = total[:, group * LANES : (group + 1) * LANES]
    arrived(down_hops)
    total = keep_d[z]
    for step in range(nz - 1):
        total = total + r5d[step].astype(F32)
    fin_d[...] = total
    red_o[4]()

    arrived(back_hops)
    pool_total = pool_send[sq_i].astype(F32)
    for step in range(seq_n - 1):
        pool_total = pool_total + pool_recv[step].astype(F32)
    far = pool_total / count_col
    far_hi = far.astype(BF)
    far_lo = (far - far_hi.astype(F32)).astype(BF)
    near = live_sum[...]
    near_hi = near.astype(BF)
    near_lo = (near - near_hi.astype(F32)).astype(BF)
    left = jnp.concatenate([near_hi, near_lo, near_hi], axis=0)
    right = jnp.concatenate([far_hi, far_hi, far_lo], axis=0)
    for part in range(2):
        cols = pl.ds((part + 1) * width, width)
        gq[:, :, :, :, :, cols] += mm(left, right[:, part * width : (part + 1) * width], TN).reshape(
            ny, nc, nz, nx, blk, width
        )
    red_q[0]()
    far_two = jnp.concatenate([far_hi, far_lo], axis=0)
    both_far = mm(far_two[:, 0:width], w_qkv(1), NT) + mm(far_two[:, width:], w_qkv(2), NT)
    spread_w[...] = both_far[0:blocks] + both_far[blocks:]

    def last_tile(tile):
        for at, step in ((1, red_q[1]), (3, red_q[2])):

            @pl.when(tile == at)
            def _(step=step):
                step()

        rows = tile_rows(tile)
        hat, scale, _ = first_norm(rows)
        extra = []
        for part in range(per_tile):
            block = tile * per_tile + part
            pos = (
                sq_i * local_len
                + lax.rem(block, spans_here) * SPAN
                + lax.broadcasted_iota(jnp.int32, (SPAN, 1), 0)
            )
            live = jnp.where(pos < len_ref[block // spans_here], 1.0, 0.0)
            extra.append(live * spread_w[pl.ds(block, 1), :])
        dh1 = jnp.concatenate(extra, axis=0)
        for part in range(3):
            dh1 = dh1 + mm(qkv[rows, pl.ds(part * width, width)], w_qkv(part), NT)
        nacc[0] += fold_rows(dh1 * hat)
        nacc[1] += fold_rows(dh1)
        dx_ref[rows, :] += norm_back(dh1 * nrow[0:1, :], hat, scale)

    each(tiles, last_tile)
    keep_dx.start()
    norm_rows = [jnp.sum(nacc[k], axis=0, keepdims=True) for k in range(4)]
    norm_rows.append(jnp.zeros((4, width), F32))
    norm_seq[sq_i] = jnp.concatenate(norm_rows, axis=0)
    norm_hops = [
        hop(norm_seq.at[sq_i], norm_seq.at[sq_i], NORM_SEQ + step - 1, (dp_i, seq_peer(step)))
        for step in range(1, seq_n)
    ]
    norm_hops_dp = [
        hop(norm_dp.at[dp_i], norm_dp.at[dp_i], NORM_DP + step - 1, (dp_peer(step), sq_i))
        for step in range(1, dp_n)
    ]
    start(norm_hops)
    red_q[3]()
    arrived(norm_hops)
    total = norm_seq[0]
    for k in range(1, seq_n):
        total = total + norm_seq[k]
    norm_dp[dp_i] = total
    start(norm_hops_dp)

    def partial(values_in):
        squares = fold_rows(values_in * values_in)
        return sum(
            squares[:, k * LANES : (k + 1) * LANES] for k in range(squares.shape[1] // LANES)
        )

    early = partial(fin_u[...]) + partial(fin_d[...]) + partial(fin_o[...])
    red_q[4]()
    psq[sq_i] = early + partial(fin_q[...])
    seq_hops = [
        hop(psq.at[sq_i], psq.at[sq_i], SQUARE_SEQ + step - 1, (dp_i, seq_peer(step)))
        for step in range(1, seq_n)
    ]
    start(seq_hops)
    sent(back_hops)
    for part in range(nz):
        sent(part_hops(part)[3])
    sent(down_hops)
    sent(norm_hops)
    arrived(norm_hops_dp)
    sent(norm_hops_dp)
    total = norm_dp[0]
    for k in range(1, dp_n):
        total = total + norm_dp[k]
    norm_sum[...] = total
    arrived(seq_hops)
    total = psq[0]
    for k in range(1, seq_n):
        total = total + psq[k]
    psd[dp_i] = total
    dp_hops = [
        hop(psd.at[dp_i], psd.at[dp_i], SQUARE_DP + step - 1, (dp_peer(step), sq_i))
        for step in range(1, dp_n)
    ]
    start(dp_hops)
    arrived(dp_hops)
    total = psd[0]
    for k in range(1, dp_n):
        total = total + psd[k]
    total_ref[...] = total
    sent(seq_hops)
    sent(dp_hops)
    keep_act.wait()
    keep_dx.wait()


def update_kernel(
    act_in, dx_in, total_ref, gq_ref, go_ref, gu_ref, gd_ref, gn_ref,
    wq_ref, wo_ref, wu_ref, wd_ref, wn_ref, fq_ref, fo_ref, fu_ref, fd_ref, fn_ref,
    sq_ref, so_ref, su_ref, sd_ref, sn_ref,
    act_out, dx_out, norm_ref, nq, nfq, nsq, no, nfo, nso, nu, nfu, nsu, nd, nfd, nsd,
    nn, nfn, nsn, act_s, dx_s, sems_in, sems_out,
):
    pieces = 4
    piece = act_s.shape[0] // pieces
    moves = []
    for k in range(pieces):
        rows = pl.ds(k * piece, piece)
        for n, (src, mid, dst) in enumerate(
            ((dx_in, dx_s, dx_out), (act_in, act_s, act_out))
        ):
            moves.append((
                pltpu.make_async_copy(src.at[rows], mid.at[rows], sems_in.at[n * pieces + k]),
                pltpu.make_async_copy(mid.at[rows], dst.at[rows], sems_out.at[n * pieces + k]),
            ))
    for inward, _ in moves:
        inward.start()
    norm_grads = gn_ref[...]
    total = jnp.sum(total_ref[...]) + jnp.sum(norm_grads * norm_grads)
    total = jnp.full((1, 1), total, F32)
    grad_norm = jnp.sqrt(total)
    factor = clip_bound / jnp.maximum(grad_norm, clip_bound)
    norm_ref[...] = grad_norm

    def update(weight, grad_in, first, second, outs, rate, decay):
        new = adamw_update(weight, grad_in, first, second, factor, rate, decay)
        for out, value in zip(outs, new):
            out[...] = value

    for inward, outward in moves:
        inward.wait()
        outward.start()
    for w, g, m, s, outs in (
        (wq_ref, gq_ref, fq_ref, sq_ref, (nq, nfq, nsq)),
        (wo_ref, go_ref, fo_ref, so_ref, (no, nfo, nso)),
        (wu_ref, gu_ref, fu_ref, su_ref, (nu, nfu, nsu)),
        (wd_ref, gd_ref, fd_ref, sd_ref, (nd, nfd, nsd)),
    ):
        update(w[...], g[...], m[...], s[...], outs, rate_matrix, decay_coef)
    count, cols = wn_ref.shape
    width = norm_grads.shape[1]
    place = (lax.axis_index("dp") * lax.axis_size("seq") + lax.axis_index("seq")) * cols
    turned = pltpu.roll(norm_grads, lax.rem(width - place, width), 1)
    update(
        wn_ref[...], turned[0:count, 0:cols], fn_ref[...], sn_ref[...], (nn, nfn, nsn),
        rate_norm, 0.0,
    )
    for _, outward in moves:
        outward.wait()


def fused_device(
    tokens, cotangent, lengths, w_qkv, w_out, w_up, w_down, norm_params,
    first_qkv, first_out, first_up, first_down, first_norm,
    second_qkv, second_out, second_up, second_down, second_norm,
):
    item_count, local_len, width = tokens.shape
    rows_all = item_count * local_len
    dp_n, seq_n = lax.axis_size("dp"), lax.axis_size("seq")
    nc = 2
    ny = dp_n // nc
    nx = ny
    nz = seq_n // nx
    blk, width3 = w_qkv.shape
    ff = w_up.shape[1]
    dblk = w_down.shape[0]
    blocks = rows_all // SPAN
    far_n = seq_n * blocks
    keys_n = SPAN + local_len // SPAN * seq_n
    part_n = ff // nz
    up_rows = nz * blk
    half = width // 2

    def bufs(b, n):
        cut = (n // 2) // LANES * LANES
        rest = n - cut
        taken = [pltpu.VMEM((nz, nx, b, cut), BF), pltpu.VMEM((ny, nz, b, rest), BF)]
        return [
            *taken,
            pltpu.VMEM((nz, b, n), BF),
            pltpu.VMEM((ny, nz, nx, b, n), BF),
            *taken,
            pltpu.VMEM((nz, b, cut), BF),
            pltpu.VMEM((nz, b, rest), BF),
            pltpu.VMEM((nz - 1, b, n), BF),
        ]

    whole = pl.BlockSpec(memory_space=pltpu.VMEM)
    outside = pl.BlockSpec(memory_space=pl.ANY)
    part_rows = up_rows + dblk
    outs = pl.pallas_call(
        layer_kernel,
        out_shape=[
            jax.ShapeDtypeStruct((rows_all, width), BF),
            jax.ShapeDtypeStruct((rows_all, width), F32),
            jax.ShapeDtypeStruct(w_qkv.shape, F32),
            jax.ShapeDtypeStruct(w_out.shape, F32),
            jax.ShapeDtypeStruct(w_up.shape, F32),
            jax.ShapeDtypeStruct(w_down.shape, F32),
            jax.ShapeDtypeStruct((8, width), F32),
            jax.ShapeDtypeStruct((8, LANES), F32),
        ],
        in_specs=[pl.BlockSpec(memory_space=pltpu.SMEM), outside, outside] + [whole] * 5,
        out_specs=[outside, outside] + [whole] * 6,
        scratch_shapes=[
            pltpu.VMEM((ny, nc, nz, nx, blk, 2 * width + LANES), BF),
            pltpu.VMEM((ny, nc, nz, nx, blk, 2 * width), BF),
            pltpu.VMEM((ny, nc, nz, nx, blk, ff), BF),
            pltpu.VMEM((ny, nc, nz, nx, dblk, width), BF),
            pltpu.VMEM((rows_all, width3), BF),
            pltpu.VMEM((rows_all, width), BF),
            pltpu.VMEM((blocks, width // LANES, keys_n, 2 * SPAN), BF),
            pltpu.VMEM((ny, nc, nz, nx, blk, width3), F32),
            pltpu.VMEM((ny, nc, nz, nx, blk, width), F32),
            pltpu.VMEM((rows_all, width), F32),
            pltpu.VMEM((rows_all, width), BF),
            pltpu.VMEM((width, rows_all), BF),
            pltpu.VMEM((width, rows_all), BF),
            pltpu.VMEM((rows_all, part_n), BF),
            pltpu.VMEM((rows_all, part_n), BF),
            pltpu.VMEM((ny, nx, part_rows, width), F32),
            pltpu.VMEM((ny, nx, part_rows, width), BF),
            pltpu.VMEM((nz, ny, nx, part_rows, width), BF),
            pltpu.VMEM((nx, part_rows, half), BF),
            pltpu.VMEM((ny, part_rows, half), BF),
            pltpu.VMEM((nz, nx, part_rows, half), BF),
            pltpu.VMEM((nz, ny, part_rows, half), BF),
            pltpu.VMEM((nz, part_rows, half), BF),
            pltpu.VMEM((nz, part_rows, half), BF),
            pltpu.VMEM((nz, nz, blk, width), BF),
            pltpu.VMEM((nz - 1, nz, blk, width), BF),
            pltpu.VMEM((nz, blk, width), F32),
            pltpu.VMEM((nz, dblk, width), F32),
            pltpu.VMEM((nz, dblk, width), BF),
            pltpu.VMEM((nz - 1, dblk, width), BF),
            *bufs(blk, width3),
            *bufs(blk, width),
            pltpu.VMEM((seq_n, blocks, 2 * width), BF),
            pltpu.VMEM((far_n, 2 * width), BF),
            pltpu.VMEM((far_n, 2 * width), F32),
            pltpu.VMEM((seq_n, blocks, 2 * width), BF),
            pltpu.VMEM((seq_n - 1, blocks, 2 * width), BF),
            pltpu.VMEM((blocks, width), F32),
            pltpu.VMEM((blocks, width), F32),
            pltpu.VMEM((8, width), F32),
            pltpu.VMEM((4, 8, width), F32),
            pltpu.VMEM((LANES, LANES), F32),
            pltpu.VMEM((seq_n, 8, width), F32),
            pltpu.VMEM((dp_n, 8, width), F32),
            pltpu.VMEM((seq_n, 8, LANES), F32),
            pltpu.VMEM((dp_n, 8, LANES), F32),
            pltpu.VMEM((rows_all, width), BF),
            pltpu.VMEM((rows_all, width), BF),
            pltpu.VMEM((rows_all, width), F32),
            pltpu.SemaphoreType.DMA((COPIES,)),
            pltpu.SemaphoreType.DMA((COPIES,)),
            pltpu.SemaphoreType.DMA((4,)),
        ],
        compiler_params=pltpu.CompilerParams(
            collective_id=0, has_side_effects=True, vmem_limit_bytes=64 * 1024 * 1024 - 65536
        ),
    )(
        lengths,
        tokens.reshape(rows_all, width),
        cotangent.reshape(rows_all, width),
        w_qkv, w_out, w_up, w_down, norm_params,
    )
    weights = (w_qkv, w_out, w_up, w_down, norm_params)
    new = pl.pallas_call(
        update_kernel,
        out_shape=[
            jax.ShapeDtypeStruct((rows_all, width), BF),
            jax.ShapeDtypeStruct((rows_all, width), F32),
            jax.ShapeDtypeStruct((1, 1), F32),
            *(jax.ShapeDtypeStruct(w.shape, F32) for w in weights for _ in range(3)),
        ],
        in_specs=[outside, outside] + [whole] * 21,
        out_specs=[outside, outside] + [whole] * 16,
        scratch_shapes=[
            pltpu.VMEM((rows_all, width), BF),
            pltpu.VMEM((rows_all, width), F32),
            pltpu.SemaphoreType.DMA((8,)),
            pltpu.SemaphoreType.DMA((8,)),
        ],
        compiler_params=pltpu.CompilerParams(vmem_limit_bytes=64 * 1024 * 1024 - 65536),
    )(
        outs[0], outs[1], outs[7], *outs[2:7], *weights,
        first_qkv, first_out, first_up, first_down, first_norm,
        second_qkv, second_out, second_up, second_down, second_norm,
    )
    return (
        new[0].reshape(tokens.shape), new[1].reshape(tokens.shape), new[2].reshape(()),
        *new[3:],
    )


def solution(mesh):
    placed = (
        P("dp", "seq", None),
        P("dp", "seq", None),
        P("dp"),
        P(("dp", "seq"), None),
        P(("dp", "seq"), None),
        P(("dp", "seq"), None),
        P(("dp", "seq"), None),
        P(None, ("dp", "seq")),
        P(("dp", "seq"), None),
        P(("dp", "seq"), None),
        P(("dp", "seq"), None),
        P(("dp", "seq"), None),
        P(None, ("dp", "seq")),
        P(("dp", "seq"), None),
        P(("dp", "seq"), None),
        P(("dp", "seq"), None),
        P(("dp", "seq"), None),
        P(None, ("dp", "seq")),
    )
    dp_n, seq_n = mesh.shape["dp"], mesh.shape["seq"]
    fits = dp_n == 4 and seq_n % 2 == 0 and WIDTH // (dp_n * seq_n) == 16
    return jax.shard_map(
        fused_device if fits else generic_device,
        mesh=mesh,
        in_specs=placed,
        out_specs=(
            P("dp", "seq", None),
            P("dp", "seq", None),
            P(),
            P(("dp", "seq"), None),
            P(("dp", "seq"), None),
            P(("dp", "seq"), None),
            P(("dp", "seq"), None),
            P(("dp", "seq"), None),
            P(("dp", "seq"), None),
            P(("dp", "seq"), None),
            P(("dp", "seq"), None),
            P(("dp", "seq"), None),
            P(("dp", "seq"), None),
            P(("dp", "seq"), None),
            P(("dp", "seq"), None),
            P(None, ("dp", "seq")),
            P(None, ("dp", "seq")),
            P(None, ("dp", "seq")),
        ),
        check_vma=False,
    )
```

```python
import functools
import math

import jax
import jax.numpy as jnp
from jax import lax
from jax.experimental import pallas as pl
from jax.experimental.pallas import tpu as pltpu
from jax.sharding import PartitionSpec as P

HEADS = 8
HEAD_DIM = 64
SPAN = 128
STEP = 10
WIDTH = 512


eps_norm = 1e-05
neg_fill = -1e30
beta_one = 0.9
beta_two = 0.999
adam_eps = 1e-08
decay_coef = 0.1
rate_matrix = 0.05
rate_norm = 0.5
clip_bound = 1.0


def normalize(values_in, gain_row, shift_row):
    center = values_in - jnp.mean(values_in, axis=-1, keepdims=True)
    spread = jnp.mean(center * center, axis=-1, keepdims=True)
    return center * lax.rsqrt(spread + eps_norm) * gain_row + shift_row


def adamw_update(weight, grad_in, first_old, second_old, factor, step_rate, weight_decay):
    clipped = grad_in * factor
    first_new = beta_one * first_old + (1.0 - beta_one) * clipped
    second_new = beta_two * second_old + (1.0 - beta_two) * clipped * clipped
    first_hat = first_new / (1.0 - beta_one**STEP)
    second_hat = second_new / (1.0 - beta_two**STEP)
    weight_new = weight - step_rate * (
        first_hat / (jnp.sqrt(second_hat) + adam_eps) + weight_decay * weight
    )
    return (weight_new, first_new, second_new)


def generic_device(
    tokens,
    cotangent,
    lengths,
    w_qkv,
    w_out,
    w_up,
    w_down,
    norm_params,
    first_qkv,
    first_out,
    first_up,
    first_down,
    first_norm,
    second_qkv,
    second_out,
    second_up,
    second_down,
    second_norm,
):
    item_count, local_len, model_width = tokens.shape
    row_count = item_count * local_len
    spans_here = local_len // SPAN
    spans_all = spans_here * lax.axis_size("seq")
    seq_rank = lax.axis_index("seq")
    score_scale = HEAD_DIM ** (-0.5)
    full_qkv, full_out, full_up, full_down, full_norm = (
        lax.all_gather(w_qkv.astype(jnp.bfloat16), ("dp", "seq"), axis=0, tiled=True),
        lax.all_gather(w_out.astype(jnp.bfloat16), ("dp", "seq"), axis=0, tiled=True),
        lax.all_gather(w_up.astype(jnp.bfloat16), ("dp", "seq"), axis=0, tiled=True),
        lax.all_gather(w_down.astype(jnp.bfloat16), ("dp", "seq"), axis=0, tiled=True),
        lax.all_gather(norm_params.astype(jnp.bfloat16), ("dp", "seq"), axis=1, tiled=True),
    )
    norm_rows = full_norm.astype(jnp.float32)
    tokens_f = tokens.reshape(row_count, model_width).astype(jnp.float32)
    normed, back_one = jax.vjp(normalize, tokens_f, norm_rows[0], norm_rows[1])
    normed_b = normed.astype(jnp.bfloat16)
    qkv_b = jnp.dot(normed_b, full_qkv, preferred_element_type=jnp.float32).astype(jnp.bfloat16)
    qkv_view = qkv_b.reshape(item_count, spans_here, SPAN, 3, HEADS, HEAD_DIM)
    query_part = qkv_view[:, :, :, 0]
    key_part = qkv_view[:, :, :, 1]
    value_part = qkv_view[:, :, :, 2]
    local_pos = seq_rank * local_len + jnp.arange(local_len, dtype=jnp.int32)
    live_mask = (local_pos[None, :] < lengths[:, None]).reshape(item_count, spans_here, SPAN)
    live_f = live_mask.astype(jnp.float32)
    counts_here = jnp.maximum(jnp.sum(live_f, axis=2), 1.0)
    pooled = jnp.einsum(
        "ist,istchd->ischd",
        live_mask.astype(jnp.bfloat16),
        qkv_view[:, :, :, 1:],
        preferred_element_type=jnp.float32,
    )
    pooled = (pooled / counts_here[:, :, None, None, None]).astype(jnp.bfloat16)
    pooled_all = lax.all_gather(pooled, "seq", axis=1, tiled=True)
    pooled_keys = pooled_all[:, :, 0]
    pooled_values = pooled_all[:, :, 1]
    all_pos = jnp.arange(spans_all * SPAN, dtype=jnp.int32).reshape(spans_all, SPAN)
    counts_all = jnp.sum((all_pos[None] < lengths[:, None, None]).astype(jnp.float32), axis=2)
    span_ids = seq_rank * spans_here + jnp.arange(spans_here, dtype=jnp.int32)
    far_valid = (counts_all[:, None, :] > 0.0) & (
        span_ids[None, :, None] != jnp.arange(spans_all, dtype=jnp.int32)[None, None, :]
    )
    near_mask = live_mask[:, :, None, None, :]
    far_mask = far_valid[:, :, None, None, :]

    def scores_of():
        near_raw = (
            jnp.einsum(
                "isqhd,iskhd->ishqk", query_part, key_part, preferred_element_type=jnp.float32
            )
            * score_scale
        )
        far_raw = (
            jnp.einsum(
                "isqhd,irhd->ishqr", query_part, pooled_keys, preferred_element_type=jnp.float32
            )
            * score_scale
        )
        return (jnp.where(near_mask, near_raw, neg_fill), jnp.where(far_mask, far_raw, neg_fill))

    near_s, far_s = scores_of()
    score_top = jnp.maximum(
        jnp.max(near_s, axis=-1, keepdims=True), jnp.max(far_s, axis=-1, keepdims=True)
    )
    exp_total = jnp.sum(jnp.exp(near_s - score_top), axis=-1, keepdims=True) + jnp.sum(
        jnp.exp(far_s - score_top), axis=-1, keepdims=True
    )
    log_total = score_top + jnp.log(exp_total)
    near_pb = jnp.exp(near_s - log_total).astype(jnp.bfloat16)
    far_pb = jnp.exp(far_s - log_total).astype(jnp.bfloat16)
    mixed_rows = jnp.einsum(
        "ishqk,iskhd->isqhd", near_pb, value_part, preferred_element_type=jnp.float32
    )
    mixed_rows = mixed_rows + jnp.einsum(
        "ishqr,irhd->isqhd", far_pb, pooled_values, preferred_element_type=jnp.float32
    )
    mixed_b = mixed_rows.reshape(row_count, model_width).astype(jnp.bfloat16)
    residual = tokens_f + jnp.dot(mixed_b, full_out, preferred_element_type=jnp.float32)
    normed_two, back_two = jax.vjp(normalize, residual, norm_rows[2], norm_rows[3])
    normed_two_b = normed_two.astype(jnp.bfloat16)
    up_pre = jnp.dot(normed_two_b, full_up, preferred_element_type=jnp.float32)
    gated, gelu_back = jax.vjp(jax.nn.gelu, up_pre)
    gated_b = gated.astype(jnp.bfloat16)
    layer_out = residual + jnp.dot(gated_b, full_down, preferred_element_type=jnp.float32)
    activations = layer_out.astype(jnp.bfloat16).reshape(item_count, local_len, model_width)
    grad_out_b = cotangent.reshape(row_count, model_width)
    grad_down = jnp.dot(gated_b.T, grad_out_b, preferred_element_type=jnp.float32)
    grad_gated = jnp.dot(grad_out_b, full_down.T, preferred_element_type=jnp.float32)
    grad_up_pre = gelu_back(grad_gated)[0].astype(jnp.bfloat16)
    grad_up = jnp.dot(normed_two_b.T, grad_up_pre, preferred_element_type=jnp.float32)
    grad_normed_two = jnp.dot(grad_up_pre, full_up.T, preferred_element_type=jnp.float32)
    grad_resid_ln, grad_gain_two, grad_shift_two = back_two(grad_normed_two)
    grad_resid = grad_out_b.astype(jnp.float32) + grad_resid_ln
    grad_attn_b = grad_resid.astype(jnp.bfloat16)
    grad_out_proj = jnp.dot(mixed_b.T, grad_attn_b, preferred_element_type=jnp.float32)
    grad_mixed = jnp.dot(grad_attn_b, full_out.T, preferred_element_type=jnp.float32).astype(
        jnp.bfloat16
    )
    grad_mixed = grad_mixed.reshape(item_count, spans_here, SPAN, HEADS, HEAD_DIM)
    near_s, far_s = scores_of()
    near_pf = jnp.exp(near_s - log_total)
    far_pf = jnp.exp(far_s - log_total)
    near_pb = near_pf.astype(jnp.bfloat16)
    far_pb = far_pf.astype(jnp.bfloat16)
    grad_near = jnp.einsum(
        "isqhd,iskhd->ishqk", grad_mixed, value_part, preferred_element_type=jnp.float32
    )
    grad_far = jnp.einsum(
        "isqhd,irhd->ishqr", grad_mixed, pooled_values, preferred_element_type=jnp.float32
    )
    row_delta = jnp.sum(near_pf * grad_near, axis=-1, keepdims=True) + jnp.sum(
        far_pf * grad_far, axis=-1, keepdims=True
    )
    dscore_near = (near_pf * (grad_near - row_delta)).astype(jnp.bfloat16)
    dscore_far = (far_pf * (grad_far - row_delta)).astype(jnp.bfloat16)
    grad_query = jnp.einsum(
        "ishqk,iskhd->isqhd", dscore_near, key_part, preferred_element_type=jnp.float32
    )
    grad_query = (
        grad_query
        + jnp.einsum(
            "ishqr,irhd->isqhd", dscore_far, pooled_keys, preferred_element_type=jnp.float32
        )
    ) * score_scale
    grad_keys = (
        jnp.einsum(
            "ishqk,isqhd->iskhd", dscore_near, query_part, preferred_element_type=jnp.float32
        )
        * score_scale
    )
    grad_values = jnp.einsum(
        "ishqk,isqhd->iskhd", near_pb, grad_mixed, preferred_element_type=jnp.float32
    )
    grad_pool_keys = (
        jnp.einsum("ishqr,isqhd->irhd", dscore_far, query_part, preferred_element_type=jnp.float32)
        * score_scale
    )
    grad_pool_values = jnp.einsum(
        "ishqr,isqhd->irhd", far_pb, grad_mixed, preferred_element_type=jnp.float32
    )
    pool_grads = jnp.stack([grad_pool_keys, grad_pool_values], axis=2)
    pool_mine = lax.psum_scatter(
        pool_grads.astype(jnp.bfloat16), "seq", scatter_dimension=1, tiled=True
    ).astype(jnp.float32)
    spread_back = pool_mine / counts_here[:, :, None, None, None]
    grad_kv = (
        jnp.stack([grad_keys, grad_values], axis=3)
        + live_f[:, :, :, None, None, None] * spread_back[:, :, None]
    )
    grad_qkv_rows = jnp.concatenate([grad_query[:, :, :, None], grad_kv], axis=3)
    grad_qkv_b = grad_qkv_rows.reshape(row_count, 3 * model_width).astype(jnp.bfloat16)
    grad_qkv = jnp.dot(normed_b.T, grad_qkv_b, preferred_element_type=jnp.float32)
    grad_normed = jnp.dot(grad_qkv_b, full_qkv.T, preferred_element_type=jnp.float32)
    grad_in_ln, grad_gain_one, grad_shift_one = back_one(grad_normed)
    input_grad = (grad_resid + grad_in_ln).reshape(item_count, local_len, model_width)
    grad_norm_rows = jnp.stack([grad_gain_one, grad_shift_one, grad_gain_two, grad_shift_two])
    red_qkv, red_out, red_up, red_down, red_norm = (
        lax.psum_scatter(grad_qkv, ("dp", "seq"), scatter_dimension=0, tiled=True),
        lax.psum_scatter(grad_out_proj, ("dp", "seq"), scatter_dimension=0, tiled=True),
        lax.psum_scatter(grad_up, ("dp", "seq"), scatter_dimension=0, tiled=True),
        lax.psum_scatter(grad_down, ("dp", "seq"), scatter_dimension=0, tiled=True),
        lax.psum_scatter(grad_norm_rows, ("dp", "seq"), scatter_dimension=1, tiled=True),
    )
    squares = jnp.sum(red_qkv * red_qkv) + jnp.sum(red_out * red_out) + jnp.sum(red_up * red_up)
    squares = squares + jnp.sum(red_down * red_down) + jnp.sum(red_norm * red_norm)
    total_sq = lax.psum(squares, ("dp", "seq"))
    grad_norm = jnp.sqrt(total_sq)
    factor = clip_bound / jnp.maximum(grad_norm, clip_bound)
    new_qkv, new_first_qkv, new_second_qkv = adamw_update(
        w_qkv, red_qkv, first_qkv, second_qkv, factor, rate_matrix, decay_coef
    )
    new_out, new_first_out, new_second_out = adamw_update(
        w_out, red_out, first_out, second_out, factor, rate_matrix, decay_coef
    )
    new_up, new_first_up, new_second_up = adamw_update(
        w_up, red_up, first_up, second_up, factor, rate_matrix, decay_coef
    )
    new_down, new_first_down, new_second_down = adamw_update(
        w_down, red_down, first_down, second_down, factor, rate_matrix, decay_coef
    )
    new_norm, new_first_norm, new_second_norm = adamw_update(
        norm_params, red_norm, first_norm, second_norm, factor, rate_norm, 0.0
    )
    return (
        activations,
        input_grad,
        grad_norm,
        new_qkv,
        new_first_qkv,
        new_second_qkv,
        new_out,
        new_first_out,
        new_second_out,
        new_up,
        new_first_up,
        new_second_up,
        new_down,
        new_first_down,
        new_second_down,
        new_norm,
        new_first_norm,
        new_second_norm,
    )


BF = jnp.bfloat16
F32 = jnp.float32
MESH = pl.DeviceIdType.MESH
LANES = 128
TILE = 512
NN = (((1,), (0,)), ((), ()))
NT = (((1,), (1,)), ((), ()))
TN = (((0,), (0,)), ((), ()))
GATHER, SPREAD, PARTS, DOWN, OUTER, INNER, POOL, POOLBACK = 0, 22, 62, 94, 97, 105, 113, 120
NORM_SEQ, NORM_DP, SQUARE_SEQ, SQUARE_DP, COPIES = 127, 134, 137, 144, 147


def mm(left, right, dims=NN):
    return lax.dot_general(left, right, dims, preferred_element_type=F32)


def centered(values_in):
    center = values_in - jnp.mean(values_in, axis=-1, keepdims=True)
    scale = lax.rsqrt(jnp.mean(center * center, axis=-1, keepdims=True) + eps_norm)
    return center * scale, scale


def norm_back(grad_hat, hat, scale):
    mean_grad = jnp.mean(grad_hat, axis=-1, keepdims=True)
    mean_both = jnp.mean(grad_hat * hat, axis=-1, keepdims=True)
    return scale * (grad_hat - mean_grad - hat * mean_both)


def fold_rows(values_in):
    rows, width = values_in.shape
    return jnp.sum(values_in.reshape(rows // 8, 8, width), axis=0)


def layer_kernel(
    len_ref, x_any, dy_any, wq_ref, wo_ref, wu_ref, wd_ref, nrm_ref,
    act_any, dx_any, fin_q, fin_o, fin_u, fin_d, norm_sum, total_ref,
    bkv, bqo, bu, bd, qkv, mix, prob, dscore_s, gq, go, yacc, h2_s, ht_s, dyt_s, act_s, dup_s,
    own_p, s1p, r1p, s2ap, s2bp, r2ap, r2bp, r3ap, r3bp, s4p, r4p, fin_p, keep_d, s5d, r5d,
    s2aq, s2bq, s3q, r1q, r2aq, r2bq, r3aq, r3bq, r4q,
    s2ao, s2bo, s3o, r1o, r2ao, r2bo, r3ao, r3bo, r4o,
    pool_all, pool_far, pool_grad, pool_send, pool_recv, live_sum, spread_w,
    nrow, nacc, ntall, norm_seq, norm_dp, psq, psd, x_ref, dy_ref, dx_ref,
    send_sem, recv_sem, local_sem,
):
    ny, nc, nz, nx, blk, _ = bu.shape
    dblk = bd.shape[4]
    rows_all, width = x_ref.shape
    width3 = 3 * width
    ff = wu_ref.shape[1]
    seq_n = nz * nx
    dp_n = ny * nc
    local_len = rows_all // len_ref.shape[0]
    spans_here = local_len // SPAN
    blocks = rows_all // SPAN
    spans_all = spans_here * seq_n
    tiles = rows_all // TILE
    per_tile = TILE // SPAN
    pairs = width // LANES
    part_n = ff // nz
    ffn_rows = 2 * TILE
    dp_i = lax.axis_index("dp")
    sq_i = lax.axis_index("seq")
    y, c = dp_i // nc, dp_i % nc
    z, x = sq_i // nx, sq_i % nx

    def dev(yy, cc, zz, xx):
        return (yy * nc + cc, zz * nx + xx)

    twin = dev(y, 1 - c, z, x)
    over_x = dev(y, c, z, 1 - x)
    over_y = dev(1 - y, c, z, x)

    def seq_peer(step):
        return lax.rem(sq_i + step, seq_n)

    def dp_peer(step):
        return lax.rem(dp_i + step, dp_n)

    def z_peer(step):
        return lax.rem(z + step, nz)

    def hop(src, dst, index, target):
        return pltpu.make_async_remote_copy(
            src_ref=src, dst_ref=dst, send_sem=send_sem.at[index],
            recv_sem=recv_sem.at[index], device_id=target, device_id_type=MESH,
        )

    def start(hops):
        for one in hops:
            one.start()

    def arrived(hops):
        for one in hops:
            one.wait_recv()

    def sent(hops):
        for one in hops:
            one.wait_send()

    def each(count, body):
        def step(index, carry):
            body(index)
            return carry

        lax.fori_loop(0, count, step, 0)

    def tile_rows(tile):
        return pl.ds(pl.multiple_of(tile * TILE, TILE), TILE)

    load_x = pltpu.make_async_copy(x_any, x_ref, local_sem.at[0])
    load_dy = pltpu.make_async_copy(dy_any, dy_ref, local_sem.at[1])
    keep_act = pltpu.make_async_copy(dy_ref, act_any, local_sem.at[2])
    keep_dx = pltpu.make_async_copy(dx_ref, dx_any, local_sem.at[3])
    load_dy.start()
    load_x.start()

    barrier = pltpu.get_barrier_semaphore()
    for step in range(1, seq_n):
        pl.semaphore_signal(
            barrier, inc=1, device_id=(dp_i, seq_peer(step)), device_id_type=MESH
        )
    for step in range(1, dp_n):
        pl.semaphore_signal(
            barrier, inc=1, device_id=(dp_peer(step), sq_i), device_id_type=MESH
        )

    bkv[y, c, z, x, :, 0 : 2 * width] = wq_ref[:, width:].astype(BF)
    bqo[y, c, z, x, :, 0:width] = wq_ref[:, 0:width].astype(BF)
    bqo[y, c, z, x, :, width:] = wo_ref[...].astype(BF)
    count = nrm_ref.shape[0]
    ntall[...] = jnp.zeros_like(ntall)
    ntall[0:count, 0:blk] = nrm_ref[...]
    bkv[y, c, z, x, :, 2 * width :] = ntall[...].T[0:blk].astype(BF)
    for part in range(nz):
        for group in range(dp_n):
            lo, at = part * part_n + group * LANES, (group * nz + part) * LANES
            bu[y, c, z, x, :, lo : lo + LANES] = wu_ref[:, at : at + LANES].astype(BF)
    bd[y, c, z, x] = wd_ref[...].astype(BF)
    pl.semaphore_wait(barrier, seq_n + dp_n - 2)

    def gather_hops(full, base):
        cut = (full.shape[5] // 2) // LANES * LANES
        one, two = pl.ds(0, cut), pl.ds(cut, full.shape[5] - cut)

        def same(part, index, target):
            return hop(part, part, base + index, target)

        first = [
            same(full.at[y, c, z, x], step - 1, dev(y, c, z_peer(step), x))
            for step in range(1, nz)
        ]
        second = [
            same(full.at[y, c, :, x, :, one], 3, over_x),
            same(full.at[y, c, :, x, :, two], 4, over_y),
        ]
        third = [
            same(full.at[y, c, :, :, :, one], 5, over_y),
            same(full.at[:, c, :, x, :, two], 6, over_x),
        ]
        last = [same(full.at[:, c], 7, twin)]
        return first, second, third, last

    def direct(full, base):
        mine = full.at[y, c, z, x]
        return [
            hop(mine, mine, base + step - 1, dev(y, c, z_peer(step), x)) for step in range(1, nz)
        ]

    def spread_hops(part):
        base = SPREAD + part * 10
        cols = pl.ds(pl.multiple_of(part * part_n, part_n), part_n)
        one = pl.ds(pl.multiple_of(part * part_n, LANES), part_n // 2)
        two = pl.ds(pl.multiple_of(part * part_n + part_n // 2, LANES), part_n // 2)
        d_one, d_two = pl.ds(0, width // 2), pl.ds(width // 2, width // 2)

        def same(place, index, target):
            return hop(place, place, base + index, target)

        return (
            [
                same(bu.at[y, c, :, x, :, one], 0, over_x),
                same(bu.at[y, c, :, x, :, two], 1, over_y),
                same(bd.at[y, c, part, x, :, d_one], 2, over_x),
                same(bd.at[y, c, part, x, :, d_two], 3, over_y),
            ],
            [
                same(bu.at[y, c, :, :, :, one], 4, over_y),
                same(bu.at[:, c, :, x, :, two], 5, over_x),
                same(bd.at[y, c, part, :, :, d_one], 6, over_y),
                same(bd.at[:, c, part, x, :, d_two], 7, over_x),
            ],
            [
                same(bu.at[:, c, :, :, :, cols], 8, twin),
                same(bd.at[:, c, part], 9, twin),
            ],
        )

    def pass_on(part, stage):
        hops = spread_hops(part)
        arrived(hops[stage])
        start(hops[stage + 1])

    hops_kv = gather_hops(bkv, GATHER)
    hops_qo = gather_hops(bqo, GATHER + 8)
    direct_u = direct(bu, GATHER + 16)
    direct_d = direct(bd, GATHER + 19)
    start(hops_kv[0])
    start(hops_qo[0])
    start(direct_u)
    start(direct_d)
    nacc[...] = jnp.zeros_like(nacc)
    arrived(hops_kv[0])
    start(hops_kv[1])
    load_dy.wait()

    def turn_dy(tile):
        rows = tile_rows(tile)
        dyt_s[:, rows] = dy_ref[rows, :].astype(F32).T.astype(BF)

    each(tiles // 2, turn_dy)
    arrived(hops_kv[1])
    start(hops_kv[2])
    arrived(hops_qo[0])
    start(hops_qo[1])
    load_x.wait()
    each(tiles // 2, lambda tile: turn_dy(tile + tiles // 2))
    arrived(hops_kv[2])
    start(hops_kv[3])
    arrived(hops_qo[1])
    start(hops_qo[2])
    arrived(direct_u)
    arrived(direct_d)
    for part in range(nz):
        start(spread_hops(part)[0])
    arrived(hops_kv[3])

    norm_cols = bkv[:, :, :, :, :, 2 * width :].reshape(width, LANES).astype(F32)
    nrow[...] = norm_cols.T[0:8]

    def w_qkv(part):
        if part == 0:
            return bqo[:, :, :, :, :, 0:width].reshape(width, width)
        return bkv[:, :, :, :, :, (part - 1) * width : part * width].reshape(width, width)

    def first_norm(rows):
        hat, scale = centered(x_ref[rows, :].astype(F32))
        return hat, scale, (hat * nrow[0:1, :] + nrow[1:2, :]).astype(BF)

    def live_pick(tile):
        block_at = lax.broadcasted_iota(jnp.int32, (blocks, TILE), 0)
        row_at = lax.broadcasted_iota(jnp.int32, (blocks, TILE), 1) + tile * TILE
        pos = sq_i * local_len + lax.rem(row_at, local_len)
        item = row_at // local_len
        length = jnp.zeros((blocks, TILE), jnp.int32)
        for i in range(TILE // local_len):
            at = tile * (TILE // local_len) + i
            length = jnp.where(item == at, len_ref[at], length)
        return jnp.where((row_at // SPAN == block_at) & (pos < length), 1.0, 0.0).astype(BF)

    def kv_tile(tile, pooled):
        rows = tile_rows(tile)
        _, _, h1 = first_norm(rows)
        h2_s[rows, :] = h1
        for part in (1, 2):
            qkv[rows, pl.ds(part * width, width)] = mm(h1, w_qkv(part)).astype(BF)

        @pl.when(tile == 3)
        def _():
            arrived(hops_qo[2])
            start(hops_qo[3])

        return pooled + mm(live_pick(tile), qkv[rows, width:])

    pooled = lax.fori_loop(0, tiles, kv_tile, jnp.zeros((blocks, 2 * width), F32))
    block_col = lax.broadcasted_iota(jnp.int32, (blocks, 1), 0)
    length_col = jnp.zeros((blocks, 1), jnp.int32)
    for i in range(blocks // spans_here):
        length_col = jnp.where(block_col // spans_here == i, len_ref[i], length_col)
    first_pos = sq_i * local_len + lax.rem(block_col, spans_here) * SPAN
    count_col = jnp.clip(length_col - first_pos, 1, SPAN).astype(F32)
    pool_all[sq_i] = (pooled / count_col).astype(BF)
    pool_hops = [
        hop(pool_all.at[sq_i], pool_all.at[sq_i], POOL + step - 1, (dp_i, seq_peer(step)))
        for step in range(1, seq_n)
    ]
    start(pool_hops)
    pass_on(0, 0)
    arrived(hops_qo[3])

    def q_tile(tile):
        rows = tile_rows(tile)
        qkv[rows, 0:width] = mm(h2_s[rows, :], w_qkv(0)).astype(BF)

    each(tiles, q_tile)
    arrived(pool_hops)

    far_n = seq_n * blocks
    to_row = lax.broadcasted_iota(jnp.int32, (far_n, far_n), 0)
    to_col = lax.broadcasted_iota(jnp.int32, (far_n, far_n), 1)
    item_row, span_row = to_row // spans_all, to_row % spans_all
    wanted = (span_row // spans_here) * blocks + item_row * spans_here + span_row % spans_here
    order = jnp.where(wanted == to_col, 1.0, 0.0).astype(BF)
    pool_far[...] = mm(order, pool_all[...].reshape(far_n, 2 * width)).astype(BF)

    keys_n = SPAN + spans_all
    lane = lax.broadcasted_iota(jnp.int32, (1, LANES), 1)
    score_scale = HEAD_DIM ** (-0.5)
    half_a = jnp.where(lane < HEAD_DIM, 1.0, 0.0)
    half_b = jnp.where(lane >= HEAD_DIM, 1.0, 0.0)
    query_a, query_b = (half_a * score_scale).astype(BF), (half_b * score_scale).astype(BF)
    grad_a, grad_b = half_a.astype(BF), half_b.astype(BF)

    def both(near_rows, far_rows, cols):
        far_cols = pl.ds(cols.start - width, cols.size)
        return jnp.concatenate([qkv[near_rows, cols], pool_far[far_rows, far_cols]], axis=0)

    def cols_of(third, pair):
        return pl.ds(third * width + pair * LANES, LANES)

    def by_head(rows_in, first, second):
        return jnp.concatenate([rows_in * first, rows_in * second], axis=0)

    units = [(sub, pair) for sub in range(spans_here) for pair in range(pairs)]
    items = blocks // spans_here

    def rows_of(item, sub):
        return pl.ds(pl.multiple_of(item * local_len + sub * SPAN, SPAN), SPAN)

    def far_of(item):
        return pl.ds(pl.multiple_of(item * spans_all, spans_all), spans_all)

    def attend(item):
        for at, moves in (
            (0, ((1, 0),)), (1, ((0, 1),)), (2, ((2, 0),)), (3, ((1, 1),)),
            (4, ((3, 0),)), (6, ((2, 1),)), (7, ((3, 1),)),
        ):

            @pl.when(item == at)
            def _(moves=moves):
                for part, stage in moves:
                    pass_on(part, stage)

        far_rows = far_of(item)
        length = len_ref[item]
        key_at = lax.broadcasted_iota(jnp.int32, (keys_n, 2 * SPAN), 0)
        span_at = key_at - SPAN

        def seen(sub):
            mine = sq_i * spans_here + sub
            near_ok = (key_at < SPAN) & (mine * SPAN + key_at < length)
            return near_ok | ((key_at >= SPAN) & (span_at * SPAN < length) & (span_at != mine))

        scores = []
        for sub, pair in units:
            rows = rows_of(item, sub)
            kk = both(rows, far_rows, cols_of(1, pair))
            scores.append(mm(kk, by_head(qkv[rows, cols_of(0, pair)], query_a, query_b), NT))
        for (sub, pair), score in zip(units, scores):
            score = jnp.where(seen(sub), score, neg_fill)
            raised = jnp.exp(score - jnp.max(score, axis=0, keepdims=True))
            share = raised * (1.0 / jnp.sum(raised, axis=0, keepdims=True))
            prob[item * spans_here + sub, pair] = share.astype(BF)
        for sub in range(spans_here):
            rows = rows_of(item, sub)
            mixed = []
            for pair in range(pairs):
                vv = both(rows, far_rows, cols_of(2, pair))
                stacked = mm(vv, prob[item * spans_here + sub, pair], TN)
                mixed += [stacked[0:HEAD_DIM, 0:SPAN], stacked[HEAD_DIM:, SPAN:]]
            mix[rows, :] = jnp.concatenate(mixed, axis=0).T.astype(BF)

    each(items, attend)
    for group in (*hops_kv, *hops_qo, direct_u, direct_d, pool_hops):
        sent(group)

    w_out = bqo[:, :, :, :, :, width:].reshape(width, width)
    gelu_in = math.sqrt(2.0 / math.pi)
    gelu_cube = 0.044715

    def second_norm(rows):
        x1 = x_ref[rows, :].astype(F32) + mm(mix[rows, :], w_out)
        hat, scale = centered(x1)
        return x1, hat, scale

    def ffn_open(tile):
        rows = tile_rows(tile)
        x1, hat, _ = second_norm(rows)
        yacc[rows, :] = x1
        dx_ref[rows, :] = jnp.zeros((TILE, width), F32)
        h2 = hat * nrow[2:3, :] + nrow[3:4, :]
        h2_s[rows, :] = h2.astype(BF)
        ht_s[:, rows] = h2.T.astype(BF)

    each(tiles, ffn_open)

    half_cols = width // 2
    one_p, two_p = pl.ds(0, half_cols), pl.ds(half_cols, half_cols)
    up_rows = nz * blk

    def part_hops(part):
        base = PARTS + part * 8
        return (
            [hop(s1p, r1p.at[part], base, twin)],
            [
                hop(s1p.at[1 - y, :, :, one_p], r2ap.at[part], base + 1, over_y),
                hop(s1p.at[:, 1 - x, :, two_p], r2bp.at[part], base + 2, over_x),
            ],
            [
                hop(s2ap.at[1 - x], r3ap.at[part], base + 3, over_x),
                hop(s2bp.at[1 - y], r3bp.at[part], base + 4, over_y),
            ],
            [
                hop(
                    s4p.at[part, z_peer(step)], r4p.at[step - 1, part], base + 4 + step,
                    dev(y, c, z_peer(step), x),
                )
                for step in range(1, nz)
            ],
        )

    def down_cols(group):
        cols = pl.ds(pl.multiple_of(group * LANES, LANES), LANES)
        return gq[:, :, :, :, :, cols].reshape(width, LANES)

    def part_first(part):
        for yy in range(ny):
            for xx in range(nx):
                for zz in range(nz):
                    at = pl.ds(zz * blk, blk)
                    own_p[yy, xx, at] = go[yy, c, zz, xx]
                    s1p[yy, xx, at] = go[yy, 1 - c, zz, xx].astype(BF)
            mine = down_cols(yy * nc + c).T
            other = down_cols(yy * nc + 1 - c).T
            for xx in range(nx):
                own_p[yy, xx, up_rows:] = mine[xx * dblk : (xx + 1) * dblk]
                s1p[yy, xx, up_rows:] = other[xx * dblk : (xx + 1) * dblk].astype(BF)
        start(part_hops(part)[0])

    def part_second(part):
        hops = part_hops(part)
        arrived(hops[0])
        sent(hops[0])

        def add(index):
            yy, xx = index // nx, index % nx
            total = own_p[yy, xx] + r1p[part, yy, xx].astype(F32)
            own_p[yy, xx] = total
            s1p[yy, xx] = total.astype(BF)

        each(ny * nx, add)
        start(hops[1])

    def part_third(part):
        hops = part_hops(part)
        arrived(hops[1])
        sent(hops[1])
        for xx in range(nx):
            total = own_p[y, xx, :, one_p] + r2ap[part, xx].astype(F32)
            own_p[y, xx, :, one_p] = total
            s2ap[xx] = total.astype(BF)
        for yy in range(ny):
            total = own_p[yy, x, :, two_p] + r2bp[part, yy].astype(F32)
            own_p[yy, x, :, two_p] = total
            s2bp[yy] = total.astype(BF)
        start(hops[2])

    def part_fourth(part):
        hops = part_hops(part)
        arrived(hops[2])
        sent(hops[2])
        own_p[y, x, :, one_p] += r3ap[part].astype(F32)
        own_p[y, x, :, two_p] += r3bp[part].astype(F32)
        for zz in range(nz):
            s4p[part, zz] = own_p[y, x, zz * blk : (zz + 1) * blk].astype(BF)
        fin_p[part] = own_p[y, x, pl.ds(pl.multiple_of(z * blk, blk), blk)]
        down = own_p[y, x, up_rows:]
        keep_d[part] = down
        s5d[part] = down.astype(BF)
        start(hops[3])

    down_hops = [
        hop(
            s5d.at[z_peer(step)], r5d.at[step - 1], DOWN + step - 1, dev(y, c, z_peer(step), x)
        )
        for step in range(1, nz)
    ]

    def ffn_part(part, carry):
        cols = pl.ds(pl.multiple_of(part * part_n, part_n), part_n)
        arrived(spread_hops(part)[2])
        w_up = bu[:, :, :, :, :, cols].reshape(width, part_n)
        w_down = bd[:, :, part].reshape(part_n, width)

        def ffn_tile(tile):
            @pl.when((part > 0) & (tile == 1))
            def _():
                part_second(part - 1)

            rows = pl.ds(pl.multiple_of(tile * ffn_rows, ffn_rows), ffn_rows)
            for piece in range(ffn_rows // TILE):
                some = tile_rows(tile * (ffn_rows // TILE) + piece)
                up = mm(h2_s[some, :], w_up)
                square = up * up
                bent = jnp.tanh(up * (gelu_in + (gelu_in * gelu_cube) * square))
                half = 0.5 + 0.5 * bent
                act_s[some, :] = (up * half).astype(BF)
                rate = half + (up * (1.0 - bent * bent)) * (
                    0.5 * gelu_in + (1.5 * gelu_in * gelu_cube) * square
                )
                dup_s[some, :] = (mm(dy_ref[some, :], w_down, NT) * rate).astype(BF)
            yacc[rows, :] += mm(act_s[rows, :], w_down)
            dx_ref[rows, :] += mm(dup_s[rows, :], w_up, NT)

        each(rows_all // ffn_rows, ffn_tile)

        @pl.when(part > 0)
        def _():
            part_third(part - 1)

        gq[:, :, :, :, :, 0:part_n] = mm(dyt_s[...], act_s[...]).reshape(go.shape)
        go[...] = mm(ht_s[...], dup_s[...]).reshape(go.shape)

        @pl.when(part > 0)
        def _():
            part_fourth(part - 1)

        part_first(part)
        return carry

    lax.fori_loop(0, nz, ffn_part, 0)

    def ffn_close(tile):
        @pl.when(tile == 1)
        def _():
            part_second(nz - 1)

        rows = tile_rows(tile)
        _, hat, scale = second_norm(rows)
        dh2 = dx_ref[rows, :]
        nacc[2] += fold_rows(dh2 * hat)
        nacc[3] += fold_rows(dh2)
        dx1 = dy_ref[rows, :].astype(F32) + norm_back(dh2 * nrow[2:3, :], hat, scale)
        dy_ref[rows, :] = yacc[rows, :].astype(BF)
        dx_ref[rows, :] = dx1
        dz = dx1.astype(BF)
        act_s[rows, :] = dz
        ht_s[:, rows] = mix[rows, :].astype(F32).T.astype(BF)
        mix[rows, :] = mm(dz, w_out, NT).astype(BF)

    each(tiles, ffn_close)
    keep_act.start()
    for part in range(nz):
        for group in spread_hops(part):
            sent(group)
    go[...] = mm(ht_s[...], act_s[...]).reshape(go.shape)

    def reduce_steps(full, s1, r1, s2a, s2b, r2a, r2b, r3a, r3b, s3, r4, fin, base):
        own = full.at[:, c]
        n = s1.shape[4]
        cut = (n // 2) // LANES * LANES
        one, two = pl.ds(0, cut), pl.ds(cut, n - cut)
        hop1 = [hop(s1, r1, base, twin)]
        hop2 = [
            hop(s1.at[1 - y, :, :, :, one], r2a, base + 1, over_y),
            hop(s1.at[:, :, 1 - x, :, two], r2b, base + 2, over_x),
        ]
        hop3 = [
            hop(s2a.at[:, 1 - x], r3a, base + 3, over_x),
            hop(s2b.at[1 - y], r3b, base + 4, over_y),
        ]
        hop4 = [
            hop(
                s3.at[z_peer(step)], r4.at[step - 1], base + 4 + step,
                dev(y, c, z_peer(step), x),
            )
            for step in range(1, nz)
        ]

        def places(index):
            return index // (nz * nx), (index // nx) % nz, index % nx

        def stage1():
            def load(index):
                yy, zz, xx = places(index)
                s1[yy, zz, xx] = full[yy, 1 - c, zz, xx].astype(BF)

            each(ny * nz * nx, load)
            start(hop1)

        def stage2():
            arrived(hop1)
            sent(hop1)

            def add(index):
                yy, zz, xx = places(index)
                total = own[yy, zz, xx] + r1[yy, zz, xx].astype(F32)
                own[yy, zz, xx] = total
                s1[yy, zz, xx] = total.astype(BF)

            each(ny * nz * nx, add)
            start(hop2)

        def stage3():
            arrived(hop2)
            for zz in range(nz):
                for xx in range(nx):
                    total = own[y, zz, xx, :, one] + r2a[zz, xx].astype(F32)
                    own[y, zz, xx, :, one] = total
                    s2a[zz, xx] = total.astype(BF)
            start(hop3[0:1])
            for yy in range(ny):
                for zz in range(nz):
                    total = own[yy, zz, x, :, two] + r2b[yy, zz].astype(F32)
                    own[yy, zz, x, :, two] = total
                    s2b[yy, zz] = total.astype(BF)
            start(hop3[1:2])

        def stage4():
            arrived(hop3)
            for zz in range(nz):
                total = own[y, zz, x, :, one] + r3a[zz].astype(F32)
                own[y, zz, x, :, one] = total
                s3[zz, :, one] = total.astype(BF)
                total = own[y, zz, x, :, two] + r3b[zz].astype(F32)
                own[y, zz, x, :, two] = total
                s3[zz, :, two] = total.astype(BF)
            start(hop4)

        def stage5():
            arrived(hop4)
            total = own[y, z, x]
            for step in range(nz - 1):
                total = total + r4[step].astype(F32)
            fin[...] = total
            sent(hop2)
            sent(hop3)
            sent(hop4)

        return stage1, stage2, stage3, stage4, stage5

    red_o = reduce_steps(
        go, bu.at[:, 0, :, :, :, pl.ds(0, width)], r1o, s2ao, s2bo, r2ao, r2bo, r3ao, r3bo, s3o,
        r4o, fin_o, OUTER,
    )
    red_q = reduce_steps(
        gq, bu.at[:, 1, :, :, :, pl.ds(0, width3)], r1q, s2aq, s2bq, r2aq, r2bq, r3aq, r3bq,
        s3q, r4q, fin_q, INNER,
    )
    red_o[0]()

    def last_third():
        part_third(nz - 1)

    def fourth_and_down():
        part_fourth(nz - 1)
        start(down_hops)

    def attend_back(item):
        for at, step in (
            (0, last_third), (2, fourth_and_down), (3, red_o[1]), (5, red_o[2]), (7, red_o[3])
        ):

            @pl.when(item == at)
            def _(step=step):
                step()

        far_rows = far_of(item)
        dshares = []
        for sub, pair in units:
            rows = rows_of(item, sub)
            vv = both(rows, far_rows, cols_of(2, pair))
            dshares.append(mm(vv, by_head(mix[rows, cols_of(0, pair)], grad_a, grad_b), NT))
        for (sub, pair), dshare in zip(units, dshares):
            share = prob[item * spans_here + sub, pair].astype(F32)
            inner = jnp.sum(share * dshare, axis=0, keepdims=True)
            dscore_s[sub, pair] = (share * (dshare - inner)).astype(BF)
        far_k, far_v = [0.0] * pairs, [0.0] * pairs
        for sub in range(spans_here):
            rows = rows_of(item, sub)
            dqs = []
            for pair in range(pairs):
                dscore = dscore_s[sub, pair]
                stacked = mm(both(rows, far_rows, cols_of(1, pair)), dscore, TN)
                dqs += [stacked[0:HEAD_DIM, 0:SPAN], stacked[HEAD_DIM:, SPAN:]]
                dk = mm(dscore, by_head(qkv[rows, cols_of(0, pair)], query_a, query_b))
                dv = mm(
                    prob[item * spans_here + sub, pair],
                    by_head(mix[rows, cols_of(0, pair)], grad_a, grad_b),
                )
                qkv[rows, cols_of(1, pair)] = dk[0:SPAN].astype(BF)
                qkv[rows, cols_of(2, pair)] = dv[0:SPAN].astype(BF)
                far_k[pair] = far_k[pair] + dk[SPAN:]
                far_v[pair] = far_v[pair] + dv[SPAN:]
            dq = jnp.concatenate(dqs, axis=0).T * score_scale
            qkv[rows, 0:width] = dq.astype(BF)
        for pair in range(pairs):
            pool_grad[far_rows, cols_of(0, pair)] = far_k[pair]
            pool_grad[far_rows, cols_of(1, pair)] = far_v[pair]

    each(items, attend_back)

    back_row = lax.broadcasted_iota(jnp.int32, (far_n, far_n), 0)
    back_col = lax.broadcasted_iota(jnp.int32, (far_n, far_n), 1)
    owner, place = back_row // blocks, back_row % blocks
    source = (place // spans_here) * spans_all + owner * spans_here + place % spans_here
    reorder = jnp.where(source == back_col, 1.0, 0.0).astype(BF)
    pool_send[...] = (
        mm(reorder, pool_grad[...].astype(BF)).astype(BF).reshape(seq_n, blocks, 2 * width)
    )
    back_hops = [
        hop(
            pool_send.at[seq_peer(step)], pool_recv.at[step - 1], POOLBACK + step - 1,
            (dp_i, seq_peer(step)),
        )
        for step in range(1, seq_n)
    ]
    start(back_hops)

    live_sum[...] = jnp.zeros_like(live_sum)

    def turn_h1(tile):
        rows = tile_rows(tile)
        _, _, h1 = first_norm(rows)
        ht_s[:, rows] = h1.astype(F32).T.astype(BF)
        live_sum[...] += mm(live_pick(tile), h1)

    each(tiles, turn_h1)
    for part in range(3):
        cols = pl.ds(part * width, width)
        gq[:, :, :, :, :, cols] = mm(ht_s[...], qkv[:, cols]).reshape(
            ny, nc, nz, nx, blk, width
        )
    for part in range(nz):
        arrived(part_hops(part)[3])
        total = fin_p[part]
        for step in range(nz - 1):
            total = total + r4p[step, part].astype(F32)
        for group in range(dp_n):
            at = (group * nz + part) * LANES
            fin_u[:, at : at + LANES] = total[:, group * LANES : (group + 1) * LANES]
    arrived(down_hops)
    total = keep_d[z]
    for step in range(nz - 1):
        total = total + r5d[step].astype(F32)
    fin_d[...] = total
    red_o[4]()

    arrived(back_hops)
    pool_total = pool_send[sq_i].astype(F32)
    for step in range(seq_n - 1):
        pool_total = pool_total + pool_recv[step].astype(F32)
    far = pool_total / count_col
    far_hi = far.astype(BF)
    far_lo = (far - far_hi.astype(F32)).astype(BF)
    near = live_sum[...]
    near_hi = near.astype(BF)
    near_lo = (near - near_hi.astype(F32)).astype(BF)
    left = jnp.concatenate([near_hi, near_lo, near_hi], axis=0)
    right = jnp.concatenate([far_hi, far_hi, far_lo], axis=0)
    for part in range(2):
        cols = pl.ds((part + 1) * width, width)
        gq[:, :, :, :, :, cols] += mm(left, right[:, part * width : (part + 1) * width], TN).reshape(
            ny, nc, nz, nx, blk, width
        )
    red_q[0]()
    far_two = jnp.concatenate([far_hi, far_lo], axis=0)
    both_far = mm(far_two[:, 0:width], w_qkv(1), NT) + mm(far_two[:, width:], w_qkv(2), NT)
    spread_w[...] = both_far[0:blocks] + both_far[blocks:]

    def last_tile(tile):
        for at, step in ((1, red_q[1]), (3, red_q[2])):

            @pl.when(tile == at)
            def _(step=step):
                step()

        rows = tile_rows(tile)
        hat, scale, _ = first_norm(rows)
        extra = []
        for part in range(per_tile):
            block = tile * per_tile + part
            pos = (
                sq_i * local_len
                + lax.rem(block, spans_here) * SPAN
                + lax.broadcasted_iota(jnp.int32, (SPAN, 1), 0)
            )
            live = jnp.where(pos < len_ref[block // spans_here], 1.0, 0.0)
            extra.append(live * spread_w[pl.ds(block, 1), :])
        dh1 = jnp.concatenate(extra, axis=0)
        for part in range(3):
            dh1 = dh1 + mm(qkv[rows, pl.ds(part * width, width)], w_qkv(part), NT)
        nacc[0] += fold_rows(dh1 * hat)
        nacc[1] += fold_rows(dh1)
        dx_ref[rows, :] += norm_back(dh1 * nrow[0:1, :], hat, scale)

    each(tiles, last_tile)
    keep_dx.start()
    norm_rows = [jnp.sum(nacc[k], axis=0, keepdims=True) for k in range(4)]
    norm_rows.append(jnp.zeros((4, width), F32))
    norm_seq[sq_i] = jnp.concatenate(norm_rows, axis=0)
    norm_hops = [
        hop(norm_seq.at[sq_i], norm_seq.at[sq_i], NORM_SEQ + step - 1, (dp_i, seq_peer(step)))
        for step in range(1, seq_n)
    ]
    norm_hops_dp = [
        hop(norm_dp.at[dp_i], norm_dp.at[dp_i], NORM_DP + step - 1, (dp_peer(step), sq_i))
        for step in range(1, dp_n)
    ]
    start(norm_hops)
    red_q[3]()
    arrived(norm_hops)
    total = norm_seq[0]
    for k in range(1, seq_n):
        total = total + norm_seq[k]
    norm_dp[dp_i] = total
    start(norm_hops_dp)

    def partial(values_in):
        squares = fold_rows(values_in * values_in)
        return sum(
            squares[:, k * LANES : (k + 1) * LANES] for k in range(squares.shape[1] // LANES)
        )

    early = partial(fin_u[...]) + partial(fin_d[...]) + partial(fin_o[...])
    red_q[4]()
    psq[sq_i] = early + partial(fin_q[...])
    seq_hops = [
        hop(psq.at[sq_i], psq.at[sq_i], SQUARE_SEQ + step - 1, (dp_i, seq_peer(step)))
        for step in range(1, seq_n)
    ]
    start(seq_hops)
    sent(back_hops)
    for part in range(nz):
        sent(part_hops(part)[3])
    sent(down_hops)
    sent(norm_hops)
    arrived(norm_hops_dp)
    sent(norm_hops_dp)
    total = norm_dp[0]
    for k in range(1, dp_n):
        total = total + norm_dp[k]
    norm_sum[...] = total
    arrived(seq_hops)
    total = psq[0]
    for k in range(1, seq_n):
        total = total + psq[k]
    psd[dp_i] = total
    dp_hops = [
        hop(psd.at[dp_i], psd.at[dp_i], SQUARE_DP + step - 1, (dp_peer(step), sq_i))
        for step in range(1, dp_n)
    ]
    start(dp_hops)
    arrived(dp_hops)
    total = psd[0]
    for k in range(1, dp_n):
        total = total + psd[k]
    total_ref[...] = total
    sent(seq_hops)
    sent(dp_hops)
    keep_act.wait()
    keep_dx.wait()


def update_kernel(
    act_in, dx_in, total_ref, gq_ref, go_ref, gu_ref, gd_ref, gn_ref,
    wq_ref, wo_ref, wu_ref, wd_ref, wn_ref, fq_ref, fo_ref, fu_ref, fd_ref, fn_ref,
    sq_ref, so_ref, su_ref, sd_ref, sn_ref,
    act_out, dx_out, norm_ref, nq, nfq, nsq, no, nfo, nso, nu, nfu, nsu, nd, nfd, nsd,
    nn, nfn, nsn, act_s, dx_s, sems_in, sems_out,
):
    pieces = 4
    piece = act_s.shape[0] // pieces
    moves = []
    for k in range(pieces):
        rows = pl.ds(k * piece, piece)
        for n, (src, mid, dst) in enumerate(
            ((dx_in, dx_s, dx_out), (act_in, act_s, act_out))
        ):
            moves.append((
                pltpu.make_async_copy(src.at[rows], mid.at[rows], sems_in.at[n * pieces + k]),
                pltpu.make_async_copy(mid.at[rows], dst.at[rows], sems_out.at[n * pieces + k]),
            ))
    for inward, _ in moves:
        inward.start()
    norm_grads = gn_ref[...]
    total = jnp.sum(total_ref[...]) + jnp.sum(norm_grads * norm_grads)
    total = jnp.full((1, 1), total, F32)
    grad_norm = jnp.sqrt(total)
    factor = clip_bound / jnp.maximum(grad_norm, clip_bound)
    norm_ref[...] = grad_norm

    def update(weight, grad_in, first, second, outs, rate, decay):
        new = adamw_update(weight, grad_in, first, second, factor, rate, decay)
        for out, value in zip(outs, new):
            out[...] = value

    for inward, outward in moves:
        inward.wait()
        outward.start()
    for w, g, m, s, outs in (
        (wq_ref, gq_ref, fq_ref, sq_ref, (nq, nfq, nsq)),
        (wo_ref, go_ref, fo_ref, so_ref, (no, nfo, nso)),
        (wu_ref, gu_ref, fu_ref, su_ref, (nu, nfu, nsu)),
        (wd_ref, gd_ref, fd_ref, sd_ref, (nd, nfd, nsd)),
    ):
        update(w[...], g[...], m[...], s[...], outs, rate_matrix, decay_coef)
    count, cols = wn_ref.shape
    width = norm_grads.shape[1]
    place = (lax.axis_index("dp") * lax.axis_size("seq") + lax.axis_index("seq")) * cols
    turned = pltpu.roll(norm_grads, lax.rem(width - place, width), 1)
    update(
        wn_ref[...], turned[0:count, 0:cols], fn_ref[...], sn_ref[...], (nn, nfn, nsn),
        rate_norm, 0.0,
    )
    for _, outward in moves:
        outward.wait()


def fused_device(
    tokens, cotangent, lengths, w_qkv, w_out, w_up, w_down, norm_params,
    first_qkv, first_out, first_up, first_down, first_norm,
    second_qkv, second_out, second_up, second_down, second_norm,
):
    item_count, local_len, width = tokens.shape
    rows_all = item_count * local_len
    dp_n, seq_n = lax.axis_size("dp"), lax.axis_size("seq")
    nc = 2
    ny = dp_n // nc
    nx = ny
    nz = seq_n // nx
    blk, width3 = w_qkv.shape
    ff = w_up.shape[1]
    dblk = w_down.shape[0]
    blocks = rows_all // SPAN
    far_n = seq_n * blocks
    keys_n = SPAN + local_len // SPAN * seq_n
    part_n = ff // nz
    up_rows = nz * blk
    half = width // 2

    def bufs(b, n):
        cut = (n // 2) // LANES * LANES
        rest = n - cut
        taken = [pltpu.VMEM((nz, nx, b, cut), BF), pltpu.VMEM((ny, nz, b, rest), BF)]
        return [
            *taken,
            pltpu.VMEM((nz, b, n), BF),
            pltpu.VMEM((ny, nz, nx, b, n), BF),
            *taken,
            pltpu.VMEM((nz, b, cut), BF),
            pltpu.VMEM((nz, b, rest), BF),
            pltpu.VMEM((nz - 1, b, n), BF),
        ]

    whole = pl.BlockSpec(memory_space=pltpu.VMEM)
    outside = pl.BlockSpec(memory_space=pl.ANY)
    part_rows = up_rows + dblk
    outs = pl.pallas_call(
        layer_kernel,
        out_shape=[
            jax.ShapeDtypeStruct((rows_all, width), BF),
            jax.ShapeDtypeStruct((rows_all, width), F32),
            jax.ShapeDtypeStruct(w_qkv.shape, F32),
            jax.ShapeDtypeStruct(w_out.shape, F32),
            jax.ShapeDtypeStruct(w_up.shape, F32),
            jax.ShapeDtypeStruct(w_down.shape, F32),
            jax.ShapeDtypeStruct((8, width), F32),
            jax.ShapeDtypeStruct((8, LANES), F32),
        ],
        in_specs=[pl.BlockSpec(memory_space=pltpu.SMEM), outside, outside] + [whole] * 5,
        out_specs=[outside, outside] + [whole] * 6,
        scratch_shapes=[
            pltpu.VMEM((ny, nc, nz, nx, blk, 2 * width + LANES), BF),
            pltpu.VMEM((ny, nc, nz, nx, blk, 2 * width), BF),
            pltpu.VMEM((ny, nc, nz, nx, blk, ff), BF),
            pltpu.VMEM((ny, nc, nz, nx, dblk, width), BF),
            pltpu.VMEM((rows_all, width3), BF),
            pltpu.VMEM((rows_all, width), BF),
            pltpu.VMEM((blocks, width // LANES, keys_n, 2 * SPAN), BF),
            pltpu.VMEM((local_len // SPAN, width // LANES, keys_n, 2 * SPAN), BF),
            pltpu.VMEM((ny, nc, nz, nx, blk, width3), F32),
            pltpu.VMEM((ny, nc, nz, nx, blk, width), F32),
            pltpu.VMEM((rows_all, width), F32),
            pltpu.VMEM((rows_all, width), BF),
            pltpu.VMEM((width, rows_all), BF),
            pltpu.VMEM((width, rows_all), BF),
            pltpu.VMEM((rows_all, part_n), BF),
            pltpu.VMEM((rows_all, part_n), BF),
            pltpu.VMEM((ny, nx, part_rows, width), F32),
            pltpu.VMEM((ny, nx, part_rows, width), BF),
            pltpu.VMEM((nz, ny, nx, part_rows, width), BF),
            pltpu.VMEM((nx, part_rows, half), BF),
            pltpu.VMEM((ny, part_rows, half), BF),
            pltpu.VMEM((nz, nx, part_rows, half), BF),
            pltpu.VMEM((nz, ny, part_rows, half), BF),
            pltpu.VMEM((nz, part_rows, half), BF),
            pltpu.VMEM((nz, part_rows, half), BF),
            pltpu.VMEM((nz, nz, blk, width), BF),
            pltpu.VMEM((nz - 1, nz, blk, width), BF),
            pltpu.VMEM((nz, blk, width), F32),
            pltpu.VMEM((nz, dblk, width), F32),
            pltpu.VMEM((nz, dblk, width), BF),
            pltpu.VMEM((nz - 1, dblk, width), BF),
            *bufs(blk, width3),
            *bufs(blk, width),
            pltpu.VMEM((seq_n, blocks, 2 * width), BF),
            pltpu.VMEM((far_n, 2 * width), BF),
            pltpu.VMEM((far_n, 2 * width), F32),
            pltpu.VMEM((seq_n, blocks, 2 * width), BF),
            pltpu.VMEM((seq_n - 1, blocks, 2 * width), BF),
            pltpu.VMEM((blocks, width), F32),
            pltpu.VMEM((blocks, width), F32),
            pltpu.VMEM((8, width), F32),
            pltpu.VMEM((4, 8, width), F32),
            pltpu.VMEM((LANES, LANES), F32),
            pltpu.VMEM((seq_n, 8, width), F32),
            pltpu.VMEM((dp_n, 8, width), F32),
            pltpu.VMEM((seq_n, 8, LANES), F32),
            pltpu.VMEM((dp_n, 8, LANES), F32),
            pltpu.VMEM((rows_all, width), BF),
            pltpu.VMEM((rows_all, width), BF),
            pltpu.VMEM((rows_all, width), F32),
            pltpu.SemaphoreType.DMA((COPIES,)),
            pltpu.SemaphoreType.DMA((COPIES,)),
            pltpu.SemaphoreType.DMA((4,)),
        ],
        compiler_params=pltpu.CompilerParams(
            collective_id=0, has_side_effects=True, vmem_limit_bytes=64 * 1024 * 1024 - 65536
        ),
    )(
        lengths,
        tokens.reshape(rows_all, width),
        cotangent.reshape(rows_all, width),
        w_qkv, w_out, w_up, w_down, norm_params,
    )
    weights = (w_qkv, w_out, w_up, w_down, norm_params)
    new = pl.pallas_call(
        update_kernel,
        out_shape=[
            jax.ShapeDtypeStruct((rows_all, width), BF),
            jax.ShapeDtypeStruct((rows_all, width), F32),
            jax.ShapeDtypeStruct((1, 1), F32),
            *(jax.ShapeDtypeStruct(w.shape, F32) for w in weights for _ in range(3)),
        ],
        in_specs=[outside, outside] + [whole] * 21,
        out_specs=[outside, outside] + [whole] * 16,
        scratch_shapes=[
            pltpu.VMEM((rows_all, width), BF),
            pltpu.VMEM((rows_all, width), F32),
            pltpu.SemaphoreType.DMA((8,)),
            pltpu.SemaphoreType.DMA((8,)),
        ],
        compiler_params=pltpu.CompilerParams(vmem_limit_bytes=64 * 1024 * 1024 - 65536),
    )(
        outs[0], outs[1], outs[7], *outs[2:7], *weights,
        first_qkv, first_out, first_up, first_down, first_norm,
        second_qkv, second_out, second_up, second_down, second_norm,
    )
    return (
        new[0].reshape(tokens.shape), new[1].reshape(tokens.shape), new[2].reshape(()),
        *new[3:],
    )


def solution(mesh):
    placed = (
        P("dp", "seq", None),
        P("dp", "seq", None),
        P("dp"),
        P(("dp", "seq"), None),
        P(("dp", "seq"), None),
        P(("dp", "seq"), None),
        P(("dp", "seq"), None),
        P(None, ("dp", "seq")),
        P(("dp", "seq"), None),
        P(("dp", "seq"), None),
        P(("dp", "seq"), None),
        P(("dp", "seq"), None),
        P(None, ("dp", "seq")),
        P(("dp", "seq"), None),
        P(("dp", "seq"), None),
        P(("dp", "seq"), None),
        P(("dp", "seq"), None),
        P(None, ("dp", "seq")),
    )
    dp_n, seq_n = mesh.shape["dp"], mesh.shape["seq"]
    fits = dp_n == 4 and seq_n % 2 == 0 and WIDTH // (dp_n * seq_n) == 16
    return jax.shard_map(
        fused_device if fits else generic_device,
        mesh=mesh,
        in_specs=placed,
        out_specs=(
            P("dp", "seq", None),
            P("dp", "seq", None),
            P(),
            P(("dp", "seq"), None),
            P(("dp", "seq"), None),
            P(("dp", "seq"), None),
            P(("dp", "seq"), None),
            P(("dp", "seq"), None),
            P(("dp", "seq"), None),
            P(("dp", "seq"), None),
            P(("dp", "seq"), None),
            P(("dp", "seq"), None),
            P(("dp", "seq"), None),
            P(("dp", "seq"), None),
            P(("dp", "seq"), None),
            P(None, ("dp", "seq")),
            P(None, ("dp", "seq")),
            P(None, ("dp", "seq")),
        ),
        check_vma=False,
    )
```

```python
import functools
import math

import jax
import jax.numpy as jnp
from jax import lax
from jax.experimental import pallas as pl
from jax.experimental.pallas import tpu as pltpu
from jax.sharding import PartitionSpec as P

HEADS = 8
HEAD_DIM = 64
SPAN = 128
STEP = 10
WIDTH = 512


eps_norm = 1e-05
neg_fill = -1e30
beta_one = 0.9
beta_two = 0.999
adam_eps = 1e-08
decay_coef = 0.1
rate_matrix = 0.05
rate_norm = 0.5
clip_bound = 1.0


def normalize(values_in, gain_row, shift_row):
    center = values_in - jnp.mean(values_in, axis=-1, keepdims=True)
    spread = jnp.mean(center * center, axis=-1, keepdims=True)
    return center * lax.rsqrt(spread + eps_norm) * gain_row + shift_row


def adamw_update(weight, grad_in, first_old, second_old, factor, step_rate, weight_decay):
    clipped = grad_in * factor
    first_new = beta_one * first_old + (1.0 - beta_one) * clipped
    second_new = beta_two * second_old + (1.0 - beta_two) * clipped * clipped
    first_hat = first_new / (1.0 - beta_one**STEP)
    second_hat = second_new / (1.0 - beta_two**STEP)
    weight_new = weight - step_rate * (
        first_hat / (jnp.sqrt(second_hat) + adam_eps) + weight_decay * weight
    )
    return (weight_new, first_new, second_new)


def generic_device(
    tokens,
    cotangent,
    lengths,
    w_qkv,
    w_out,
    w_up,
    w_down,
    norm_params,
    first_qkv,
    first_out,
    first_up,
    first_down,
    first_norm,
    second_qkv,
    second_out,
    second_up,
    second_down,
    second_norm,
):
    item_count, local_len, model_width = tokens.shape
    row_count = item_count * local_len
    spans_here = local_len // SPAN
    spans_all = spans_here * lax.axis_size("seq")
    seq_rank = lax.axis_index("seq")
    score_scale = HEAD_DIM ** (-0.5)
    full_qkv, full_out, full_up, full_down, full_norm = (
        lax.all_gather(w_qkv.astype(jnp.bfloat16), ("dp", "seq"), axis=0, tiled=True),
        lax.all_gather(w_out.astype(jnp.bfloat16), ("dp", "seq"), axis=0, tiled=True),
        lax.all_gather(w_up.astype(jnp.bfloat16), ("dp", "seq"), axis=0, tiled=True),
        lax.all_gather(w_down.astype(jnp.bfloat16), ("dp", "seq"), axis=0, tiled=True),
        lax.all_gather(norm_params.astype(jnp.bfloat16), ("dp", "seq"), axis=1, tiled=True),
    )
    norm_rows = full_norm.astype(jnp.float32)
    tokens_f = tokens.reshape(row_count, model_width).astype(jnp.float32)
    normed, back_one = jax.vjp(normalize, tokens_f, norm_rows[0], norm_rows[1])
    normed_b = normed.astype(jnp.bfloat16)
    qkv_b = jnp.dot(normed_b, full_qkv, preferred_element_type=jnp.float32).astype(jnp.bfloat16)
    qkv_view = qkv_b.reshape(item_count, spans_here, SPAN, 3, HEADS, HEAD_DIM)
    query_part = qkv_view[:, :, :, 0]
    key_part = qkv_view[:, :, :, 1]
    value_part = qkv_view[:, :, :, 2]
    local_pos = seq_rank * local_len + jnp.arange(local_len, dtype=jnp.int32)
    live_mask = (local_pos[None, :] < lengths[:, None]).reshape(item_count, spans_here, SPAN)
    live_f = live_mask.astype(jnp.float32)
    counts_here = jnp.maximum(jnp.sum(live_f, axis=2), 1.0)
    pooled = jnp.einsum(
        "ist,istchd->ischd",
        live_mask.astype(jnp.bfloat16),
        qkv_view[:, :, :, 1:],
        preferred_element_type=jnp.float32,
    )
    pooled = (pooled / counts_here[:, :, None, None, None]).astype(jnp.bfloat16)
    pooled_all = lax.all_gather(pooled, "seq", axis=1, tiled=True)
    pooled_keys = pooled_all[:, :, 0]
    pooled_values = pooled_all[:, :, 1]
    all_pos = jnp.arange(spans_all * SPAN, dtype=jnp.int32).reshape(spans_all, SPAN)
    counts_all = jnp.sum((all_pos[None] < lengths[:, None, None]).astype(jnp.float32), axis=2)
    span_ids = seq_rank * spans_here + jnp.arange(spans_here, dtype=jnp.int32)
    far_valid = (counts_all[:, None, :] > 0.0) & (
        span_ids[None, :, None] != jnp.arange(spans_all, dtype=jnp.int32)[None, None, :]
    )
    near_mask = live_mask[:, :, None, None, :]
    far_mask = far_valid[:, :, None, None, :]

    def scores_of():
        near_raw = (
            jnp.einsum(
                "isqhd,iskhd->ishqk", query_part, key_part, preferred_element_type=jnp.float32
            )
            * score_scale
        )
        far_raw = (
            jnp.einsum(
                "isqhd,irhd->ishqr", query_part, pooled_keys, preferred_element_type=jnp.float32
            )
            * score_scale
        )
        return (jnp.where(near_mask, near_raw, neg_fill), jnp.where(far_mask, far_raw, neg_fill))

    near_s, far_s = scores_of()
    score_top = jnp.maximum(
        jnp.max(near_s, axis=-1, keepdims=True), jnp.max(far_s, axis=-1, keepdims=True)
    )
    exp_total = jnp.sum(jnp.exp(near_s - score_top), axis=-1, keepdims=True) + jnp.sum(
        jnp.exp(far_s - score_top), axis=-1, keepdims=True
    )
    log_total = score_top + jnp.log(exp_total)
    near_pb = jnp.exp(near_s - log_total).astype(jnp.bfloat16)
    far_pb = jnp.exp(far_s - log_total).astype(jnp.bfloat16)
    mixed_rows = jnp.einsum(
        "ishqk,iskhd->isqhd", near_pb, value_part, preferred_element_type=jnp.float32
    )
    mixed_rows = mixed_rows + jnp.einsum(
        "ishqr,irhd->isqhd", far_pb, pooled_values, preferred_element_type=jnp.float32
    )
    mixed_b = mixed_rows.reshape(row_count, model_width).astype(jnp.bfloat16)
    residual = tokens_f + jnp.dot(mixed_b, full_out, preferred_element_type=jnp.float32)
    normed_two, back_two = jax.vjp(normalize, residual, norm_rows[2], norm_rows[3])
    normed_two_b = normed_two.astype(jnp.bfloat16)
    up_pre = jnp.dot(normed_two_b, full_up, preferred_element_type=jnp.float32)
    gated, gelu_back = jax.vjp(jax.nn.gelu, up_pre)
    gated_b = gated.astype(jnp.bfloat16)
    layer_out = residual + jnp.dot(gated_b, full_down, preferred_element_type=jnp.float32)
    activations = layer_out.astype(jnp.bfloat16).reshape(item_count, local_len, model_width)
    grad_out_b = cotangent.reshape(row_count, model_width)
    grad_down = jnp.dot(gated_b.T, grad_out_b, preferred_element_type=jnp.float32)
    grad_gated = jnp.dot(grad_out_b, full_down.T, preferred_element_type=jnp.float32)
    grad_up_pre = gelu_back(grad_gated)[0].astype(jnp.bfloat16)
    grad_up = jnp.dot(normed_two_b.T, grad_up_pre, preferred_element_type=jnp.float32)
    grad_normed_two = jnp.dot(grad_up_pre, full_up.T, preferred_element_type=jnp.float32)
    grad_resid_ln, grad_gain_two, grad_shift_two = back_two(grad_normed_two)
    grad_resid = grad_out_b.astype(jnp.float32) + grad_resid_ln
    grad_attn_b = grad_resid.astype(jnp.bfloat16)
    grad_out_proj = jnp.dot(mixed_b.T, grad_attn_b, preferred_element_type=jnp.float32)
    grad_mixed = jnp.dot(grad_attn_b, full_out.T, preferred_element_type=jnp.float32).astype(
        jnp.bfloat16
    )
    grad_mixed = grad_mixed.reshape(item_count, spans_here, SPAN, HEADS, HEAD_DIM)
    near_s, far_s = scores_of()
    near_pf = jnp.exp(near_s - log_total)
    far_pf = jnp.exp(far_s - log_total)
    near_pb = near_pf.astype(jnp.bfloat16)
    far_pb = far_pf.astype(jnp.bfloat16)
    grad_near = jnp.einsum(
        "isqhd,iskhd->ishqk", grad_mixed, value_part, preferred_element_type=jnp.float32
    )
    grad_far = jnp.einsum(
        "isqhd,irhd->ishqr", grad_mixed, pooled_values, preferred_element_type=jnp.float32
    )
    row_delta = jnp.sum(near_pf * grad_near, axis=-1, keepdims=True) + jnp.sum(
        far_pf * grad_far, axis=-1, keepdims=True
    )
    dscore_near = (near_pf * (grad_near - row_delta)).astype(jnp.bfloat16)
    dscore_far = (far_pf * (grad_far - row_delta)).astype(jnp.bfloat16)
    grad_query = jnp.einsum(
        "ishqk,iskhd->isqhd", dscore_near, key_part, preferred_element_type=jnp.float32
    )
    grad_query = (
        grad_query
        + jnp.einsum(
            "ishqr,irhd->isqhd", dscore_far, pooled_keys, preferred_element_type=jnp.float32
        )
    ) * score_scale
    grad_keys = (
        jnp.einsum(
            "ishqk,isqhd->iskhd", dscore_near, query_part, preferred_element_type=jnp.float32
        )
        * score_scale
    )
    grad_values = jnp.einsum(
        "ishqk,isqhd->iskhd", near_pb, grad_mixed, preferred_element_type=jnp.float32
    )
    grad_pool_keys = (
        jnp.einsum("ishqr,isqhd->irhd", dscore_far, query_part, preferred_element_type=jnp.float32)
        * score_scale
    )
    grad_pool_values = jnp.einsum(
        "ishqr,isqhd->irhd", far_pb, grad_mixed, preferred_element_type=jnp.float32
    )
    pool_grads = jnp.stack([grad_pool_keys, grad_pool_values], axis=2)
    pool_mine = lax.psum_scatter(
        pool_grads.astype(jnp.bfloat16), "seq", scatter_dimension=1, tiled=True
    ).astype(jnp.float32)
    spread_back = pool_mine / counts_here[:, :, None, None, None]
    grad_kv = (
        jnp.stack([grad_keys, grad_values], axis=3)
        + live_f[:, :, :, None, None, None] * spread_back[:, :, None]
    )
    grad_qkv_rows = jnp.concatenate([grad_query[:, :, :, None], grad_kv], axis=3)
    grad_qkv_b = grad_qkv_rows.reshape(row_count, 3 * model_width).astype(jnp.bfloat16)
    grad_qkv = jnp.dot(normed_b.T, grad_qkv_b, preferred_element_type=jnp.float32)
    grad_normed = jnp.dot(grad_qkv_b, full_qkv.T, preferred_element_type=jnp.float32)
    grad_in_ln, grad_gain_one, grad_shift_one = back_one(grad_normed)
    input_grad = (grad_resid + grad_in_ln).reshape(item_count, local_len, model_width)
    grad_norm_rows = jnp.stack([grad_gain_one, grad_shift_one, grad_gain_two, grad_shift_two])
    red_qkv, red_out, red_up, red_down, red_norm = (
        lax.psum_scatter(grad_qkv, ("dp", "seq"), scatter_dimension=0, tiled=True),
        lax.psum_scatter(grad_out_proj, ("dp", "seq"), scatter_dimension=0, tiled=True),
        lax.psum_scatter(grad_up, ("dp", "seq"), scatter_dimension=0, tiled=True),
        lax.psum_scatter(grad_down, ("dp", "seq"), scatter_dimension=0, tiled=True),
        lax.psum_scatter(grad_norm_rows, ("dp", "seq"), scatter_dimension=1, tiled=True),
    )
    squares = jnp.sum(red_qkv * red_qkv) + jnp.sum(red_out * red_out) + jnp.sum(red_up * red_up)
    squares = squares + jnp.sum(red_down * red_down) + jnp.sum(red_norm * red_norm)
    total_sq = lax.psum(squares, ("dp", "seq"))
    grad_norm = jnp.sqrt(total_sq)
    factor = clip_bound / jnp.maximum(grad_norm, clip_bound)
    new_qkv, new_first_qkv, new_second_qkv = adamw_update(
        w_qkv, red_qkv, first_qkv, second_qkv, factor, rate_matrix, decay_coef
    )
    new_out, new_first_out, new_second_out = adamw_update(
        w_out, red_out, first_out, second_out, factor, rate_matrix, decay_coef
    )
    new_up, new_first_up, new_second_up = adamw_update(
        w_up, red_up, first_up, second_up, factor, rate_matrix, decay_coef
    )
    new_down, new_first_down, new_second_down = adamw_update(
        w_down, red_down, first_down, second_down, factor, rate_matrix, decay_coef
    )
    new_norm, new_first_norm, new_second_norm = adamw_update(
        norm_params, red_norm, first_norm, second_norm, factor, rate_norm, 0.0
    )
    return (
        activations,
        input_grad,
        grad_norm,
        new_qkv,
        new_first_qkv,
        new_second_qkv,
        new_out,
        new_first_out,
        new_second_out,
        new_up,
        new_first_up,
        new_second_up,
        new_down,
        new_first_down,
        new_second_down,
        new_norm,
        new_first_norm,
        new_second_norm,
    )


BF = jnp.bfloat16
F32 = jnp.float32
MESH = pl.DeviceIdType.MESH
LANES = 128
TILE = 512
NN = (((1,), (0,)), ((), ()))
NT = (((1,), (1,)), ((), ()))
TN = (((0,), (0,)), ((), ()))
GATHER, SPREAD, PARTS, DOWN, OUTER, INNER, POOL, POOLBACK = 0, 22, 62, 94, 97, 105, 121, 128
NORM_SEQ, NORM_DP, SQUARE_SEQ, SQUARE_DP, COPIES = 135, 142, 145, 152, 155


def mm(left, right, dims=NN):
    return lax.dot_general(left, right, dims, preferred_element_type=F32)


def centered(values_in):
    center = values_in - jnp.mean(values_in, axis=-1, keepdims=True)
    scale = lax.rsqrt(jnp.mean(center * center, axis=-1, keepdims=True) + eps_norm)
    return center * scale, scale


def norm_back(grad_hat, hat, scale):
    mean_grad = jnp.mean(grad_hat, axis=-1, keepdims=True)
    mean_both = jnp.mean(grad_hat * hat, axis=-1, keepdims=True)
    return scale * (grad_hat - mean_grad - hat * mean_both)


def fold_rows(values_in):
    rows, width = values_in.shape
    return jnp.sum(values_in.reshape(rows // 8, 8, width), axis=0)


def layer_kernel(
    len_ref, x_any, dy_any, wq_ref, wo_ref, wu_ref, wd_ref, nrm_ref,
    act_any, dx_any, fin_q, fin_o, fin_u, fin_d, norm_sum, total_ref,
    bkv, bqo, bu, bd, qkv, mix, prob, gq, go, yacc, h2_s, ht_s, dyt_s, act_s, dup_s,
    own_p, kept_p, s1p, r1p, s2ap, s2bp, r2ap, r2bp, r3ap, r3bp, s4p, r4p, fin_p, keep_d, s5d, r5d,
    s2aq, s2bq, s3q, r1q, r2aq, r2bq, r3aq, r3bq, r4q,
    s2ak, s2bk, s3k, r1k, r2ak, r2bk, r3ak, r3bk, r4k,
    s2ao, s2bo, s3o, r1o, r2ao, r2bo, r3ao, r3bo, r4o,
    pool_all, pool_far, pool_grad, pool_send, pool_recv, live_sum, spread_w,
    nrow, nacc, ntall, norm_seq, norm_dp, psq, psd, x_ref, dy_ref, dx_ref,
    send_sem, recv_sem, local_sem,
):
    ny, nc, nz, nx, blk, _ = bu.shape
    dblk = bd.shape[4]
    rows_all, width = x_ref.shape
    width3 = 3 * width
    ff = wu_ref.shape[1]
    seq_n = nz * nx
    dp_n = ny * nc
    local_len = rows_all // len_ref.shape[0]
    spans_here = local_len // SPAN
    blocks = rows_all // SPAN
    spans_all = spans_here * seq_n
    tiles = rows_all // TILE
    per_tile = TILE // SPAN
    pairs = width // LANES
    part_n = ff // nz
    ffn_rows = 2 * TILE
    dp_i = lax.axis_index("dp")
    sq_i = lax.axis_index("seq")
    y, c = dp_i // nc, dp_i % nc
    z, x = sq_i // nx, sq_i % nx

    def dev(yy, cc, zz, xx):
        return (yy * nc + cc, zz * nx + xx)

    twin = dev(y, 1 - c, z, x)
    over_x = dev(y, c, z, 1 - x)
    over_y = dev(1 - y, c, z, x)

    def seq_peer(step):
        return lax.rem(sq_i + step, seq_n)

    def dp_peer(step):
        return lax.rem(dp_i + step, dp_n)

    def z_peer(step):
        return lax.rem(z + step, nz)

    def hop(src, dst, index, target):
        return pltpu.make_async_remote_copy(
            src_ref=src, dst_ref=dst, send_sem=send_sem.at[index],
            recv_sem=recv_sem.at[index], device_id=target, device_id_type=MESH,
        )

    def start(hops):
        for one in hops:
            one.start()

    def arrived(hops):
        for one in hops:
            one.wait_recv()

    def sent(hops):
        for one in hops:
            one.wait_send()

    def each(count, body):
        def step(index, carry):
            body(index)
            return carry

        lax.fori_loop(0, count, step, 0)

    def flat(count, body):
        for index in range(count):
            body(index)

    def tile_rows(tile):
        if isinstance(tile, int):
            return pl.ds(tile * TILE, TILE)
        return pl.ds(pl.multiple_of(tile * TILE, TILE), TILE)

    load_x = pltpu.make_async_copy(x_any, x_ref, local_sem.at[0])
    load_dy = pltpu.make_async_copy(dy_any, dy_ref, local_sem.at[1])
    keep_act = pltpu.make_async_copy(dy_ref, act_any, local_sem.at[2])
    keep_dx = pltpu.make_async_copy(dx_ref, dx_any, local_sem.at[3])
    load_dy.start()
    load_x.start()

    barrier = pltpu.get_barrier_semaphore()
    for step in range(1, seq_n):
        pl.semaphore_signal(
            barrier, inc=1, device_id=(dp_i, seq_peer(step)), device_id_type=MESH
        )
    for step in range(1, dp_n):
        pl.semaphore_signal(
            barrier, inc=1, device_id=(dp_peer(step), sq_i), device_id_type=MESH
        )

    bkv[y, c, z, x, :, 0 : 2 * width] = wq_ref[:, width:].astype(BF)
    bqo[y, c, z, x, :, 0:width] = wq_ref[:, 0:width].astype(BF)
    bqo[y, c, z, x, :, width:] = wo_ref[...].astype(BF)
    count = nrm_ref.shape[0]
    ntall[...] = jnp.zeros_like(ntall)
    ntall[0:count, 0:blk] = nrm_ref[...]
    bkv[y, c, z, x, :, 2 * width :] = ntall[...].T[0:blk].astype(BF)
    for part in range(nz):
        for group in range(dp_n):
            lo, at = part * part_n + group * LANES, (group * nz + part) * LANES
            bu[y, c, z, x, :, lo : lo + LANES] = wu_ref[:, at : at + LANES].astype(BF)
    bd[y, c, z, x] = wd_ref[...].astype(BF)
    pl.semaphore_wait(barrier, seq_n + dp_n - 2)

    def gather_hops(full, base):
        cut = (full.shape[5] // 2) // LANES * LANES
        one, two = pl.ds(0, cut), pl.ds(cut, full.shape[5] - cut)

        def same(part, index, target):
            return hop(part, part, base + index, target)

        first = [
            same(full.at[y, c, z, x], step - 1, dev(y, c, z_peer(step), x))
            for step in range(1, nz)
        ]
        second = [
            same(full.at[y, c, :, x, :, one], 3, over_x),
            same(full.at[y, c, :, x, :, two], 4, over_y),
        ]
        third = [
            same(full.at[y, c, :, :, :, one], 5, over_y),
            same(full.at[:, c, :, x, :, two], 6, over_x),
        ]
        last = [same(full.at[:, c], 7, twin)]
        return first, second, third, last

    def direct(full, base):
        mine = full.at[y, c, z, x]
        return [
            hop(mine, mine, base + step - 1, dev(y, c, z_peer(step), x)) for step in range(1, nz)
        ]

    def spread_hops(part):
        base = SPREAD + part * 10
        cols = pl.ds(pl.multiple_of(part * part_n, part_n), part_n)
        one = pl.ds(pl.multiple_of(part * part_n, LANES), part_n // 2)
        two = pl.ds(pl.multiple_of(part * part_n + part_n // 2, LANES), part_n // 2)
        d_one, d_two = pl.ds(0, width // 2), pl.ds(width // 2, width // 2)

        def same(place, index, target):
            return hop(place, place, base + index, target)

        return (
            [
                same(bu.at[y, c, :, x, :, one], 0, over_x),
                same(bu.at[y, c, :, x, :, two], 1, over_y),
                same(bd.at[y, c, part, x, :, d_one], 2, over_x),
                same(bd.at[y, c, part, x, :, d_two], 3, over_y),
            ],
            [
                same(bu.at[y, c, :, :, :, one], 4, over_y),
                same(bu.at[:, c, :, x, :, two], 5, over_x),
                same(bd.at[y, c, part, :, :, d_one], 6, over_y),
                same(bd.at[:, c, part, x, :, d_two], 7, over_x),
            ],
            [
                same(bu.at[:, c, :, :, :, cols], 8, twin),
                same(bd.at[:, c, part], 9, twin),
            ],
        )

    def pass_on(part, stage):
        hops = spread_hops(part)
        arrived(hops[stage])
        start(hops[stage + 1])

    hops_kv = gather_hops(bkv, GATHER)
    hops_qo = gather_hops(bqo, GATHER + 8)
    direct_u = direct(bu, GATHER + 16)
    direct_d = direct(bd, GATHER + 19)
    start(hops_kv[0])
    start(hops_qo[0])
    start(direct_u)
    start(direct_d)
    nacc[...] = jnp.zeros_like(nacc)
    arrived(hops_kv[0])
    start(hops_kv[1])
    load_dy.wait()

    def turn_dy(tile):
        rows = tile_rows(tile)
        dyt_s[:, rows] = dy_ref[rows, :].astype(F32).T.astype(BF)

    each(tiles // 2, turn_dy)
    arrived(hops_kv[1])
    start(hops_kv[2])
    arrived(hops_qo[0])
    start(hops_qo[1])
    load_x.wait()
    each(tiles // 2, lambda tile: turn_dy(tile + tiles // 2))
    arrived(hops_kv[2])
    start(hops_kv[3])
    arrived(hops_qo[1])
    start(hops_qo[2])
    arrived(direct_u)
    arrived(direct_d)
    for part in range(nz):
        start(spread_hops(part)[0])
    arrived(hops_kv[3])

    norm_cols = bkv[:, :, :, :, :, 2 * width :].reshape(width, LANES).astype(F32)
    nrow[...] = norm_cols.T[0:8]

    def w_qkv(part):
        if part == 0:
            return bqo[:, :, :, :, :, 0:width].reshape(width, width)
        return bkv[:, :, :, :, :, (part - 1) * width : part * width].reshape(width, width)

    def first_norm(rows):
        hat, scale = centered(x_ref[rows, :].astype(F32))
        return hat, scale, (hat * nrow[0:1, :] + nrow[1:2, :]).astype(BF)

    def live_pick(tile):
        block_at = lax.broadcasted_iota(jnp.int32, (blocks, TILE), 0)
        row_at = lax.broadcasted_iota(jnp.int32, (blocks, TILE), 1) + tile * TILE
        pos = sq_i * local_len + lax.rem(row_at, local_len)
        item = row_at // local_len
        length = jnp.zeros((blocks, TILE), jnp.int32)
        for i in range(TILE // local_len):
            at = tile * (TILE // local_len) + i
            length = jnp.where(item == at, len_ref[at], length)
        return jnp.where((row_at // SPAN == block_at) & (pos < length), 1.0, 0.0).astype(BF)

    def kv_tile(tile, pooled):
        rows = tile_rows(tile)
        _, _, h1 = first_norm(rows)
        h2_s[rows, :] = h1
        for part in (1, 2):
            qkv[rows, pl.ds(part * width, width)] = mm(h1, w_qkv(part)).astype(BF)

        if tile == 3:
            arrived(hops_qo[2])
            start(hops_qo[3])
        return pooled + mm(live_pick(tile), qkv[rows, width:])

    pooled = jnp.zeros((blocks, 2 * width), F32)
    for index in range(tiles):
        pooled = kv_tile(index, pooled)
    block_col = lax.broadcasted_iota(jnp.int32, (blocks, 1), 0)
    length_col = jnp.zeros((blocks, 1), jnp.int32)
    for i in range(blocks // spans_here):
        length_col = jnp.where(block_col // spans_here == i, len_ref[i], length_col)
    first_pos = sq_i * local_len + lax.rem(block_col, spans_here) * SPAN
    count_col = jnp.clip(length_col - first_pos, 1, SPAN).astype(F32)
    pool_all[sq_i] = (pooled / count_col).astype(BF)
    pool_hops = [
        hop(pool_all.at[sq_i], pool_all.at[sq_i], POOL + step - 1, (dp_i, seq_peer(step)))
        for step in range(1, seq_n)
    ]
    start(pool_hops)
    pass_on(0, 0)
    arrived(hops_qo[3])

    def q_tile(tile):
        rows = tile_rows(tile)
        qkv[rows, 0:width] = mm(h2_s[rows, :], w_qkv(0)).astype(BF)

    flat(tiles, q_tile)
    arrived(pool_hops)

    far_n = seq_n * blocks
    to_row = lax.broadcasted_iota(jnp.int32, (far_n, far_n), 0)
    to_col = lax.broadcasted_iota(jnp.int32, (far_n, far_n), 1)
    item_row, span_row = to_row // spans_all, to_row % spans_all
    wanted = (span_row // spans_here) * blocks + item_row * spans_here + span_row % spans_here
    order = jnp.where(wanted == to_col, 1.0, 0.0).astype(BF)
    pool_far[...] = mm(order, pool_all[...].reshape(far_n, 2 * width)).astype(BF)

    keys_n = SPAN + spans_all
    lane = lax.broadcasted_iota(jnp.int32, (1, LANES), 1)
    score_scale = HEAD_DIM ** (-0.5)
    half_a = jnp.where(lane < HEAD_DIM, 1.0, 0.0)
    half_b = jnp.where(lane >= HEAD_DIM, 1.0, 0.0)
    query_a, query_b = (half_a * score_scale).astype(BF), (half_b * score_scale).astype(BF)
    grad_a, grad_b = half_a.astype(BF), half_b.astype(BF)

    def both(near_rows, far_rows, cols):
        far_cols = pl.ds(cols.start - width, cols.size)
        return jnp.concatenate([qkv[near_rows, cols], pool_far[far_rows, far_cols]], axis=0)

    def cols_of(third, pair):
        return pl.ds(third * width + pair * LANES, LANES)

    def by_head(rows_in, first, second):
        return jnp.concatenate([rows_in * first, rows_in * second], axis=0)

    units = [(sub, pair) for sub in range(spans_here) for pair in range(pairs)]
    items = blocks // spans_here

    def rows_of(item, sub):
        return pl.ds(pl.multiple_of(item * local_len + sub * SPAN, SPAN), SPAN)

    def far_of(item):
        return pl.ds(pl.multiple_of(item * spans_all, spans_all), spans_all)

    def attend(item):
        for at, moves in (
            (0, ((1, 0),)), (1, ((0, 1),)), (2, ((2, 0),)), (3, ((1, 1),)),
            (4, ((3, 0),)), (6, ((2, 1),)), (7, ((3, 1),)),
        ):

            @pl.when(item == at)
            def _(moves=moves):
                for part, stage in moves:
                    pass_on(part, stage)

        far_rows = far_of(item)
        length = len_ref[item]
        key_at = lax.broadcasted_iota(jnp.int32, (keys_n, 2 * SPAN), 0)
        span_at = key_at - SPAN

        def seen(sub):
            mine = sq_i * spans_here + sub
            near_ok = (key_at < SPAN) & (mine * SPAN + key_at < length)
            return near_ok | ((key_at >= SPAN) & (span_at * SPAN < length) & (span_at != mine))

        scores = []
        for sub, pair in units:
            rows = rows_of(item, sub)
            kk = both(rows, far_rows, cols_of(1, pair))
            scores.append(mm(kk, by_head(qkv[rows, cols_of(0, pair)], query_a, query_b), NT))
        for (sub, pair), score in zip(units, scores):
            score = jnp.where(seen(sub), score, neg_fill)
            raised = jnp.exp(score - jnp.max(score, axis=0, keepdims=True))
            share = raised * (1.0 / jnp.sum(raised, axis=0, keepdims=True))
            prob[item * spans_here + sub, pair] = share.astype(BF)
        for sub in range(spans_here):
            rows = rows_of(item, sub)
            mixed = []
            for pair in range(pairs):
                vv = both(rows, far_rows, cols_of(2, pair))
                stacked = mm(vv, prob[item * spans_here + sub, pair], TN)
                mixed += [stacked[0:HEAD_DIM, 0:SPAN], stacked[HEAD_DIM:, SPAN:]]
            mix[rows, :] = jnp.concatenate(mixed, axis=0).T.astype(BF)

    each(items, attend)
    for group in (*hops_kv, *hops_qo, direct_u, direct_d, pool_hops):
        sent(group)

    w_out = bqo[:, :, :, :, :, width:].reshape(width, width)
    gelu_in = math.sqrt(2.0 / math.pi)
    gelu_cube = 0.044715

    def second_norm(rows):
        x1 = x_ref[rows, :].astype(F32) + mm(mix[rows, :], w_out)
        hat, scale = centered(x1)
        return x1, hat, scale

    def ffn_open(tile):
        rows = tile_rows(tile)
        x1, hat, _ = second_norm(rows)
        yacc[rows, :] = x1
        dx_ref[rows, :] = jnp.zeros((TILE, width), F32)
        h2 = hat * nrow[2:3, :] + nrow[3:4, :]
        h2_s[rows, :] = h2.astype(BF)
        ht_s[:, rows] = h2.T.astype(BF)

    flat(tiles, ffn_open)

    half_cols = width // 2
    one_p, two_p = pl.ds(0, half_cols), pl.ds(half_cols, half_cols)
    up_rows = nz * blk

    def part_hops(part):
        base = PARTS + part * 8
        slot = part % 2
        return (
            [hop(s1p, r1p.at[slot], base, twin)],
            [
                hop(s1p.at[1 - y, :, :, one_p], r2ap.at[slot], base + 1, over_y),
                hop(s1p.at[:, 1 - x, :, two_p], r2bp.at[slot], base + 2, over_x),
            ],
            [
                hop(s2ap.at[1 - x], r3ap.at[slot], base + 3, over_x),
                hop(s2bp.at[1 - y], r3bp.at[slot], base + 4, over_y),
            ],
            [
                hop(
                    s4p.at[part, z_peer(step)], r4p.at[step - 1, part], base + 4 + step,
                    dev(y, c, z_peer(step), x),
                )
                for step in range(1, nz)
            ],
        )

    def down_cols(group):
        cols = pl.ds(pl.multiple_of(group * LANES, LANES), LANES)
        return gq[:, :, :, :, :, cols].reshape(width, LANES)

    def part_first(part):
        for yy in range(ny):
            for xx in range(nx):
                for zz in range(nz):
                    at = pl.ds(zz * blk, blk)
                    own_p[yy, xx, at] = go[yy, c, zz, xx]
                    s1p[yy, xx, at] = go[yy, 1 - c, zz, xx].astype(BF)
            mine = down_cols(yy * nc + c).T
            other = down_cols(yy * nc + 1 - c).T
            for xx in range(nx):
                own_p[yy, xx, up_rows:] = mine[xx * dblk : (xx + 1) * dblk]
                s1p[yy, xx, up_rows:] = other[xx * dblk : (xx + 1) * dblk].astype(BF)
        start(part_hops(part)[0])

    def part_second(part):
        hops = part_hops(part)
        arrived(hops[0])
        sent(hops[0])

        def add(index):
            yy, xx = index // nx, index % nx
            total = own_p[yy, xx] + r1p[part % 2, yy, xx].astype(F32)
            own_p[yy, xx] = total
            s1p[yy, xx] = total.astype(BF)

        each(ny * nx, add)
        start(hops[1])

    def part_third(part):
        hops = part_hops(part)
        arrived(hops[1])
        sent(hops[1])
        for xx in range(nx):
            total = own_p[y, xx, :, one_p] + r2ap[part % 2, xx].astype(F32)
            own_p[y, xx, :, one_p] = total
            s2ap[xx] = total.astype(BF)
        for yy in range(ny):
            total = own_p[yy, x, :, two_p] + r2bp[part % 2, yy].astype(F32)
            own_p[yy, x, :, two_p] = total
            s2bp[yy] = total.astype(BF)
        kept_p[...] = own_p[y, x]
        start(hops[2])

    def part_fourth(part):
        hops = part_hops(part)
        arrived(hops[2])
        sent(hops[2])
        kept_p[:, one_p] += r3ap[part % 2].astype(F32)
        kept_p[:, two_p] += r3bp[part % 2].astype(F32)
        for zz in range(nz):
            s4p[part, zz] = kept_p[zz * blk : (zz + 1) * blk].astype(BF)
        fin_p[part] = kept_p[pl.ds(pl.multiple_of(z * blk, blk), blk)]
        down = kept_p[up_rows:]
        keep_d[part] = down
        s5d[part] = down.astype(BF)
        start(hops[3])

    down_hops = [
        hop(
            s5d.at[z_peer(step)], r5d.at[step - 1], DOWN + step - 1, dev(y, c, z_peer(step), x)
        )
        for step in range(1, nz)
    ]

    def ffn_part(part, carry):
        cols = pl.ds(pl.multiple_of(part * part_n, part_n), part_n)
        arrived(spread_hops(part)[2])
        w_up = bu[:, :, :, :, :, cols].reshape(width, part_n)
        w_down = bd[:, :, part].reshape(part_n, width)

        def ffn_tile(tile):
            @pl.when((part > 0) & (tile == 1))
            def _():
                part_second(part - 1)

            rows = pl.ds(pl.multiple_of(tile * ffn_rows, ffn_rows), ffn_rows)
            for piece in range(ffn_rows // TILE):
                some = tile_rows(tile * (ffn_rows // TILE) + piece)
                up = mm(h2_s[some, :], w_up)
                square = up * up
                bent = jnp.tanh(up * (gelu_in + (gelu_in * gelu_cube) * square))
                half = 0.5 + 0.5 * bent
                act_s[some, :] = (up * half).astype(BF)
                rate = half + (up * (1.0 - bent * bent)) * (
                    0.5 * gelu_in + (1.5 * gelu_in * gelu_cube) * square
                )
                dup_s[some, :] = (mm(dy_ref[some, :], w_down, NT) * rate).astype(BF)
            yacc[rows, :] += mm(act_s[rows, :], w_down)
            dx_ref[rows, :] += mm(dup_s[rows, :], w_up, NT)

        each(rows_all // ffn_rows, ffn_tile)

        @pl.when(part > 1)
        def _():
            part_fourth(part - 2)

        gq[:, :, :, :, :, 0:part_n] = mm(dyt_s[...], act_s[...]).reshape(go.shape)
        go[...] = mm(ht_s[...], dup_s[...]).reshape(go.shape)

        @pl.when(part > 0)
        def _():
            part_third(part - 1)

        part_first(part)
        return carry

    lax.fori_loop(0, nz, ffn_part, 0)

    def ffn_close(tile):
        if tile == 2:
            part_second(nz - 1)
        if tile == 3:
            part_fourth(nz - 2)
        rows = tile_rows(tile)
        _, hat, scale = second_norm(rows)
        dh2 = dx_ref[rows, :]
        nacc[2] += fold_rows(dh2 * hat)
        nacc[3] += fold_rows(dh2)
        dx1 = dy_ref[rows, :].astype(F32) + norm_back(dh2 * nrow[2:3, :], hat, scale)
        dy_ref[rows, :] = yacc[rows, :].astype(BF)
        dx_ref[rows, :] = dx1
        dz = dx1.astype(BF)
        act_s[rows, :] = dz
        ht_s[:, rows] = mix[rows, :].astype(F32).T.astype(BF)
        mix[rows, :] = mm(dz, w_out, NT).astype(BF)

    flat(tiles, ffn_close)
    keep_act.start()
    for part in range(nz):
        for group in spread_hops(part):
            sent(group)
    go[...] = mm(ht_s[...], act_s[...]).reshape(go.shape)

    def reduce_steps(full, cols, s1, r1, s2a, s2b, r2a, r2b, r3a, r3b, s3, r4, fin, base):
        full = full.at[:, :, :, :, :, cols]
        own = full.at[:, c]
        n = s1.shape[4]
        cut = (n // 2) // LANES * LANES
        one, two = pl.ds(0, cut), pl.ds(cut, n - cut)
        hop1 = [hop(s1, r1, base, twin)]
        hop2 = [
            hop(s1.at[1 - y, :, :, :, one], r2a, base + 1, over_y),
            hop(s1.at[:, :, 1 - x, :, two], r2b, base + 2, over_x),
        ]
        hop3 = [
            hop(s2a.at[:, 1 - x], r3a, base + 3, over_x),
            hop(s2b.at[1 - y], r3b, base + 4, over_y),
        ]
        hop4 = [
            hop(
                s3.at[z_peer(step)], r4.at[step - 1], base + 4 + step,
                dev(y, c, z_peer(step), x),
            )
            for step in range(1, nz)
        ]

        def places(index):
            return index // (nz * nx), (index // nx) % nz, index % nx

        def stage1():
            def load(index):
                yy, zz, xx = places(index)
                s1[yy, zz, xx] = full[yy, 1 - c, zz, xx].astype(BF)

            each(ny * nz * nx, load)
            start(hop1)

        def stage2():
            arrived(hop1)
            sent(hop1)

            def add(index):
                yy, zz, xx = places(index)
                total = own[yy, zz, xx] + r1[yy, zz, xx].astype(F32)
                own[yy, zz, xx] = total
                s1[yy, zz, xx] = total.astype(BF)

            each(ny * nz * nx, add)
            start(hop2)

        def stage3():
            arrived(hop2)
            for zz in range(nz):
                for xx in range(nx):
                    total = own[y, zz, xx, :, one] + r2a[zz, xx].astype(F32)
                    own[y, zz, xx, :, one] = total
                    s2a[zz, xx] = total.astype(BF)
            start(hop3[0:1])
            for yy in range(ny):
                for zz in range(nz):
                    total = own[yy, zz, x, :, two] + r2b[yy, zz].astype(F32)
                    own[yy, zz, x, :, two] = total
                    s2b[yy, zz] = total.astype(BF)
            start(hop3[1:2])

        def stage4():
            arrived(hop3)
            for zz in range(nz):
                total = own[y, zz, x, :, one] + r3a[zz].astype(F32)
                own[y, zz, x, :, one] = total
                s3[zz, :, one] = total.astype(BF)
                total = own[y, zz, x, :, two] + r3b[zz].astype(F32)
                own[y, zz, x, :, two] = total
                s3[zz, :, two] = total.astype(BF)
            start(hop4)

        def stage5():
            arrived(hop4)
            total = own[y, z, x]
            for step in range(nz - 1):
                total = total + r4[step].astype(F32)
            fin[:, cols] = total
            sent(hop2)
            sent(hop3)
            sent(hop4)

        return stage1, stage2, stage3, stage4, stage5

    cols_q, cols_kv = pl.ds(0, width), pl.ds(width, 2 * width)
    red_o = reduce_steps(
        go, cols_q, bu.at[:, 0, :, :, :, cols_q], r1o, s2ao, s2bo, r2ao, r2bo, r3ao, r3bo, s3o,
        r4o, fin_o, OUTER,
    )
    red_q = reduce_steps(
        gq, cols_q, bu.at[:, 1, :, :, :, cols_q], r1q, s2aq, s2bq, r2aq, r2bq, r3aq, r3bq,
        s3q, r4q, fin_q, INNER,
    )
    red_kv = reduce_steps(
        gq, cols_kv, bu.at[:, 1, :, :, :, cols_kv], r1k, s2ak, s2bk, r2ak, r2bk, r3ak, r3bk,
        s3k, r4k, fin_q, INNER + 8,
    )
    red_o[0]()

    def last_third():
        part_third(nz - 1)

    def fourth_and_down():
        part_fourth(nz - 1)
        start(down_hops)

    def attend_back(item):
        for at, step in (
            (0, red_o[1]), (1, last_third), (3, fourth_and_down), (4, red_o[2]), (7, red_o[3])
        ):

            @pl.when(item == at)
            def _(step=step):
                step()

        far_rows = far_of(item)
        dshares = []
        for sub, pair in units:
            rows = rows_of(item, sub)
            vv = both(rows, far_rows, cols_of(2, pair))
            dshares.append(mm(vv, by_head(mix[rows, cols_of(0, pair)], grad_a, grad_b), NT))
        far_k, far_v = [0.0] * pairs, [0.0] * pairs
        for (sub, pair), dshare in zip(units, dshares):
            rows, at = rows_of(item, sub), item * spans_here + sub
            share = prob[at, pair]
            dv = mm(share, by_head(mix[rows, cols_of(0, pair)], grad_a, grad_b))
            qkv[rows, cols_of(2, pair)] = dv[0:SPAN].astype(BF)
            far_v[pair] = far_v[pair] + dv[SPAN:]
            share = share.astype(F32)
            inner = jnp.sum(share * dshare, axis=0, keepdims=True)
            prob[at, pair] = (share * (dshare - inner)).astype(BF)
        for sub in range(spans_here):
            rows = rows_of(item, sub)
            dqs = []
            for pair in range(pairs):
                dscore = prob[item * spans_here + sub, pair]
                stacked = mm(both(rows, far_rows, cols_of(1, pair)), dscore, TN)
                dqs += [stacked[0:HEAD_DIM, 0:SPAN], stacked[HEAD_DIM:, SPAN:]]
                dk = mm(dscore, by_head(qkv[rows, cols_of(0, pair)], query_a, query_b))
                qkv[rows, cols_of(1, pair)] = dk[0:SPAN].astype(BF)
                far_k[pair] = far_k[pair] + dk[SPAN:]
            dq = jnp.concatenate(dqs, axis=0).T * score_scale
            qkv[rows, 0:width] = dq.astype(BF)
        for pair in range(pairs):
            pool_grad[far_rows, cols_of(0, pair)] = far_k[pair]
            pool_grad[far_rows, cols_of(1, pair)] = far_v[pair]

    each(items, attend_back)

    back_row = lax.broadcasted_iota(jnp.int32, (far_n, far_n), 0)
    back_col = lax.broadcasted_iota(jnp.int32, (far_n, far_n), 1)
    owner, place = back_row // blocks, back_row % blocks
    source = (place // spans_here) * spans_all + owner * spans_here + place % spans_here
    reorder = jnp.where(source == back_col, 1.0, 0.0).astype(BF)
    pool_send[...] = (
        mm(reorder, pool_grad[...].astype(BF)).astype(BF).reshape(seq_n, blocks, 2 * width)
    )
    back_hops = [
        hop(
            pool_send.at[seq_peer(step)], pool_recv.at[step - 1], POOLBACK + step - 1,
            (dp_i, seq_peer(step)),
        )
        for step in range(1, seq_n)
    ]
    start(back_hops)

    live_sum[...] = jnp.zeros_like(live_sum)

    def turn_h1(tile):
        rows = tile_rows(tile)
        _, _, h1 = first_norm(rows)
        ht_s[:, rows] = h1.astype(F32).T.astype(BF)
        live_sum[...] += mm(live_pick(tile), h1)

    each(tiles, turn_h1)
    for part in range(3):
        cols = pl.ds(part * width, width)
        gq[:, :, :, :, :, cols] = mm(ht_s[...], qkv[:, cols]).reshape(
            ny, nc, nz, nx, blk, width
        )
        if part == 0:
            red_q[0]()
    red_q[1]()
    for part in range(nz):
        arrived(part_hops(part)[3])
        total = fin_p[part]
        for step in range(nz - 1):
            total = total + r4p[step, part].astype(F32)
        for group in range(dp_n):
            at = (group * nz + part) * LANES
            fin_u[:, at : at + LANES] = total[:, group * LANES : (group + 1) * LANES]
    arrived(down_hops)
    total = keep_d[z]
    for step in range(nz - 1):
        total = total + r5d[step].astype(F32)
    fin_d[...] = total
    red_o[4]()

    arrived(back_hops)
    pool_total = pool_send[sq_i].astype(F32)
    for step in range(seq_n - 1):
        pool_total = pool_total + pool_recv[step].astype(F32)
    far = pool_total / count_col
    far_hi = far.astype(BF)
    far_lo = (far - far_hi.astype(F32)).astype(BF)
    near = live_sum[...]
    near_hi = near.astype(BF)
    near_lo = (near - near_hi.astype(F32)).astype(BF)
    left = jnp.concatenate([near_hi, near_lo, near_hi], axis=0)
    right = jnp.concatenate([far_hi, far_hi, far_lo], axis=0)
    for part in range(2):
        cols = pl.ds((part + 1) * width, width)
        gq[:, :, :, :, :, cols] += mm(left, right[:, part * width : (part + 1) * width], TN).reshape(
            ny, nc, nz, nx, blk, width
        )
    red_kv[0]()
    far_two = jnp.concatenate([far_hi, far_lo], axis=0)
    both_far = mm(far_two[:, 0:width], w_qkv(1), NT) + mm(far_two[:, width:], w_qkv(2), NT)
    spread_w[...] = both_far[0:blocks] + both_far[blocks:]

    def last_tile(tile):
        @pl.when(tile == 1)
        def _():
            red_kv[1]()

        @pl.when(tile == 2)
        def _():
            red_q[2]()

        rows = tile_rows(tile)
        hat, scale, _ = first_norm(rows)
        extra = []
        for part in range(per_tile):
            block = tile * per_tile + part
            pos = (
                sq_i * local_len
                + lax.rem(block, spans_here) * SPAN
                + lax.broadcasted_iota(jnp.int32, (SPAN, 1), 0)
            )
            live = jnp.where(pos < len_ref[block // spans_here], 1.0, 0.0)
            extra.append(live * spread_w[pl.ds(block, 1), :])
        dh1 = jnp.concatenate(extra, axis=0)
        for part in range(3):
            dh1 = dh1 + mm(qkv[rows, pl.ds(part * width, width)], w_qkv(part), NT)
        nacc[0] += fold_rows(dh1 * hat)
        nacc[1] += fold_rows(dh1)
        dx_ref[rows, :] += norm_back(dh1 * nrow[0:1, :], hat, scale)

    each(tiles, last_tile)
    keep_dx.start()
    norm_rows = [jnp.sum(nacc[k], axis=0, keepdims=True) for k in range(4)]
    norm_rows.append(jnp.zeros((4, width), F32))
    norm_seq[sq_i] = jnp.concatenate(norm_rows, axis=0)
    norm_hops = [
        hop(norm_seq.at[sq_i], norm_seq.at[sq_i], NORM_SEQ + step - 1, (dp_i, seq_peer(step)))
        for step in range(1, seq_n)
    ]
    norm_hops_dp = [
        hop(norm_dp.at[dp_i], norm_dp.at[dp_i], NORM_DP + step - 1, (dp_peer(step), sq_i))
        for step in range(1, dp_n)
    ]
    start(norm_hops)
    red_kv[2]()
    red_q[3]()
    arrived(norm_hops)
    total = norm_seq[0]
    for k in range(1, seq_n):
        total = total + norm_seq[k]
    norm_dp[dp_i] = total
    start(norm_hops_dp)
    red_kv[3]()
    red_q[4]()

    def partial(values_in):
        squares = fold_rows(values_in * values_in)
        return sum(
            squares[:, k * LANES : (k + 1) * LANES] for k in range(squares.shape[1] // LANES)
        )

    early = partial(fin_u[...]) + partial(fin_d[...]) + partial(fin_o[...])
    red_kv[4]()
    psq[sq_i] = early + partial(fin_q[...])
    seq_hops = [
        hop(psq.at[sq_i], psq.at[sq_i], SQUARE_SEQ + step - 1, (dp_i, seq_peer(step)))
        for step in range(1, seq_n)
    ]
    start(seq_hops)
    sent(back_hops)
    for part in range(nz):
        sent(part_hops(part)[3])
    sent(down_hops)
    sent(norm_hops)
    arrived(norm_hops_dp)
    sent(norm_hops_dp)
    total = norm_dp[0]
    for k in range(1, dp_n):
        total = total + norm_dp[k]
    norm_sum[...] = total
    arrived(seq_hops)
    total = psq[0]
    for k in range(1, seq_n):
        total = total + psq[k]
    psd[dp_i] = total
    dp_hops = [
        hop(psd.at[dp_i], psd.at[dp_i], SQUARE_DP + step - 1, (dp_peer(step), sq_i))
        for step in range(1, dp_n)
    ]
    start(dp_hops)
    arrived(dp_hops)
    total = psd[0]
    for k in range(1, dp_n):
        total = total + psd[k]
    total_ref[...] = total
    sent(seq_hops)
    sent(dp_hops)
    keep_act.wait()
    keep_dx.wait()


def update_kernel(
    act_in, dx_in, total_ref, gq_ref, go_ref, gu_ref, gd_ref, gn_ref,
    wq_ref, wo_ref, wu_ref, wd_ref, wn_ref, fq_ref, fo_ref, fu_ref, fd_ref, fn_ref,
    sq_ref, so_ref, su_ref, sd_ref, sn_ref,
    act_out, dx_out, norm_ref, nq, nfq, nsq, no, nfo, nso, nu, nfu, nsu, nd, nfd, nsd,
    nn, nfn, nsn, act_s, dx_s, sems_in, sems_out,
):
    pieces = 4
    piece = act_s.shape[0] // pieces
    moves = []
    for k in range(pieces):
        rows = pl.ds(k * piece, piece)
        for n, (src, mid, dst) in enumerate(
            ((dx_in, dx_s, dx_out), (act_in, act_s, act_out))
        ):
            moves.append((
                pltpu.make_async_copy(src.at[rows], mid.at[rows], sems_in.at[n * pieces + k]),
                pltpu.make_async_copy(mid.at[rows], dst.at[rows], sems_out.at[n * pieces + k]),
            ))
    for inward, _ in moves:
        inward.start()
    norm_grads = gn_ref[...]
    total = jnp.sum(total_ref[...]) + jnp.sum(norm_grads * norm_grads)
    total = jnp.full((1, 1), total, F32)
    grad_norm = jnp.sqrt(total)
    factor = clip_bound / jnp.maximum(grad_norm, clip_bound)
    norm_ref[...] = grad_norm

    def update(weight, grad_in, first, second, outs, rate, decay):
        new = adamw_update(weight, grad_in, first, second, factor, rate, decay)
        for out, value in zip(outs, new):
            out[...] = value

    for inward, outward in moves:
        inward.wait()
        outward.start()
    for w, g, m, s, outs in (
        (wq_ref, gq_ref, fq_ref, sq_ref, (nq, nfq, nsq)),
        (wo_ref, go_ref, fo_ref, so_ref, (no, nfo, nso)),
        (wu_ref, gu_ref, fu_ref, su_ref, (nu, nfu, nsu)),
        (wd_ref, gd_ref, fd_ref, sd_ref, (nd, nfd, nsd)),
    ):
        update(w[...], g[...], m[...], s[...], outs, rate_matrix, decay_coef)
    count, cols = wn_ref.shape
    width = norm_grads.shape[1]
    place = (lax.axis_index("dp") * lax.axis_size("seq") + lax.axis_index("seq")) * cols
    turned = pltpu.roll(norm_grads, lax.rem(width - place, width), 1)
    update(
        wn_ref[...], turned[0:count, 0:cols], fn_ref[...], sn_ref[...], (nn, nfn, nsn),
        rate_norm, 0.0,
    )
    for _, outward in moves:
        outward.wait()


def fused_device(
    tokens, cotangent, lengths, w_qkv, w_out, w_up, w_down, norm_params,
    first_qkv, first_out, first_up, first_down, first_norm,
    second_qkv, second_out, second_up, second_down, second_norm,
):
    item_count, local_len, width = tokens.shape
    rows_all = item_count * local_len
    dp_n, seq_n = lax.axis_size("dp"), lax.axis_size("seq")
    nc = 2
    ny = dp_n // nc
    nx = ny
    nz = seq_n // nx
    blk, width3 = w_qkv.shape
    ff = w_up.shape[1]
    dblk = w_down.shape[0]
    blocks = rows_all // SPAN
    far_n = seq_n * blocks
    keys_n = SPAN + local_len // SPAN * seq_n
    part_n = ff // nz
    up_rows = nz * blk
    half = width // 2

    def bufs(b, n):
        cut = (n // 2) // LANES * LANES
        rest = n - cut
        taken = [pltpu.VMEM((nz, nx, b, cut), BF), pltpu.VMEM((ny, nz, b, rest), BF)]
        return [
            *taken,
            pltpu.VMEM((nz, b, n), BF),
            pltpu.VMEM((ny, nz, nx, b, n), BF),
            *taken,
            pltpu.VMEM((nz, b, cut), BF),
            pltpu.VMEM((nz, b, rest), BF),
            pltpu.VMEM((nz - 1, b, n), BF),
        ]

    whole = pl.BlockSpec(memory_space=pltpu.VMEM)
    outside = pl.BlockSpec(memory_space=pl.ANY)
    part_rows = up_rows + dblk
    outs = pl.pallas_call(
        layer_kernel,
        out_shape=[
            jax.ShapeDtypeStruct((rows_all, width), BF),
            jax.ShapeDtypeStruct((rows_all, width), F32),
            jax.ShapeDtypeStruct(w_qkv.shape, F32),
            jax.ShapeDtypeStruct(w_out.shape, F32),
            jax.ShapeDtypeStruct(w_up.shape, F32),
            jax.ShapeDtypeStruct(w_down.shape, F32),
            jax.ShapeDtypeStruct((8, width), F32),
            jax.ShapeDtypeStruct((8, LANES), F32),
        ],
        in_specs=[pl.BlockSpec(memory_space=pltpu.SMEM), outside, outside] + [whole] * 5,
        out_specs=[outside, outside] + [whole] * 6,
        scratch_shapes=[
            pltpu.VMEM((ny, nc, nz, nx, blk, 2 * width + LANES), BF),
            pltpu.VMEM((ny, nc, nz, nx, blk, 2 * width), BF),
            pltpu.VMEM((ny, nc, nz, nx, blk, ff), BF),
            pltpu.VMEM((ny, nc, nz, nx, dblk, width), BF),
            pltpu.VMEM((rows_all, width3), BF),
            pltpu.VMEM((rows_all, width), BF),
            pltpu.VMEM((blocks, width // LANES, keys_n, 2 * SPAN), BF),
            pltpu.VMEM((ny, nc, nz, nx, blk, width3), F32),
            pltpu.VMEM((ny, nc, nz, nx, blk, width), F32),
            pltpu.VMEM((rows_all, width), F32),
            pltpu.VMEM((rows_all, width), BF),
            pltpu.VMEM((width, rows_all), BF),
            pltpu.VMEM((width, rows_all), BF),
            pltpu.VMEM((rows_all, part_n), BF),
            pltpu.VMEM((rows_all, part_n), BF),
            pltpu.VMEM((ny, nx, part_rows, width), F32),
            pltpu.VMEM((part_rows, width), F32),
            pltpu.VMEM((ny, nx, part_rows, width), BF),
            pltpu.VMEM((2, ny, nx, part_rows, width), BF),
            pltpu.VMEM((nx, part_rows, half), BF),
            pltpu.VMEM((ny, part_rows, half), BF),
            pltpu.VMEM((2, nx, part_rows, half), BF),
            pltpu.VMEM((2, ny, part_rows, half), BF),
            pltpu.VMEM((2, part_rows, half), BF),
            pltpu.VMEM((2, part_rows, half), BF),
            pltpu.VMEM((nz, nz, blk, width), BF),
            pltpu.VMEM((nz - 1, nz, blk, width), BF),
            pltpu.VMEM((nz, blk, width), F32),
            pltpu.VMEM((nz, dblk, width), F32),
            pltpu.VMEM((nz, dblk, width), BF),
            pltpu.VMEM((nz - 1, dblk, width), BF),
            *bufs(blk, width),
            *bufs(blk, 2 * width),
            *bufs(blk, width),
            pltpu.VMEM((seq_n, blocks, 2 * width), BF),
            pltpu.VMEM((far_n, 2 * width), BF),
            pltpu.VMEM((far_n, 2 * width), F32),
            pltpu.VMEM((seq_n, blocks, 2 * width), BF),
            pltpu.VMEM((seq_n - 1, blocks, 2 * width), BF),
            pltpu.VMEM((blocks, width), F32),
            pltpu.VMEM((blocks, width), F32),
            pltpu.VMEM((8, width), F32),
            pltpu.VMEM((4, 8, width), F32),
            pltpu.VMEM((LANES, LANES), F32),
            pltpu.VMEM((seq_n, 8, width), F32),
            pltpu.VMEM((dp_n, 8, width), F32),
            pltpu.VMEM((seq_n, 8, LANES), F32),
            pltpu.VMEM((dp_n, 8, LANES), F32),
            pltpu.VMEM((rows_all, width), BF),
            pltpu.VMEM((rows_all, width), BF),
            pltpu.VMEM((rows_all, width), F32),
            pltpu.SemaphoreType.DMA((COPIES,)),
            pltpu.SemaphoreType.DMA((COPIES,)),
            pltpu.SemaphoreType.DMA((4,)),
        ],
        compiler_params=pltpu.CompilerParams(
            collective_id=0, has_side_effects=True, vmem_limit_bytes=64 * 1024 * 1024 - 65536
        ),
    )(
        lengths,
        tokens.reshape(rows_all, width),
        cotangent.reshape(rows_all, width),
        w_qkv, w_out, w_up, w_down, norm_params,
    )
    weights = (w_qkv, w_out, w_up, w_down, norm_params)
    new = pl.pallas_call(
        update_kernel,
        out_shape=[
            jax.ShapeDtypeStruct((rows_all, width), BF),
            jax.ShapeDtypeStruct((rows_all, width), F32),
            jax.ShapeDtypeStruct((1, 1), F32),
            *(jax.ShapeDtypeStruct(w.shape, F32) for w in weights for _ in range(3)),
        ],
        in_specs=[outside, outside] + [whole] * 21,
        out_specs=[outside, outside] + [whole] * 16,
        scratch_shapes=[
            pltpu.VMEM((rows_all, width), BF),
            pltpu.VMEM((rows_all, width), F32),
            pltpu.SemaphoreType.DMA((8,)),
            pltpu.SemaphoreType.DMA((8,)),
        ],
        compiler_params=pltpu.CompilerParams(vmem_limit_bytes=64 * 1024 * 1024 - 65536),
    )(
        outs[0], outs[1], outs[7], *outs[2:7], *weights,
        first_qkv, first_out, first_up, first_down, first_norm,
        second_qkv, second_out, second_up, second_down, second_norm,
    )
    return (
        new[0].reshape(tokens.shape), new[1].reshape(tokens.shape), new[2].reshape(()),
        *new[3:],
    )


def solution(mesh):
    placed = (
        P("dp", "seq", None),
        P("dp", "seq", None),
        P("dp"),
        P(("dp", "seq"), None),
        P(("dp", "seq"), None),
        P(("dp", "seq"), None),
        P(("dp", "seq"), None),
        P(None, ("dp", "seq")),
        P(("dp", "seq"), None),
        P(("dp", "seq"), None),
        P(("dp", "seq"), None),
        P(("dp", "seq"), None),
        P(None, ("dp", "seq")),
        P(("dp", "seq"), None),
        P(("dp", "seq"), None),
        P(("dp", "seq"), None),
        P(("dp", "seq"), None),
        P(None, ("dp", "seq")),
    )
    dp_n, seq_n = mesh.shape["dp"], mesh.shape["seq"]
    fits = dp_n == 4 and seq_n % 2 == 0 and WIDTH // (dp_n * seq_n) == 16
    return jax.shard_map(
        fused_device if fits else generic_device,
        mesh=mesh,
        in_specs=placed,
        out_specs=(
            P("dp", "seq", None),
            P("dp", "seq", None),
            P(),
            P(("dp", "seq"), None),
            P(("dp", "seq"), None),
            P(("dp", "seq"), None),
            P(("dp", "seq"), None),
            P(("dp", "seq"), None),
            P(("dp", "seq"), None),
            P(("dp", "seq"), None),
            P(("dp", "seq"), None),
            P(("dp", "seq"), None),
            P(("dp", "seq"), None),
            P(("dp", "seq"), None),
            P(("dp", "seq"), None),
            P(None, ("dp", "seq")),
            P(None, ("dp", "seq")),
            P(None, ("dp", "seq")),
        ),
        check_vma=False,
    )
```

```python
import functools
import math

import jax
import jax.numpy as jnp
from jax import lax
from jax.experimental import pallas as pl
from jax.experimental.pallas import tpu as pltpu
from jax.sharding import PartitionSpec as P

HEADS = 8
HEAD_DIM = 64
SPAN = 128
STEP = 10
WIDTH = 512


eps_norm = 1e-05
neg_fill = -1e30
beta_one = 0.9
beta_two = 0.999
adam_eps = 1e-08
decay_coef = 0.1
rate_matrix = 0.05
rate_norm = 0.5
clip_bound = 1.0


def normalize(values_in, gain_row, shift_row):
    center = values_in - jnp.mean(values_in, axis=-1, keepdims=True)
    spread = jnp.mean(center * center, axis=-1, keepdims=True)
    return center * lax.rsqrt(spread + eps_norm) * gain_row + shift_row


def adamw_update(weight, grad_in, first_old, second_old, factor, step_rate, weight_decay):
    clipped = grad_in * factor
    first_new = beta_one * first_old + (1.0 - beta_one) * clipped
    second_new = beta_two * second_old + (1.0 - beta_two) * clipped * clipped
    first_hat = first_new / (1.0 - beta_one**STEP)
    second_hat = second_new / (1.0 - beta_two**STEP)
    weight_new = weight - step_rate * (
        first_hat / (jnp.sqrt(second_hat) + adam_eps) + weight_decay * weight
    )
    return (weight_new, first_new, second_new)


def generic_device(
    tokens,
    cotangent,
    lengths,
    w_qkv,
    w_out,
    w_up,
    w_down,
    norm_params,
    first_qkv,
    first_out,
    first_up,
    first_down,
    first_norm,
    second_qkv,
    second_out,
    second_up,
    second_down,
    second_norm,
):
    item_count, local_len, model_width = tokens.shape
    row_count = item_count * local_len
    spans_here = local_len // SPAN
    spans_all = spans_here * lax.axis_size("seq")
    seq_rank = lax.axis_index("seq")
    score_scale = HEAD_DIM ** (-0.5)
    full_qkv, full_out, full_up, full_down, full_norm = (
        lax.all_gather(w_qkv.astype(jnp.bfloat16), ("dp", "seq"), axis=0, tiled=True),
        lax.all_gather(w_out.astype(jnp.bfloat16), ("dp", "seq"), axis=0, tiled=True),
        lax.all_gather(w_up.astype(jnp.bfloat16), ("dp", "seq"), axis=0, tiled=True),
        lax.all_gather(w_down.astype(jnp.bfloat16), ("dp", "seq"), axis=0, tiled=True),
        lax.all_gather(norm_params.astype(jnp.bfloat16), ("dp", "seq"), axis=1, tiled=True),
    )
    norm_rows = full_norm.astype(jnp.float32)
    tokens_f = tokens.reshape(row_count, model_width).astype(jnp.float32)
    normed, back_one = jax.vjp(normalize, tokens_f, norm_rows[0], norm_rows[1])
    normed_b = normed.astype(jnp.bfloat16)
    qkv_b = jnp.dot(normed_b, full_qkv, preferred_element_type=jnp.float32).astype(jnp.bfloat16)
    qkv_view = qkv_b.reshape(item_count, spans_here, SPAN, 3, HEADS, HEAD_DIM)
    query_part = qkv_view[:, :, :, 0]
    key_part = qkv_view[:, :, :, 1]
    value_part = qkv_view[:, :, :, 2]
    local_pos = seq_rank * local_len + jnp.arange(local_len, dtype=jnp.int32)
    live_mask = (local_pos[None, :] < lengths[:, None]).reshape(item_count, spans_here, SPAN)
    live_f = live_mask.astype(jnp.float32)
    counts_here = jnp.maximum(jnp.sum(live_f, axis=2), 1.0)
    pooled = jnp.einsum(
        "ist,istchd->ischd",
        live_mask.astype(jnp.bfloat16),
        qkv_view[:, :, :, 1:],
        preferred_element_type=jnp.float32,
    )
    pooled = (pooled / counts_here[:, :, None, None, None]).astype(jnp.bfloat16)
    pooled_all = lax.all_gather(pooled, "seq", axis=1, tiled=True)
    pooled_keys = pooled_all[:, :, 0]
    pooled_values = pooled_all[:, :, 1]
    all_pos = jnp.arange(spans_all * SPAN, dtype=jnp.int32).reshape(spans_all, SPAN)
    counts_all = jnp.sum((all_pos[None] < lengths[:, None, None]).astype(jnp.float32), axis=2)
    span_ids = seq_rank * spans_here + jnp.arange(spans_here, dtype=jnp.int32)
    far_valid = (counts_all[:, None, :] > 0.0) & (
        span_ids[None, :, None] != jnp.arange(spans_all, dtype=jnp.int32)[None, None, :]
    )
    near_mask = live_mask[:, :, None, None, :]
    far_mask = far_valid[:, :, None, None, :]

    def scores_of():
        near_raw = (
            jnp.einsum(
                "isqhd,iskhd->ishqk", query_part, key_part, preferred_element_type=jnp.float32
            )
            * score_scale
        )
        far_raw = (
            jnp.einsum(
                "isqhd,irhd->ishqr", query_part, pooled_keys, preferred_element_type=jnp.float32
            )
            * score_scale
        )
        return (jnp.where(near_mask, near_raw, neg_fill), jnp.where(far_mask, far_raw, neg_fill))

    near_s, far_s = scores_of()
    score_top = jnp.maximum(
        jnp.max(near_s, axis=-1, keepdims=True), jnp.max(far_s, axis=-1, keepdims=True)
    )
    exp_total = jnp.sum(jnp.exp(near_s - score_top), axis=-1, keepdims=True) + jnp.sum(
        jnp.exp(far_s - score_top), axis=-1, keepdims=True
    )
    log_total = score_top + jnp.log(exp_total)
    near_pb = jnp.exp(near_s - log_total).astype(jnp.bfloat16)
    far_pb = jnp.exp(far_s - log_total).astype(jnp.bfloat16)
    mixed_rows = jnp.einsum(
        "ishqk,iskhd->isqhd", near_pb, value_part, preferred_element_type=jnp.float32
    )
    mixed_rows = mixed_rows + jnp.einsum(
        "ishqr,irhd->isqhd", far_pb, pooled_values, preferred_element_type=jnp.float32
    )
    mixed_b = mixed_rows.reshape(row_count, model_width).astype(jnp.bfloat16)
    residual = tokens_f + jnp.dot(mixed_b, full_out, preferred_element_type=jnp.float32)
    normed_two, back_two = jax.vjp(normalize, residual, norm_rows[2], norm_rows[3])
    normed_two_b = normed_two.astype(jnp.bfloat16)
    up_pre = jnp.dot(normed_two_b, full_up, preferred_element_type=jnp.float32)
    gated, gelu_back = jax.vjp(jax.nn.gelu, up_pre)
    gated_b = gated.astype(jnp.bfloat16)
    layer_out = residual + jnp.dot(gated_b, full_down, preferred_element_type=jnp.float32)
    activations = layer_out.astype(jnp.bfloat16).reshape(item_count, local_len, model_width)
    grad_out_b = cotangent.reshape(row_count, model_width)
    grad_down = jnp.dot(gated_b.T, grad_out_b, preferred_element_type=jnp.float32)
    grad_gated = jnp.dot(grad_out_b, full_down.T, preferred_element_type=jnp.float32)
    grad_up_pre = gelu_back(grad_gated)[0].astype(jnp.bfloat16)
    grad_up = jnp.dot(normed_two_b.T, grad_up_pre, preferred_element_type=jnp.float32)
    grad_normed_two = jnp.dot(grad_up_pre, full_up.T, preferred_element_type=jnp.float32)
    grad_resid_ln, grad_gain_two, grad_shift_two = back_two(grad_normed_two)
    grad_resid = grad_out_b.astype(jnp.float32) + grad_resid_ln
    grad_attn_b = grad_resid.astype(jnp.bfloat16)
    grad_out_proj = jnp.dot(mixed_b.T, grad_attn_b, preferred_element_type=jnp.float32)
    grad_mixed = jnp.dot(grad_attn_b, full_out.T, preferred_element_type=jnp.float32).astype(
        jnp.bfloat16
    )
    grad_mixed = grad_mixed.reshape(item_count, spans_here, SPAN, HEADS, HEAD_DIM)
    near_s, far_s = scores_of()
    near_pf = jnp.exp(near_s - log_total)
    far_pf = jnp.exp(far_s - log_total)
    near_pb = near_pf.astype(jnp.bfloat16)
    far_pb = far_pf.astype(jnp.bfloat16)
    grad_near = jnp.einsum(
        "isqhd,iskhd->ishqk", grad_mixed, value_part, preferred_element_type=jnp.float32
    )
    grad_far = jnp.einsum(
        "isqhd,irhd->ishqr", grad_mixed, pooled_values, preferred_element_type=jnp.float32
    )
    row_delta = jnp.sum(near_pf * grad_near, axis=-1, keepdims=True) + jnp.sum(
        far_pf * grad_far, axis=-1, keepdims=True
    )
    dscore_near = (near_pf * (grad_near - row_delta)).astype(jnp.bfloat16)
    dscore_far = (far_pf * (grad_far - row_delta)).astype(jnp.bfloat16)
    grad_query = jnp.einsum(
        "ishqk,iskhd->isqhd", dscore_near, key_part, preferred_element_type=jnp.float32
    )
    grad_query = (
        grad_query
        + jnp.einsum(
            "ishqr,irhd->isqhd", dscore_far, pooled_keys, preferred_element_type=jnp.float32
        )
    ) * score_scale
    grad_keys = (
        jnp.einsum(
            "ishqk,isqhd->iskhd", dscore_near, query_part, preferred_element_type=jnp.float32
        )
        * score_scale
    )
    grad_values = jnp.einsum(
        "ishqk,isqhd->iskhd", near_pb, grad_mixed, preferred_element_type=jnp.float32
    )
    grad_pool_keys = (
        jnp.einsum("ishqr,isqhd->irhd", dscore_far, query_part, preferred_element_type=jnp.float32)
        * score_scale
    )
    grad_pool_values = jnp.einsum(
        "ishqr,isqhd->irhd", far_pb, grad_mixed, preferred_element_type=jnp.float32
    )
    pool_grads = jnp.stack([grad_pool_keys, grad_pool_values], axis=2)
    pool_mine = lax.psum_scatter(
        pool_grads.astype(jnp.bfloat16), "seq", scatter_dimension=1, tiled=True
    ).astype(jnp.float32)
    spread_back = pool_mine / counts_here[:, :, None, None, None]
    grad_kv = (
        jnp.stack([grad_keys, grad_values], axis=3)
        + live_f[:, :, :, None, None, None] * spread_back[:, :, None]
    )
    grad_qkv_rows = jnp.concatenate([grad_query[:, :, :, None], grad_kv], axis=3)
    grad_qkv_b = grad_qkv_rows.reshape(row_count, 3 * model_width).astype(jnp.bfloat16)
    grad_qkv = jnp.dot(normed_b.T, grad_qkv_b, preferred_element_type=jnp.float32)
    grad_normed = jnp.dot(grad_qkv_b, full_qkv.T, preferred_element_type=jnp.float32)
    grad_in_ln, grad_gain_one, grad_shift_one = back_one(grad_normed)
    input_grad = (grad_resid + grad_in_ln).reshape(item_count, local_len, model_width)
    grad_norm_rows = jnp.stack([grad_gain_one, grad_shift_one, grad_gain_two, grad_shift_two])
    red_qkv, red_out, red_up, red_down, red_norm = (
        lax.psum_scatter(grad_qkv, ("dp", "seq"), scatter_dimension=0, tiled=True),
        lax.psum_scatter(grad_out_proj, ("dp", "seq"), scatter_dimension=0, tiled=True),
        lax.psum_scatter(grad_up, ("dp", "seq"), scatter_dimension=0, tiled=True),
        lax.psum_scatter(grad_down, ("dp", "seq"), scatter_dimension=0, tiled=True),
        lax.psum_scatter(grad_norm_rows, ("dp", "seq"), scatter_dimension=1, tiled=True),
    )
    squares = jnp.sum(red_qkv * red_qkv) + jnp.sum(red_out * red_out) + jnp.sum(red_up * red_up)
    squares = squares + jnp.sum(red_down * red_down) + jnp.sum(red_norm * red_norm)
    total_sq = lax.psum(squares, ("dp", "seq"))
    grad_norm = jnp.sqrt(total_sq)
    factor = clip_bound / jnp.maximum(grad_norm, clip_bound)
    new_qkv, new_first_qkv, new_second_qkv = adamw_update(
        w_qkv, red_qkv, first_qkv, second_qkv, factor, rate_matrix, decay_coef
    )
    new_out, new_first_out, new_second_out = adamw_update(
        w_out, red_out, first_out, second_out, factor, rate_matrix, decay_coef
    )
    new_up, new_first_up, new_second_up = adamw_update(
        w_up, red_up, first_up, second_up, factor, rate_matrix, decay_coef
    )
    new_down, new_first_down, new_second_down = adamw_update(
        w_down, red_down, first_down, second_down, factor, rate_matrix, decay_coef
    )
    new_norm, new_first_norm, new_second_norm = adamw_update(
        norm_params, red_norm, first_norm, second_norm, factor, rate_norm, 0.0
    )
    return (
        activations,
        input_grad,
        grad_norm,
        new_qkv,
        new_first_qkv,
        new_second_qkv,
        new_out,
        new_first_out,
        new_second_out,
        new_up,
        new_first_up,
        new_second_up,
        new_down,
        new_first_down,
        new_second_down,
        new_norm,
        new_first_norm,
        new_second_norm,
    )


BF = jnp.bfloat16
F32 = jnp.float32
MESH = pl.DeviceIdType.MESH
LANES = 128
TILE = 512
NN = (((1,), (0,)), ((), ()))
NT = (((1,), (1,)), ((), ()))
TN = (((0,), (0,)), ((), ()))
GATHER, SPREAD, PARTS, DOWN, OUTER, INNER, POOL, POOLBACK = 0, 22, 62, 94, 97, 105, 121, 128
NORM_SEQ, NORM_DP, SQUARE_SEQ, SQUARE_DP, COPIES = 135, 142, 145, 152, 155


def mm(left, right, dims=NN):
    return lax.dot_general(left, right, dims, preferred_element_type=F32)


def centered(values_in):
    center = values_in - jnp.mean(values_in, axis=-1, keepdims=True)
    scale = lax.rsqrt(jnp.mean(center * center, axis=-1, keepdims=True) + eps_norm)
    return center * scale, scale


def norm_back(grad_hat, hat, scale):
    mean_grad = jnp.mean(grad_hat, axis=-1, keepdims=True)
    mean_both = jnp.mean(grad_hat * hat, axis=-1, keepdims=True)
    return scale * (grad_hat - mean_grad - hat * mean_both)


def fold_rows(values_in):
    rows, width = values_in.shape
    return jnp.sum(values_in.reshape(rows // 8, 8, width), axis=0)


def layer_kernel(
    len_ref, x_any, dy_any, wq_ref, wo_ref, wu_ref, wd_ref, nrm_ref,
    act_any, dx_any, fin_q, fin_o, fin_u, fin_d, norm_sum, total_ref,
    bkv, bqo, bu, bd, qkv, mix, prob, gq, go, yacc, h2_s, ht_s, dyt_s, act_s, dup_s,
    own_p, kept_p, s1p, r1p, s2ap, s2bp, r2ap, r2bp, r3ap, r3bp, s4p, r4p, fin_p, keep_d, s5d, r5d,
    s2aq, s2bq, s3q, r1q, r2aq, r2bq, r3aq, r3bq, r4q,
    s2ak, s2bk, s3k, r1k, r2ak, r2bk, r3ak, r3bk, r4k,
    s2ao, s2bo, s3o, r1o, r2ao, r2bo, r3ao, r3bo, r4o,
    pool_all, pool_far, pool_grad, pool_send, pool_recv, live_sum, spread_w,
    nrow, nacc, ntall, norm_seq, norm_dp, psq, psd, x_ref, dy_ref, dx_ref,
    send_sem, recv_sem, local_sem,
):
    ny, nc, nz, nx, blk, _ = bu.shape
    dblk = bd.shape[4]
    rows_all, width = x_ref.shape
    width3 = 3 * width
    ff = wu_ref.shape[1]
    seq_n = nz * nx
    dp_n = ny * nc
    local_len = rows_all // len_ref.shape[0]
    spans_here = local_len // SPAN
    blocks = rows_all // SPAN
    spans_all = spans_here * seq_n
    tiles = rows_all // TILE
    per_tile = TILE // SPAN
    pairs = width // LANES
    part_n = ff // nz
    ffn_rows = 2 * TILE
    dp_i = lax.axis_index("dp")
    sq_i = lax.axis_index("seq")
    y, c = dp_i // nc, dp_i % nc
    z, x = sq_i // nx, sq_i % nx

    def dev(yy, cc, zz, xx):
        return (yy * nc + cc, zz * nx + xx)

    twin = dev(y, 1 - c, z, x)
    over_x = dev(y, c, z, 1 - x)
    over_y = dev(1 - y, c, z, x)

    def seq_peer(step):
        return lax.rem(sq_i + step, seq_n)

    def dp_peer(step):
        return lax.rem(dp_i + step, dp_n)

    def z_peer(step):
        return lax.rem(z + step, nz)

    def hop(src, dst, index, target):
        return pltpu.make_async_remote_copy(
            src_ref=src, dst_ref=dst, send_sem=send_sem.at[index],
            recv_sem=recv_sem.at[index], device_id=target, device_id_type=MESH,
        )

    def start(hops):
        for one in hops:
            one.start()

    def arrived(hops):
        for one in hops:
            one.wait_recv()

    def sent(hops):
        for one in hops:
            one.wait_send()

    def each(count, body):
        def step(index, carry):
            body(index)
            return carry

        lax.fori_loop(0, count, step, 0)

    def flat(count, body):
        for index in range(count):
            body(index)

    def tile_rows(tile):
        if isinstance(tile, int):
            return pl.ds(tile * TILE, TILE)
        return pl.ds(pl.multiple_of(tile * TILE, TILE), TILE)

    load_x = pltpu.make_async_copy(x_any, x_ref, local_sem.at[0])
    load_dy = pltpu.make_async_copy(dy_any, dy_ref, local_sem.at[1])
    keep_act = pltpu.make_async_copy(dy_ref, act_any, local_sem.at[2])
    keep_dx = pltpu.make_async_copy(dx_ref, dx_any, local_sem.at[3])
    load_dy.start()
    load_x.start()

    barrier = pltpu.get_barrier_semaphore()
    for step in range(1, seq_n):
        pl.semaphore_signal(
            barrier, inc=1, device_id=(dp_i, seq_peer(step)), device_id_type=MESH
        )
    for step in range(1, dp_n):
        pl.semaphore_signal(
            barrier, inc=1, device_id=(dp_peer(step), sq_i), device_id_type=MESH
        )

    bkv[y, c, z, x, :, 0 : 2 * width] = wq_ref[:, width:].astype(BF)
    bqo[y, c, z, x, :, 0:width] = wq_ref[:, 0:width].astype(BF)
    bqo[y, c, z, x, :, width:] = wo_ref[...].astype(BF)
    count = nrm_ref.shape[0]
    ntall[...] = jnp.zeros_like(ntall)
    ntall[0:count, 0:blk] = nrm_ref[...]
    bkv[y, c, z, x, :, 2 * width :] = ntall[...].T[0:blk].astype(BF)
    for part in range(nz):
        for group in range(dp_n):
            lo, at = part * part_n + group * LANES, (group * nz + part) * LANES
            bu[y, c, z, x, :, lo : lo + LANES] = wu_ref[:, at : at + LANES].astype(BF)
    bd[y, c, z, x] = wd_ref[...].astype(BF)
    pl.semaphore_wait(barrier, seq_n + dp_n - 2)

    def gather_hops(full, base):
        cut = (full.shape[5] // 2) // LANES * LANES
        one, two = pl.ds(0, cut), pl.ds(cut, full.shape[5] - cut)

        def same(part, index, target):
            return hop(part, part, base + index, target)

        first = [
            same(full.at[y, c, z, x], step - 1, dev(y, c, z_peer(step), x))
            for step in range(1, nz)
        ]
        second = [
            same(full.at[y, c, :, x, :, one], 3, over_x),
            same(full.at[y, c, :, x, :, two], 4, over_y),
        ]
        third = [
            same(full.at[y, c, :, :, :, one], 5, over_y),
            same(full.at[:, c, :, x, :, two], 6, over_x),
        ]
        last = [same(full.at[:, c], 7, twin)]
        return first, second, third, last

    def direct(full, base):
        mine = full.at[y, c, z, x]
        return [
            hop(mine, mine, base + step - 1, dev(y, c, z_peer(step), x)) for step in range(1, nz)
        ]

    def spread_hops(part):
        base = SPREAD + part * 10
        cols = pl.ds(pl.multiple_of(part * part_n, part_n), part_n)
        one = pl.ds(pl.multiple_of(part * part_n, LANES), part_n // 2)
        two = pl.ds(pl.multiple_of(part * part_n + part_n // 2, LANES), part_n // 2)
        d_one, d_two = pl.ds(0, width // 2), pl.ds(width // 2, width // 2)

        def same(place, index, target):
            return hop(place, place, base + index, target)

        return (
            [
                same(bu.at[y, c, :, x, :, one], 0, over_x),
                same(bu.at[y, c, :, x, :, two], 1, over_y),
                same(bd.at[y, c, part, x, :, d_one], 2, over_x),
                same(bd.at[y, c, part, x, :, d_two], 3, over_y),
            ],
            [
                same(bu.at[y, c, :, :, :, one], 4, over_y),
                same(bu.at[:, c, :, x, :, two], 5, over_x),
                same(bd.at[y, c, part, :, :, d_one], 6, over_y),
                same(bd.at[:, c, part, x, :, d_two], 7, over_x),
            ],
            [
                same(bu.at[:, c, :, :, :, cols], 8, twin),
                same(bd.at[:, c, part], 9, twin),
            ],
        )

    def pass_on(part, stage):
        hops = spread_hops(part)
        arrived(hops[stage])
        start(hops[stage + 1])

    hops_kv = gather_hops(bkv, GATHER)
    hops_qo = gather_hops(bqo, GATHER + 8)
    direct_u = direct(bu, GATHER + 16)
    direct_d = direct(bd, GATHER + 19)
    start(hops_kv[0])
    start(hops_qo[0])
    nacc[...] = jnp.zeros_like(nacc)
    arrived(hops_kv[0])
    start(hops_kv[1])
    start(direct_u)
    start(direct_d)
    load_dy.wait()

    def turn_dy(tile):
        rows = tile_rows(tile)
        dyt_s[:, rows] = dy_ref[rows, :].astype(F32).T.astype(BF)

    each(tiles // 2, turn_dy)
    arrived(hops_kv[1])
    start(hops_kv[2])
    arrived(hops_qo[0])
    start(hops_qo[1])
    load_x.wait()
    each(tiles // 2, lambda tile: turn_dy(tile + tiles // 2))

    def first_hat(tile):
        rows = tile_rows(tile)
        dx_ref[rows, :] = centered(x_ref[rows, :].astype(F32))[0]

    each(tiles, first_hat)
    arrived(hops_kv[2])
    start(hops_kv[3])
    arrived(hops_qo[1])
    start(hops_qo[2])
    arrived(direct_u)
    arrived(direct_d)
    for part in range(nz):
        start(spread_hops(part)[0])
    arrived(hops_kv[3])

    norm_cols = bkv[:, :, :, :, :, 2 * width :].reshape(width, LANES).astype(F32)
    nrow[...] = norm_cols.T[0:8]

    def w_qkv(part):
        if part == 0:
            return bqo[:, :, :, :, :, 0:width].reshape(width, width)
        return bkv[:, :, :, :, :, (part - 1) * width : part * width].reshape(width, width)

    def first_norm(rows):
        hat, scale = centered(x_ref[rows, :].astype(F32))
        return hat, scale, (hat * nrow[0:1, :] + nrow[1:2, :]).astype(BF)

    def live_pick(tile):
        block_at = lax.broadcasted_iota(jnp.int32, (blocks, TILE), 0)
        row_at = lax.broadcasted_iota(jnp.int32, (blocks, TILE), 1) + tile * TILE
        pos = sq_i * local_len + lax.rem(row_at, local_len)
        item = row_at // local_len
        length = jnp.zeros((blocks, TILE), jnp.int32)
        for i in range(TILE // local_len):
            at = tile * (TILE // local_len) + i
            length = jnp.where(item == at, len_ref[at], length)
        return jnp.where((row_at // SPAN == block_at) & (pos < length), 1.0, 0.0).astype(BF)

    def kv_tile(tile, pooled):
        rows = tile_rows(tile)
        h1 = (dx_ref[rows, :] * nrow[0:1, :] + nrow[1:2, :]).astype(BF)
        h2_s[rows, :] = h1
        for part in (1, 2):
            qkv[rows, pl.ds(part * width, width)] = mm(h1, w_qkv(part)).astype(BF)

        if tile == 3:
            arrived(hops_qo[2])
            start(hops_qo[3])
        return pooled + mm(live_pick(tile), qkv[rows, width:])

    pooled = jnp.zeros((blocks, 2 * width), F32)
    for index in range(tiles):
        pooled = kv_tile(index, pooled)
    block_col = lax.broadcasted_iota(jnp.int32, (blocks, 1), 0)
    length_col = jnp.zeros((blocks, 1), jnp.int32)
    for i in range(blocks // spans_here):
        length_col = jnp.where(block_col // spans_here == i, len_ref[i], length_col)
    first_pos = sq_i * local_len + lax.rem(block_col, spans_here) * SPAN
    count_col = jnp.clip(length_col - first_pos, 1, SPAN).astype(F32)
    pool_all[sq_i] = (pooled / count_col).astype(BF)
    pool_hops = [
        hop(pool_all.at[sq_i], pool_all.at[sq_i], POOL + step - 1, (dp_i, seq_peer(step)))
        for step in range(1, seq_n)
    ]
    start(pool_hops)
    pass_on(0, 0)
    arrived(hops_qo[3])

    def q_tile(tile):
        rows = tile_rows(tile)
        qkv[rows, 0:width] = mm(h2_s[rows, :], w_qkv(0)).astype(BF)

    flat(tiles, q_tile)
    arrived(pool_hops)

    far_n = seq_n * blocks
    to_row = lax.broadcasted_iota(jnp.int32, (far_n, far_n), 0)
    to_col = lax.broadcasted_iota(jnp.int32, (far_n, far_n), 1)
    item_row, span_row = to_row // spans_all, to_row % spans_all
    wanted = (span_row // spans_here) * blocks + item_row * spans_here + span_row % spans_here
    order = jnp.where(wanted == to_col, 1.0, 0.0).astype(BF)
    pool_far[...] = mm(order, pool_all[...].reshape(far_n, 2 * width)).astype(BF)

    keys_n = SPAN + spans_all
    lane = lax.broadcasted_iota(jnp.int32, (1, LANES), 1)
    score_scale = HEAD_DIM ** (-0.5)
    half_a = jnp.where(lane < HEAD_DIM, 1.0, 0.0)
    half_b = jnp.where(lane >= HEAD_DIM, 1.0, 0.0)
    query_a, query_b = (half_a * score_scale).astype(BF), (half_b * score_scale).astype(BF)
    grad_a, grad_b = half_a.astype(BF), half_b.astype(BF)

    def both(near_rows, far_rows, cols):
        far_cols = pl.ds(cols.start - width, cols.size)
        return jnp.concatenate([qkv[near_rows, cols], pool_far[far_rows, far_cols]], axis=0)

    def cols_of(third, pair):
        return pl.ds(third * width + pair * LANES, LANES)

    def by_head(rows_in, first, second):
        return jnp.concatenate([rows_in * first, rows_in * second], axis=0)

    units = [(sub, pair) for sub in range(spans_here) for pair in range(pairs)]
    items = blocks // spans_here

    def rows_of(item, sub):
        return pl.ds(pl.multiple_of(item * local_len + sub * SPAN, SPAN), SPAN)

    def far_of(item):
        return pl.ds(pl.multiple_of(item * spans_all, spans_all), spans_all)

    def attend(item):
        for at, moves in (
            (0, ((1, 0),)), (2, ((0, 1), (2, 0))), (4, ((3, 0),)), (7, ((1, 1),)),
        ):

            @pl.when(item == at)
            def _(moves=moves):
                for part, stage in moves:
                    pass_on(part, stage)

        far_rows = far_of(item)
        length = len_ref[item]
        key_at = lax.broadcasted_iota(jnp.int32, (keys_n, 2 * SPAN), 0)
        span_at = key_at - SPAN

        def seen(sub):
            mine = sq_i * spans_here + sub
            near_ok = (key_at < SPAN) & (mine * SPAN + key_at < length)
            return near_ok | ((key_at >= SPAN) & (span_at * SPAN < length) & (span_at != mine))

        scores = []
        for sub, pair in units:
            rows = rows_of(item, sub)
            kk = both(rows, far_rows, cols_of(1, pair))
            scores.append(mm(kk, by_head(qkv[rows, cols_of(0, pair)], query_a, query_b), NT))
        for (sub, pair), score in zip(units, scores):
            score = jnp.where(seen(sub), score, neg_fill)
            raised = jnp.exp(score - jnp.max(score, axis=0, keepdims=True))
            share = raised * (1.0 / jnp.sum(raised, axis=0, keepdims=True))
            prob[item * spans_here + sub, pair] = share.astype(BF)
        for sub in range(spans_here):
            rows = rows_of(item, sub)
            mixed = []
            for pair in range(pairs):
                vv = both(rows, far_rows, cols_of(2, pair))
                stacked = mm(vv, prob[item * spans_here + sub, pair], TN)
                mixed += [stacked[0:HEAD_DIM, 0:SPAN], stacked[HEAD_DIM:, SPAN:]]
            mix[rows, :] = jnp.concatenate(mixed, axis=0).T.astype(BF)

    each(items, attend)
    for group in (*hops_kv, *hops_qo, direct_u, direct_d, pool_hops):
        sent(group)

    w_out = bqo[:, :, :, :, :, width:].reshape(width, width)
    gelu_in = math.sqrt(2.0 / math.pi)
    gelu_cube = 0.044715

    def second_norm(rows):
        x1 = x_ref[rows, :].astype(F32) + mm(mix[rows, :], w_out)
        hat, scale = centered(x1)
        return x1, hat, scale

    def ffn_open(tile):
        if tile == 2:
            pass_on(2, 1)
        rows = tile_rows(tile)
        x1, hat, _ = second_norm(rows)
        yacc[rows, :] = x1
        dx_ref[rows, :] = jnp.zeros((TILE, width), F32)
        h2 = hat * nrow[2:3, :] + nrow[3:4, :]
        h2_s[rows, :] = h2.astype(BF)
        ht_s[:, rows] = h2.T.astype(BF)

    flat(tiles, ffn_open)

    half_cols = width // 2
    one_p, two_p = pl.ds(0, half_cols), pl.ds(half_cols, half_cols)
    up_rows = nz * blk

    def part_hops(part):
        base = PARTS + part * 8
        slot = part % 2
        return (
            [hop(s1p, r1p.at[slot], base, twin)],
            [
                hop(s1p.at[1 - y, :, :, one_p], r2ap.at[slot], base + 1, over_y),
                hop(s1p.at[:, 1 - x, :, two_p], r2bp.at[slot], base + 2, over_x),
            ],
            [
                hop(s2ap.at[1 - x], r3ap.at[slot], base + 3, over_x),
                hop(s2bp.at[1 - y], r3bp.at[slot], base + 4, over_y),
            ],
            [
                hop(
                    s4p.at[part, z_peer(step)], r4p.at[step - 1, part], base + 4 + step,
                    dev(y, c, z_peer(step), x),
                )
                for step in range(1, nz)
            ],
        )

    def down_cols(group):
        cols = pl.ds(pl.multiple_of(group * LANES, LANES), LANES)
        return gq[:, :, :, :, :, cols].reshape(width, LANES)

    def part_first(part):
        for yy in range(ny):
            for xx in range(nx):
                for zz in range(nz):
                    at = pl.ds(zz * blk, blk)
                    own_p[yy, xx, at] = go[yy, c, zz, xx]
                    s1p[yy, xx, at] = go[yy, 1 - c, zz, xx].astype(BF)
            mine = down_cols(yy * nc + c).T
            other = down_cols(yy * nc + 1 - c).T
            for xx in range(nx):
                own_p[yy, xx, up_rows:] = mine[xx * dblk : (xx + 1) * dblk]
                s1p[yy, xx, up_rows:] = other[xx * dblk : (xx + 1) * dblk].astype(BF)
        start(part_hops(part)[0])

    def part_second(part):
        hops = part_hops(part)
        arrived(hops[0])
        sent(hops[0])

        def add(index):
            yy, xx = index // nx, index % nx
            total = own_p[yy, xx] + r1p[part % 2, yy, xx].astype(F32)
            own_p[yy, xx] = total
            s1p[yy, xx] = total.astype(BF)

        each(ny * nx, add)
        start(hops[1])

    def part_third(part):
        hops = part_hops(part)
        arrived(hops[1])
        sent(hops[1])
        for xx in range(nx):
            total = own_p[y, xx, :, one_p] + r2ap[part % 2, xx].astype(F32)
            own_p[y, xx, :, one_p] = total
            s2ap[xx] = total.astype(BF)
        for yy in range(ny):
            total = own_p[yy, x, :, two_p] + r2bp[part % 2, yy].astype(F32)
            own_p[yy, x, :, two_p] = total
            s2bp[yy] = total.astype(BF)
        kept_p[...] = own_p[y, x]
        start(hops[2])

    def part_fourth(part):
        hops = part_hops(part)
        arrived(hops[2])
        sent(hops[2])
        kept_p[:, one_p] += r3ap[part % 2].astype(F32)
        kept_p[:, two_p] += r3bp[part % 2].astype(F32)
        for zz in range(nz):
            s4p[part, zz] = kept_p[zz * blk : (zz + 1) * blk].astype(BF)
        fin_p[part] = kept_p[pl.ds(pl.multiple_of(z * blk, blk), blk)]
        down = kept_p[up_rows:]
        keep_d[part] = down
        s5d[part] = down.astype(BF)
        start(hops[3])

    down_hops = [
        hop(
            s5d.at[z_peer(step)], r5d.at[step - 1], DOWN + step - 1, dev(y, c, z_peer(step), x)
        )
        for step in range(1, nz)
    ]

    def ffn_part(part, carry):
        cols = pl.ds(pl.multiple_of(part * part_n, part_n), part_n)
        arrived(spread_hops(part)[2])
        w_up = bu[:, :, :, :, :, cols].reshape(width, part_n)
        w_down = bd[:, :, part].reshape(part_n, width)

        def ffn_tile(tile):
            @pl.when((part == 0) & (tile == 1))
            def _():
                pass_on(3, 1)

            @pl.when((part > 0) & (tile == 1))
            def _():
                part_second(part - 1)

            rows = pl.ds(pl.multiple_of(tile * ffn_rows, ffn_rows), ffn_rows)
            for piece in range(ffn_rows // TILE):
                some = tile_rows(tile * (ffn_rows // TILE) + piece)
                up = mm(h2_s[some, :], w_up)
                square = up * up
                bent = jnp.tanh(up * (gelu_in + (gelu_in * gelu_cube) * square))
                half = 0.5 + 0.5 * bent
                act_s[some, :] = (up * half).astype(BF)
                rate = half + (up * (1.0 - bent * bent)) * (
                    0.5 * gelu_in + (1.5 * gelu_in * gelu_cube) * square
                )
                dup_s[some, :] = (mm(dy_ref[some, :], w_down, NT) * rate).astype(BF)
            yacc[rows, :] += mm(act_s[rows, :], w_down)
            dx_ref[rows, :] += mm(dup_s[rows, :], w_up, NT)

        each(rows_all // ffn_rows, ffn_tile)

        @pl.when(part > 1)
        def _():
            part_fourth(part - 2)

        gq[:, :, :, :, :, 0:part_n] = mm(dyt_s[...], act_s[...]).reshape(go.shape)
        go[...] = mm(ht_s[...], dup_s[...]).reshape(go.shape)

        @pl.when(part > 0)
        def _():
            part_third(part - 1)

        part_first(part)
        return carry

    lax.fori_loop(0, nz, ffn_part, 0)

    def ffn_close(tile):
        if tile == 2:
            part_second(nz - 1)
        if tile == 3:
            part_fourth(nz - 2)
        rows = tile_rows(tile)
        _, hat, scale = second_norm(rows)
        dh2 = dx_ref[rows, :]
        nacc[2] += fold_rows(dh2 * hat)
        nacc[3] += fold_rows(dh2)
        dx1 = dy_ref[rows, :].astype(F32) + norm_back(dh2 * nrow[2:3, :], hat, scale)
        dy_ref[rows, :] = yacc[rows, :].astype(BF)
        dx_ref[rows, :] = dx1
        dz = dx1.astype(BF)
        act_s[rows, :] = dz
        ht_s[:, rows] = mix[rows, :].astype(F32).T.astype(BF)
        mix[rows, :] = mm(dz, w_out, NT).astype(BF)

    flat(tiles, ffn_close)
    keep_act.start()
    for part in range(nz):
        for group in spread_hops(part):
            sent(group)
    go[...] = mm(ht_s[...], act_s[...]).reshape(go.shape)

    def reduce_steps(full, cols, s1, r1, s2a, s2b, r2a, r2b, r3a, r3b, s3, r4, fin, base):
        full = full.at[:, :, :, :, :, cols]
        own = full.at[:, c]
        n = s1.shape[4]
        cut = (n // 2) // LANES * LANES
        one, two = pl.ds(0, cut), pl.ds(cut, n - cut)
        hop1 = [hop(s1, r1, base, twin)]
        hop2 = [
            hop(s1.at[1 - y, :, :, :, one], r2a, base + 1, over_y),
            hop(s1.at[:, :, 1 - x, :, two], r2b, base + 2, over_x),
        ]
        hop3 = [
            hop(s2a.at[:, 1 - x], r3a, base + 3, over_x),
            hop(s2b.at[1 - y], r3b, base + 4, over_y),
        ]
        hop4 = [
            hop(
                s3.at[z_peer(step)], r4.at[step - 1], base + 4 + step,
                dev(y, c, z_peer(step), x),
            )
            for step in range(1, nz)
        ]

        def places(index):
            return index // (nz * nx), (index // nx) % nz, index % nx

        def stage1():
            def load(index):
                yy, zz, xx = places(index)
                s1[yy, zz, xx] = full[yy, 1 - c, zz, xx].astype(BF)

            each(ny * nz * nx, load)
            start(hop1)

        def stage2():
            arrived(hop1)
            sent(hop1)

            def add(index):
                yy, zz, xx = places(index)
                total = own[yy, zz, xx] + r1[yy, zz, xx].astype(F32)
                own[yy, zz, xx] = total
                s1[yy, zz, xx] = total.astype(BF)

            each(ny * nz * nx, add)
            start(hop2)

        def stage3():
            arrived(hop2)
            for zz in range(nz):
                for xx in range(nx):
                    total = own[y, zz, xx, :, one] + r2a[zz, xx].astype(F32)
                    own[y, zz, xx, :, one] = total
                    s2a[zz, xx] = total.astype(BF)
            start(hop3[0:1])
            for yy in range(ny):
                for zz in range(nz):
                    total = own[yy, zz, x, :, two] + r2b[yy, zz].astype(F32)
                    own[yy, zz, x, :, two] = total
                    s2b[yy, zz] = total.astype(BF)
            start(hop3[1:2])

        def stage4():
            arrived(hop3)
            for zz in range(nz):
                total = own[y, zz, x, :, one] + r3a[zz].astype(F32)
                own[y, zz, x, :, one] = total
                s3[zz, :, one] = total.astype(BF)
                total = own[y, zz, x, :, two] + r3b[zz].astype(F32)
                own[y, zz, x, :, two] = total
                s3[zz, :, two] = total.astype(BF)
            start(hop4)

        def stage5():
            arrived(hop4)
            total = own[y, z, x]
            for step in range(nz - 1):
                total = total + r4[step].astype(F32)
            fin[:, cols] = total
            sent(hop2)
            sent(hop3)
            sent(hop4)

        return stage1, stage2, stage3, stage4, stage5

    cols_q, cols_kv = pl.ds(0, width), pl.ds(width, 2 * width)
    red_o = reduce_steps(
        go, cols_q, bu.at[:, 0, :, :, :, cols_q], r1o, s2ao, s2bo, r2ao, r2bo, r3ao, r3bo, s3o,
        r4o, fin_o, OUTER,
    )
    red_q = reduce_steps(
        gq, cols_q, bu.at[:, 1, :, :, :, cols_q], r1q, s2aq, s2bq, r2aq, r2bq, r3aq, r3bq,
        s3q, r4q, fin_q, INNER,
    )
    red_kv = reduce_steps(
        gq, cols_kv, bu.at[:, 1, :, :, :, cols_kv], r1k, s2ak, s2bk, r2ak, r2bk, r3ak, r3bk,
        s3k, r4k, fin_q, INNER + 8,
    )
    red_o[0]()

    def last_third():
        part_third(nz - 1)

    def fourth_and_down():
        part_fourth(nz - 1)
        start(down_hops)

    def attend_back(item):
        for at, step in (
            (0, red_o[1]), (1, last_third), (3, fourth_and_down), (4, red_o[2]), (7, red_o[3])
        ):

            @pl.when(item == at)
            def _(step=step):
                step()

        far_rows = far_of(item)
        dshares = []
        for sub, pair in units:
            rows = rows_of(item, sub)
            vv = both(rows, far_rows, cols_of(2, pair))
            dshares.append(mm(vv, by_head(mix[rows, cols_of(0, pair)], grad_a, grad_b), NT))
        far_k, far_v = [0.0] * pairs, [0.0] * pairs
        for (sub, pair), dshare in zip(units, dshares):
            rows, at = rows_of(item, sub), item * spans_here + sub
            share = prob[at, pair]
            dv = mm(share, by_head(mix[rows, cols_of(0, pair)], grad_a, grad_b))
            qkv[rows, cols_of(2, pair)] = dv[0:SPAN].astype(BF)
            far_v[pair] = far_v[pair] + dv[SPAN:]
            share = share.astype(F32)
            inner = jnp.sum(share * dshare, axis=0, keepdims=True)
            prob[at, pair] = (share * (dshare - inner)).astype(BF)
        for sub in range(spans_here):
            rows = rows_of(item, sub)
            dqs = []
            for pair in range(pairs):
                dscore = prob[item * spans_here + sub, pair]
                stacked = mm(both(rows, far_rows, cols_of(1, pair)), dscore, TN)
                dqs += [stacked[0:HEAD_DIM, 0:SPAN], stacked[HEAD_DIM:, SPAN:]]
                dk = mm(dscore, by_head(qkv[rows, cols_of(0, pair)], query_a, query_b))
                qkv[rows, cols_of(1, pair)] = dk[0:SPAN].astype(BF)
                far_k[pair] = far_k[pair] + dk[SPAN:]
            dq = jnp.concatenate(dqs, axis=0).T * score_scale
            qkv[rows, 0:width] = dq.astype(BF)
        for pair in range(pairs):
            pool_grad[far_rows, cols_of(0, pair)] = far_k[pair]
            pool_grad[far_rows, cols_of(1, pair)] = far_v[pair]

    each(items, attend_back)

    back_row = lax.broadcasted_iota(jnp.int32, (far_n, far_n), 0)
    back_col = lax.broadcasted_iota(jnp.int32, (far_n, far_n), 1)
    owner, place = back_row // blocks, back_row % blocks
    source = (place // spans_here) * spans_all + owner * spans_here + place % spans_here
    reorder = jnp.where(source == back_col, 1.0, 0.0).astype(BF)
    pool_send[...] = (
        mm(reorder, pool_grad[...].astype(BF)).astype(BF).reshape(seq_n, blocks, 2 * width)
    )
    back_hops = [
        hop(
            pool_send.at[seq_peer(step)], pool_recv.at[step - 1], POOLBACK + step - 1,
            (dp_i, seq_peer(step)),
        )
        for step in range(1, seq_n)
    ]
    start(back_hops)

    live_sum[...] = jnp.zeros_like(live_sum)

    def turn_h1(tile):
        rows = tile_rows(tile)
        _, _, h1 = first_norm(rows)
        ht_s[:, rows] = h1.astype(F32).T.astype(BF)
        live_sum[...] += mm(live_pick(tile), h1)

    each(tiles, turn_h1)
    for part in range(3):
        cols = pl.ds(part * width, width)
        gq[:, :, :, :, :, cols] = mm(ht_s[...], qkv[:, cols]).reshape(
            ny, nc, nz, nx, blk, width
        )
        if part == 0:
            red_q[0]()
    red_q[1]()
    arrived(back_hops)
    pool_total = pool_send[sq_i].astype(F32)
    for step in range(seq_n - 1):
        pool_total = pool_total + pool_recv[step].astype(F32)
    far = pool_total / count_col
    far_hi = far.astype(BF)
    far_lo = (far - far_hi.astype(F32)).astype(BF)
    near = live_sum[...]
    near_hi = near.astype(BF)
    near_lo = (near - near_hi.astype(F32)).astype(BF)
    left = jnp.concatenate([near_hi, near_lo, near_hi], axis=0)
    right = jnp.concatenate([far_hi, far_hi, far_lo], axis=0)
    for part in range(2):
        cols = pl.ds((part + 1) * width, width)
        gq[:, :, :, :, :, cols] += mm(left, right[:, part * width : (part + 1) * width], TN).reshape(
            ny, nc, nz, nx, blk, width
        )
    red_kv[0]()
    far_two = jnp.concatenate([far_hi, far_lo], axis=0)
    both_far = mm(far_two[:, 0:width], w_qkv(1), NT) + mm(far_two[:, width:], w_qkv(2), NT)
    spread_w[...] = both_far[0:blocks] + both_far[blocks:]

    def last_tile(tile):
        @pl.when(tile == 1)
        def _():
            red_kv[1]()

        @pl.when(tile == 2)
        def _():
            red_q[2]()

        rows = tile_rows(tile)
        hat, scale, _ = first_norm(rows)
        extra = []
        for part in range(per_tile):
            block = tile * per_tile + part
            pos = (
                sq_i * local_len
                + lax.rem(block, spans_here) * SPAN
                + lax.broadcasted_iota(jnp.int32, (SPAN, 1), 0)
            )
            live = jnp.where(pos < len_ref[block // spans_here], 1.0, 0.0)
            extra.append(live * spread_w[pl.ds(block, 1), :])
        dh1 = jnp.concatenate(extra, axis=0)
        for part in range(3):
            dh1 = dh1 + mm(qkv[rows, pl.ds(part * width, width)], w_qkv(part), NT)
        nacc[0] += fold_rows(dh1 * hat)
        nacc[1] += fold_rows(dh1)
        dx_ref[rows, :] += norm_back(dh1 * nrow[0:1, :], hat, scale)

    each(tiles, last_tile)
    keep_dx.start()
    norm_rows = [jnp.sum(nacc[k], axis=0, keepdims=True) for k in range(4)]
    norm_rows.append(jnp.zeros((4, width), F32))
    norm_seq[sq_i] = jnp.concatenate(norm_rows, axis=0)
    norm_hops = [
        hop(norm_seq.at[sq_i], norm_seq.at[sq_i], NORM_SEQ + step - 1, (dp_i, seq_peer(step)))
        for step in range(1, seq_n)
    ]
    norm_hops_dp = [
        hop(norm_dp.at[dp_i], norm_dp.at[dp_i], NORM_DP + step - 1, (dp_peer(step), sq_i))
        for step in range(1, dp_n)
    ]
    start(norm_hops)
    red_kv[2]()
    red_q[3]()
    for part in range(nz):
        arrived(part_hops(part)[3])
        total = fin_p[part]
        for step in range(nz - 1):
            total = total + r4p[step, part].astype(F32)
        for group in range(dp_n):
            at = (group * nz + part) * LANES
            fin_u[:, at : at + LANES] = total[:, group * LANES : (group + 1) * LANES]
    arrived(down_hops)
    total = keep_d[z]
    for step in range(nz - 1):
        total = total + r5d[step].astype(F32)
    fin_d[...] = total
    red_o[4]()

    arrived(norm_hops)
    total = norm_seq[0]
    for k in range(1, seq_n):
        total = total + norm_seq[k]
    norm_dp[dp_i] = total
    start(norm_hops_dp)
    red_kv[3]()
    red_q[4]()

    def partial(values_in):
        squares = fold_rows(values_in * values_in)
        return sum(
            squares[:, k * LANES : (k + 1) * LANES] for k in range(squares.shape[1] // LANES)
        )

    early = partial(fin_u[...]) + partial(fin_d[...]) + partial(fin_o[...])
    red_kv[4]()
    psq[sq_i] = early + partial(fin_q[...])
    seq_hops = [
        hop(psq.at[sq_i], psq.at[sq_i], SQUARE_SEQ + step - 1, (dp_i, seq_peer(step)))
        for step in range(1, seq_n)
    ]
    start(seq_hops)
    sent(back_hops)
    for part in range(nz):
        sent(part_hops(part)[3])
    sent(down_hops)
    sent(norm_hops)
    arrived(norm_hops_dp)
    sent(norm_hops_dp)
    total = norm_dp[0]
    for k in range(1, dp_n):
        total = total + norm_dp[k]
    norm_sum[...] = total
    arrived(seq_hops)
    total = psq[0]
    for k in range(1, seq_n):
        total = total + psq[k]
    psd[dp_i] = total
    dp_hops = [
        hop(psd.at[dp_i], psd.at[dp_i], SQUARE_DP + step - 1, (dp_peer(step), sq_i))
        for step in range(1, dp_n)
    ]
    start(dp_hops)
    arrived(dp_hops)
    total = psd[0]
    for k in range(1, dp_n):
        total = total + psd[k]
    total_ref[...] = total
    sent(seq_hops)
    sent(dp_hops)
    keep_act.wait()
    keep_dx.wait()


def update_kernel(
    act_in, dx_in, total_ref, gq_ref, go_ref, gu_ref, gd_ref, gn_ref,
    wq_ref, wo_ref, wu_ref, wd_ref, wn_ref, fq_ref, fo_ref, fu_ref, fd_ref, fn_ref,
    sq_ref, so_ref, su_ref, sd_ref, sn_ref,
    act_out, dx_out, norm_ref, nq, nfq, nsq, no, nfo, nso, nu, nfu, nsu, nd, nfd, nsd,
    nn, nfn, nsn, act_s, dx_s, sems_in, sems_out,
):
    pieces = 2
    piece = act_s.shape[0] // pieces
    moves = []
    for k in range(pieces):
        rows = pl.ds(k * piece, piece)
        for n, (src, mid, dst) in enumerate(
            ((dx_in, dx_s, dx_out), (act_in, act_s, act_out))
        ):
            moves.append((
                pltpu.make_async_copy(src.at[rows], mid.at[rows], sems_in.at[n * pieces + k]),
                pltpu.make_async_copy(mid.at[rows], dst.at[rows], sems_out.at[n * pieces + k]),
            ))
    for inward, _ in moves:
        inward.start()
    norm_grads = gn_ref[...]
    total = jnp.sum(total_ref[...]) + jnp.sum(norm_grads * norm_grads)
    total = jnp.full((1, 1), total, F32)
    grad_norm = jnp.sqrt(total)
    factor = clip_bound / jnp.maximum(grad_norm, clip_bound)
    norm_ref[...] = grad_norm

    def update(weight, grad_in, first, second, outs, rate, decay):
        new = adamw_update(weight, grad_in, first, second, factor, rate, decay)
        for out, value in zip(outs, new):
            out[...] = value

    for inward, outward in moves:
        inward.wait()
        outward.start()
    for w, g, m, s, outs in (
        (wq_ref, gq_ref, fq_ref, sq_ref, (nq, nfq, nsq)),
        (wo_ref, go_ref, fo_ref, so_ref, (no, nfo, nso)),
        (wu_ref, gu_ref, fu_ref, su_ref, (nu, nfu, nsu)),
        (wd_ref, gd_ref, fd_ref, sd_ref, (nd, nfd, nsd)),
    ):
        update(w[...], g[...], m[...], s[...], outs, rate_matrix, decay_coef)
    count, cols = wn_ref.shape
    width = norm_grads.shape[1]
    place = (lax.axis_index("dp") * lax.axis_size("seq") + lax.axis_index("seq")) * cols
    turned = pltpu.roll(norm_grads, lax.rem(width - place, width), 1)
    update(
        wn_ref[...], turned[0:count, 0:cols], fn_ref[...], sn_ref[...], (nn, nfn, nsn),
        rate_norm, 0.0,
    )
    for _, outward in moves:
        outward.wait()


def fused_device(
    tokens, cotangent, lengths, w_qkv, w_out, w_up, w_down, norm_params,
    first_qkv, first_out, first_up, first_down, first_norm,
    second_qkv, second_out, second_up, second_down, second_norm,
):
    item_count, local_len, width = tokens.shape
    rows_all = item_count * local_len
    dp_n, seq_n = lax.axis_size("dp"), lax.axis_size("seq")
    nc = 2
    ny = dp_n // nc
    nx = ny
    nz = seq_n // nx
    blk, width3 = w_qkv.shape
    ff = w_up.shape[1]
    dblk = w_down.shape[0]
    blocks = rows_all // SPAN
    far_n = seq_n * blocks
    keys_n = SPAN + local_len // SPAN * seq_n
    part_n = ff // nz
    up_rows = nz * blk
    half = width // 2

    def bufs(b, n):
        cut = (n // 2) // LANES * LANES
        rest = n - cut
        taken = [pltpu.VMEM((nz, nx, b, cut), BF), pltpu.VMEM((ny, nz, b, rest), BF)]
        return [
            *taken,
            pltpu.VMEM((nz, b, n), BF),
            pltpu.VMEM((ny, nz, nx, b, n), BF),
            *taken,
            pltpu.VMEM((nz, b, cut), BF),
            pltpu.VMEM((nz, b, rest), BF),
            pltpu.VMEM((nz - 1, b, n), BF),
        ]

    whole = pl.BlockSpec(memory_space=pltpu.VMEM)
    outside = pl.BlockSpec(memory_space=pl.ANY)
    part_rows = up_rows + dblk
    outs = pl.pallas_call(
        layer_kernel,
        out_shape=[
            jax.ShapeDtypeStruct((rows_all, width), BF),
            jax.ShapeDtypeStruct((rows_all, width), F32),
            jax.ShapeDtypeStruct(w_qkv.shape, F32),
            jax.ShapeDtypeStruct(w_out.shape, F32),
            jax.ShapeDtypeStruct(w_up.shape, F32),
            jax.ShapeDtypeStruct(w_down.shape, F32),
            jax.ShapeDtypeStruct((8, width), F32),
            jax.ShapeDtypeStruct((8, LANES), F32),
        ],
        in_specs=[pl.BlockSpec(memory_space=pltpu.SMEM), outside, outside] + [whole] * 5,
        out_specs=[outside, outside] + [whole] * 6,
        scratch_shapes=[
            pltpu.VMEM((ny, nc, nz, nx, blk, 2 * width + LANES), BF),
            pltpu.VMEM((ny, nc, nz, nx, blk, 2 * width), BF),
            pltpu.VMEM((ny, nc, nz, nx, blk, ff), BF),
            pltpu.VMEM((ny, nc, nz, nx, dblk, width), BF),
            pltpu.VMEM((rows_all, width3), BF),
            pltpu.VMEM((rows_all, width), BF),
            pltpu.VMEM((blocks, width // LANES, keys_n, 2 * SPAN), BF),
            pltpu.VMEM((ny, nc, nz, nx, blk, width3), F32),
            pltpu.VMEM((ny, nc, nz, nx, blk, width), F32),
            pltpu.VMEM((rows_all, width), F32),
            pltpu.VMEM((rows_all, width), BF),
            pltpu.VMEM((width, rows_all), BF),
            pltpu.VMEM((width, rows_all), BF),
            pltpu.VMEM((rows_all, part_n), BF),
            pltpu.VMEM((rows_all, part_n), BF),
            pltpu.VMEM((ny, nx, part_rows, width), F32),
            pltpu.VMEM((part_rows, width), F32),
            pltpu.VMEM((ny, nx, part_rows, width), BF),
            pltpu.VMEM((2, ny, nx, part_rows, width), BF),
            pltpu.VMEM((nx, part_rows, half), BF),
            pltpu.VMEM((ny, part_rows, half), BF),
            pltpu.VMEM((2, nx, part_rows, half), BF),
            pltpu.VMEM((2, ny, part_rows, half), BF),
            pltpu.VMEM((2, part_rows, half), BF),
            pltpu.VMEM((2, part_rows, half), BF),
            pltpu.VMEM((nz, nz, blk, width), BF),
            pltpu.VMEM((nz - 1, nz, blk, width), BF),
            pltpu.VMEM((nz, blk, width), F32),
            pltpu.VMEM((nz, dblk, width), F32),
            pltpu.VMEM((nz, dblk, width), BF),
            pltpu.VMEM((nz - 1, dblk, width), BF),
            *bufs(blk, width),
            *bufs(blk, 2 * width),
            *bufs(blk, width),
            pltpu.VMEM((seq_n, blocks, 2 * width), BF),
            pltpu.VMEM((far_n, 2 * width), BF),
            pltpu.VMEM((far_n, 2 * width), F32),
            pltpu.VMEM((seq_n, blocks, 2 * width), BF),
            pltpu.VMEM((seq_n - 1, blocks, 2 * width), BF),
            pltpu.VMEM((blocks, width), F32),
            pltpu.VMEM((blocks, width), F32),
            pltpu.VMEM((8, width), F32),
            pltpu.VMEM((4, 8, width), F32),
            pltpu.VMEM((LANES, LANES), F32),
            pltpu.VMEM((seq_n, 8, width), F32),
            pltpu.VMEM((dp_n, 8, width), F32),
            pltpu.VMEM((seq_n, 8, LANES), F32),
            pltpu.VMEM((dp_n, 8, LANES), F32),
            pltpu.VMEM((rows_all, width), BF),
            pltpu.VMEM((rows_all, width), BF),
            pltpu.VMEM((rows_all, width), F32),
            pltpu.SemaphoreType.DMA((COPIES,)),
            pltpu.SemaphoreType.DMA((COPIES,)),
            pltpu.SemaphoreType.DMA((4,)),
        ],
        compiler_params=pltpu.CompilerParams(
            collective_id=0, has_side_effects=True, vmem_limit_bytes=64 * 1024 * 1024 - 65536
        ),
    )(
        lengths,
        tokens.reshape(rows_all, width),
        cotangent.reshape(rows_all, width),
        w_qkv, w_out, w_up, w_down, norm_params,
    )
    weights = (w_qkv, w_out, w_up, w_down, norm_params)
    new = pl.pallas_call(
        update_kernel,
        out_shape=[
            jax.ShapeDtypeStruct((rows_all, width), BF),
            jax.ShapeDtypeStruct((rows_all, width), F32),
            jax.ShapeDtypeStruct((1, 1), F32),
            *(jax.ShapeDtypeStruct(w.shape, F32) for w in weights for _ in range(3)),
        ],
        in_specs=[outside, outside] + [whole] * 21,
        out_specs=[outside, outside] + [whole] * 16,
        scratch_shapes=[
            pltpu.VMEM((rows_all, width), BF),
            pltpu.VMEM((rows_all, width), F32),
            pltpu.SemaphoreType.DMA((4,)),
            pltpu.SemaphoreType.DMA((4,)),
        ],
        compiler_params=pltpu.CompilerParams(vmem_limit_bytes=64 * 1024 * 1024 - 65536),
    )(
        outs[0], outs[1], outs[7], *outs[2:7], *weights,
        first_qkv, first_out, first_up, first_down, first_norm,
        second_qkv, second_out, second_up, second_down, second_norm,
    )
    return (
        new[0].reshape(tokens.shape), new[1].reshape(tokens.shape), new[2].reshape(()),
        *new[3:],
    )


def solution(mesh):
    placed = (
        P("dp", "seq", None),
        P("dp", "seq", None),
        P("dp"),
        P(("dp", "seq"), None),
        P(("dp", "seq"), None),
        P(("dp", "seq"), None),
        P(("dp", "seq"), None),
        P(None, ("dp", "seq")),
        P(("dp", "seq"), None),
        P(("dp", "seq"), None),
        P(("dp", "seq"), None),
        P(("dp", "seq"), None),
        P(None, ("dp", "seq")),
        P(("dp", "seq"), None),
        P(("dp", "seq"), None),
        P(("dp", "seq"), None),
        P(("dp", "seq"), None),
        P(None, ("dp", "seq")),
    )
    dp_n, seq_n = mesh.shape["dp"], mesh.shape["seq"]
    fits = dp_n == 4 and seq_n % 2 == 0 and WIDTH // (dp_n * seq_n) == 16
    return jax.shard_map(
        fused_device if fits else generic_device,
        mesh=mesh,
        in_specs=placed,
        out_specs=(
            P("dp", "seq", None),
            P("dp", "seq", None),
            P(),
            P(("dp", "seq"), None),
            P(("dp", "seq"), None),
            P(("dp", "seq"), None),
            P(("dp", "seq"), None),
            P(("dp", "seq"), None),
            P(("dp", "seq"), None),
            P(("dp", "seq"), None),
            P(("dp", "seq"), None),
            P(("dp", "seq"), None),
            P(("dp", "seq"), None),
            P(("dp", "seq"), None),
            P(("dp", "seq"), None),
            P(None, ("dp", "seq")),
            P(None, ("dp", "seq")),
            P(None, ("dp", "seq")),
        ),
        check_vma=False,
    )
```

```python
import functools
import math

import jax
import jax.numpy as jnp
from jax import lax
from jax.experimental import pallas as pl
from jax.experimental.pallas import tpu as pltpu
from jax.sharding import PartitionSpec as P

HEADS = 8
HEAD_DIM = 64
SPAN = 128
STEP = 10
WIDTH = 512


eps_norm = 1e-05
neg_fill = -1e30
beta_one = 0.9
beta_two = 0.999
adam_eps = 1e-08
decay_coef = 0.1
rate_matrix = 0.05
rate_norm = 0.5
clip_bound = 1.0


def normalize(values_in, gain_row, shift_row):
    center = values_in - jnp.mean(values_in, axis=-1, keepdims=True)
    spread = jnp.mean(center * center, axis=-1, keepdims=True)
    return center * lax.rsqrt(spread + eps_norm) * gain_row + shift_row


def adamw_update(weight, grad_in, first_old, second_old, factor, step_rate, weight_decay):
    clipped = grad_in * factor
    first_new = beta_one * first_old + (1.0 - beta_one) * clipped
    second_new = beta_two * second_old + (1.0 - beta_two) * clipped * clipped
    first_hat = first_new / (1.0 - beta_one**STEP)
    second_hat = second_new / (1.0 - beta_two**STEP)
    weight_new = weight - step_rate * (
        first_hat / (jnp.sqrt(second_hat) + adam_eps) + weight_decay * weight
    )
    return (weight_new, first_new, second_new)


def generic_device(
    tokens,
    cotangent,
    lengths,
    w_qkv,
    w_out,
    w_up,
    w_down,
    norm_params,
    first_qkv,
    first_out,
    first_up,
    first_down,
    first_norm,
    second_qkv,
    second_out,
    second_up,
    second_down,
    second_norm,
):
    item_count, local_len, model_width = tokens.shape
    row_count = item_count * local_len
    spans_here = local_len // SPAN
    spans_all = spans_here * lax.axis_size("seq")
    seq_rank = lax.axis_index("seq")
    score_scale = HEAD_DIM ** (-0.5)
    full_qkv, full_out, full_up, full_down, full_norm = (
        lax.all_gather(w_qkv.astype(jnp.bfloat16), ("dp", "seq"), axis=0, tiled=True),
        lax.all_gather(w_out.astype(jnp.bfloat16), ("dp", "seq"), axis=0, tiled=True),
        lax.all_gather(w_up.astype(jnp.bfloat16), ("dp", "seq"), axis=0, tiled=True),
        lax.all_gather(w_down.astype(jnp.bfloat16), ("dp", "seq"), axis=0, tiled=True),
        lax.all_gather(norm_params.astype(jnp.bfloat16), ("dp", "seq"), axis=1, tiled=True),
    )
    norm_rows = full_norm.astype(jnp.float32)
    tokens_f = tokens.reshape(row_count, model_width).astype(jnp.float32)
    normed, back_one = jax.vjp(normalize, tokens_f, norm_rows[0], norm_rows[1])
    normed_b = normed.astype(jnp.bfloat16)
    qkv_b = jnp.dot(normed_b, full_qkv, preferred_element_type=jnp.float32).astype(jnp.bfloat16)
    qkv_view = qkv_b.reshape(item_count, spans_here, SPAN, 3, HEADS, HEAD_DIM)
    query_part = qkv_view[:, :, :, 0]
    key_part = qkv_view[:, :, :, 1]
    value_part = qkv_view[:, :, :, 2]
    local_pos = seq_rank * local_len + jnp.arange(local_len, dtype=jnp.int32)
    live_mask = (local_pos[None, :] < lengths[:, None]).reshape(item_count, spans_here, SPAN)
    live_f = live_mask.astype(jnp.float32)
    counts_here = jnp.maximum(jnp.sum(live_f, axis=2), 1.0)
    pooled = jnp.einsum(
        "ist,istchd->ischd",
        live_mask.astype(jnp.bfloat16),
        qkv_view[:, :, :, 1:],
        preferred_element_type=jnp.float32,
    )
    pooled = (pooled / counts_here[:, :, None, None, None]).astype(jnp.bfloat16)
    pooled_all = lax.all_gather(pooled, "seq", axis=1, tiled=True)
    pooled_keys = pooled_all[:, :, 0]
    pooled_values = pooled_all[:, :, 1]
    all_pos = jnp.arange(spans_all * SPAN, dtype=jnp.int32).reshape(spans_all, SPAN)
    counts_all = jnp.sum((all_pos[None] < lengths[:, None, None]).astype(jnp.float32), axis=2)
    span_ids = seq_rank * spans_here + jnp.arange(spans_here, dtype=jnp.int32)
    far_valid = (counts_all[:, None, :] > 0.0) & (
        span_ids[None, :, None] != jnp.arange(spans_all, dtype=jnp.int32)[None, None, :]
    )
    near_mask = live_mask[:, :, None, None, :]
    far_mask = far_valid[:, :, None, None, :]

    def scores_of():
        near_raw = (
            jnp.einsum(
                "isqhd,iskhd->ishqk", query_part, key_part, preferred_element_type=jnp.float32
            )
            * score_scale
        )
        far_raw = (
            jnp.einsum(
                "isqhd,irhd->ishqr", query_part, pooled_keys, preferred_element_type=jnp.float32
            )
            * score_scale
        )
        return (jnp.where(near_mask, near_raw, neg_fill), jnp.where(far_mask, far_raw, neg_fill))

    near_s, far_s = scores_of()
    score_top = jnp.maximum(
        jnp.max(near_s, axis=-1, keepdims=True), jnp.max(far_s, axis=-1, keepdims=True)
    )
    exp_total = jnp.sum(jnp.exp(near_s - score_top), axis=-1, keepdims=True) + jnp.sum(
        jnp.exp(far_s - score_top), axis=-1, keepdims=True
    )
    log_total = score_top + jnp.log(exp_total)
    near_pb = jnp.exp(near_s - log_total).astype(jnp.bfloat16)
    far_pb = jnp.exp(far_s - log_total).astype(jnp.bfloat16)
    mixed_rows = jnp.einsum(
        "ishqk,iskhd->isqhd", near_pb, value_part, preferred_element_type=jnp.float32
    )
    mixed_rows = mixed_rows + jnp.einsum(
        "ishqr,irhd->isqhd", far_pb, pooled_values, preferred_element_type=jnp.float32
    )
    mixed_b = mixed_rows.reshape(row_count, model_width).astype(jnp.bfloat16)
    residual = tokens_f + jnp.dot(mixed_b, full_out, preferred_element_type=jnp.float32)
    normed_two, back_two = jax.vjp(normalize, residual, norm_rows[2], norm_rows[3])
    normed_two_b = normed_two.astype(jnp.bfloat16)
    up_pre = jnp.dot(normed_two_b, full_up, preferred_element_type=jnp.float32)
    gated, gelu_back = jax.vjp(jax.nn.gelu, up_pre)
    gated_b = gated.astype(jnp.bfloat16)
    layer_out = residual + jnp.dot(gated_b, full_down, preferred_element_type=jnp.float32)
    activations = layer_out.astype(jnp.bfloat16).reshape(item_count, local_len, model_width)
    grad_out_b = cotangent.reshape(row_count, model_width)
    grad_down = jnp.dot(gated_b.T, grad_out_b, preferred_element_type=jnp.float32)
    grad_gated = jnp.dot(grad_out_b, full_down.T, preferred_element_type=jnp.float32)
    grad_up_pre = gelu_back(grad_gated)[0].astype(jnp.bfloat16)
    grad_up = jnp.dot(normed_two_b.T, grad_up_pre, preferred_element_type=jnp.float32)
    grad_normed_two = jnp.dot(grad_up_pre, full_up.T, preferred_element_type=jnp.float32)
    grad_resid_ln, grad_gain_two, grad_shift_two = back_two(grad_normed_two)
    grad_resid = grad_out_b.astype(jnp.float32) + grad_resid_ln
    grad_attn_b = grad_resid.astype(jnp.bfloat16)
    grad_out_proj = jnp.dot(mixed_b.T, grad_attn_b, preferred_element_type=jnp.float32)
    grad_mixed = jnp.dot(grad_attn_b, full_out.T, preferred_element_type=jnp.float32).astype(
        jnp.bfloat16
    )
    grad_mixed = grad_mixed.reshape(item_count, spans_here, SPAN, HEADS, HEAD_DIM)
    near_s, far_s = scores_of()
    near_pf = jnp.exp(near_s - log_total)
    far_pf = jnp.exp(far_s - log_total)
    near_pb = near_pf.astype(jnp.bfloat16)
    far_pb = far_pf.astype(jnp.bfloat16)
    grad_near = jnp.einsum(
        "isqhd,iskhd->ishqk", grad_mixed, value_part, preferred_element_type=jnp.float32
    )
    grad_far = jnp.einsum(
        "isqhd,irhd->ishqr", grad_mixed, pooled_values, preferred_element_type=jnp.float32
    )
    row_delta = jnp.sum(near_pf * grad_near, axis=-1, keepdims=True) + jnp.sum(
        far_pf * grad_far, axis=-1, keepdims=True
    )
    dscore_near = (near_pf * (grad_near - row_delta)).astype(jnp.bfloat16)
    dscore_far = (far_pf * (grad_far - row_delta)).astype(jnp.bfloat16)
    grad_query = jnp.einsum(
        "ishqk,iskhd->isqhd", dscore_near, key_part, preferred_element_type=jnp.float32
    )
    grad_query = (
        grad_query
        + jnp.einsum(
            "ishqr,irhd->isqhd", dscore_far, pooled_keys, preferred_element_type=jnp.float32
        )
    ) * score_scale
    grad_keys = (
        jnp.einsum(
            "ishqk,isqhd->iskhd", dscore_near, query_part, preferred_element_type=jnp.float32
        )
        * score_scale
    )
    grad_values = jnp.einsum(
        "ishqk,isqhd->iskhd", near_pb, grad_mixed, preferred_element_type=jnp.float32
    )
    grad_pool_keys = (
        jnp.einsum("ishqr,isqhd->irhd", dscore_far, query_part, preferred_element_type=jnp.float32)
        * score_scale
    )
    grad_pool_values = jnp.einsum(
        "ishqr,isqhd->irhd", far_pb, grad_mixed, preferred_element_type=jnp.float32
    )
    pool_grads = jnp.stack([grad_pool_keys, grad_pool_values], axis=2)
    pool_mine = lax.psum_scatter(
        pool_grads.astype(jnp.bfloat16), "seq", scatter_dimension=1, tiled=True
    ).astype(jnp.float32)
    spread_back = pool_mine / counts_here[:, :, None, None, None]
    grad_kv = (
        jnp.stack([grad_keys, grad_values], axis=3)
        + live_f[:, :, :, None, None, None] * spread_back[:, :, None]
    )
    grad_qkv_rows = jnp.concatenate([grad_query[:, :, :, None], grad_kv], axis=3)
    grad_qkv_b = grad_qkv_rows.reshape(row_count, 3 * model_width).astype(jnp.bfloat16)
    grad_qkv = jnp.dot(normed_b.T, grad_qkv_b, preferred_element_type=jnp.float32)
    grad_normed = jnp.dot(grad_qkv_b, full_qkv.T, preferred_element_type=jnp.float32)
    grad_in_ln, grad_gain_one, grad_shift_one = back_one(grad_normed)
    input_grad = (grad_resid + grad_in_ln).reshape(item_count, local_len, model_width)
    grad_norm_rows = jnp.stack([grad_gain_one, grad_shift_one, grad_gain_two, grad_shift_two])
    red_qkv, red_out, red_up, red_down, red_norm = (
        lax.psum_scatter(grad_qkv, ("dp", "seq"), scatter_dimension=0, tiled=True),
        lax.psum_scatter(grad_out_proj, ("dp", "seq"), scatter_dimension=0, tiled=True),
        lax.psum_scatter(grad_up, ("dp", "seq"), scatter_dimension=0, tiled=True),
        lax.psum_scatter(grad_down, ("dp", "seq"), scatter_dimension=0, tiled=True),
        lax.psum_scatter(grad_norm_rows, ("dp", "seq"), scatter_dimension=1, tiled=True),
    )
    squares = jnp.sum(red_qkv * red_qkv) + jnp.sum(red_out * red_out) + jnp.sum(red_up * red_up)
    squares = squares + jnp.sum(red_down * red_down) + jnp.sum(red_norm * red_norm)
    total_sq = lax.psum(squares, ("dp", "seq"))
    grad_norm = jnp.sqrt(total_sq)
    factor = clip_bound / jnp.maximum(grad_norm, clip_bound)
    new_qkv, new_first_qkv, new_second_qkv = adamw_update(
        w_qkv, red_qkv, first_qkv, second_qkv, factor, rate_matrix, decay_coef
    )
    new_out, new_first_out, new_second_out = adamw_update(
        w_out, red_out, first_out, second_out, factor, rate_matrix, decay_coef
    )
    new_up, new_first_up, new_second_up = adamw_update(
        w_up, red_up, first_up, second_up, factor, rate_matrix, decay_coef
    )
    new_down, new_first_down, new_second_down = adamw_update(
        w_down, red_down, first_down, second_down, factor, rate_matrix, decay_coef
    )
    new_norm, new_first_norm, new_second_norm = adamw_update(
        norm_params, red_norm, first_norm, second_norm, factor, rate_norm, 0.0
    )
    return (
        activations,
        input_grad,
        grad_norm,
        new_qkv,
        new_first_qkv,
        new_second_qkv,
        new_out,
        new_first_out,
        new_second_out,
        new_up,
        new_first_up,
        new_second_up,
        new_down,
        new_first_down,
        new_second_down,
        new_norm,
        new_first_norm,
        new_second_norm,
    )


BF = jnp.bfloat16
F32 = jnp.float32
MESH = pl.DeviceIdType.MESH
LANES = 128
TILE = 512
NN = (((1,), (0,)), ((), ()))
NT = (((1,), (1,)), ((), ()))
TN = (((0,), (0,)), ((), ()))
GATHER, SPREAD, PARTS, DOWN, OUTER, INNER, POOL, POOLBACK = 0, 22, 62, 94, 97, 105, 121, 128
NORM_SEQ, NORM_DP, SQUARE_SEQ, SQUARE_DP, COPIES = 135, 142, 145, 152, 155


def mm(left, right, dims=NN):
    return lax.dot_general(left, right, dims, preferred_element_type=F32)


def centered(values_in):
    center = values_in - jnp.mean(values_in, axis=-1, keepdims=True)
    scale = lax.rsqrt(jnp.mean(center * center, axis=-1, keepdims=True) + eps_norm)
    return center * scale, scale


def norm_back(grad_hat, hat, scale):
    mean_grad = jnp.mean(grad_hat, axis=-1, keepdims=True)
    mean_both = jnp.mean(grad_hat * hat, axis=-1, keepdims=True)
    return scale * (grad_hat - mean_grad - hat * mean_both)


def fold_rows(values_in):
    rows, width = values_in.shape
    return jnp.sum(values_in.reshape(rows // 8, 8, width), axis=0)


def layer_kernel(
    len_ref, x_any, dy_any, wq_ref, wo_ref, wu_ref, wd_ref, nrm_ref,
    act_any, dx_any, fin_q, fin_o, fin_u, fin_d, norm_sum, total_ref,
    bkv, bqo, bu, bd, qkv, mix, prob, gq, go, yacc, h2_s, ht_s, dyt_s, act_s, dup_s,
    own_p, kept_p, s1p, r1p, s2ap, s2bp, r2ap, r2bp, r3ap, r3bp, s4p, r4p, fin_p, keep_d, s5d, r5d,
    s2aq, s2bq, s3q, r1q, r2aq, r2bq, r3aq, r3bq, r4q,
    s2ak, s2bk, s3k, r1k, r2ak, r2bk, r3ak, r3bk, r4k,
    s2ao, s2bo, s3o, r1o, r2ao, r2bo, r3ao, r3bo, r4o,
    pool_all, pool_far, pool_grad, pool_send, pool_recv, live_sum, spread_w,
    nrow, nacc, ntall, norm_seq, norm_dp, psq, psd, x_ref, dy_ref, dx_ref,
    send_sem, recv_sem, local_sem,
):
    ny, nc, nz, nx, blk, _ = bu.shape
    dblk = bd.shape[4]
    rows_all, width = x_ref.shape
    width3 = 3 * width
    ff = wu_ref.shape[1]
    seq_n = nz * nx
    dp_n = ny * nc
    local_len = rows_all // len_ref.shape[0]
    spans_here = local_len // SPAN
    blocks = rows_all // SPAN
    spans_all = spans_here * seq_n
    tiles = rows_all // TILE
    per_tile = TILE // SPAN
    pairs = width // LANES
    part_n = ff // nz
    ffn_rows = 2 * TILE
    dp_i = lax.axis_index("dp")
    sq_i = lax.axis_index("seq")
    y, c = dp_i // nc, dp_i % nc
    z, x = sq_i // nx, sq_i % nx

    def dev(yy, cc, zz, xx):
        return (yy * nc + cc, zz * nx + xx)

    twin = dev(y, 1 - c, z, x)
    over_x = dev(y, c, z, 1 - x)
    over_y = dev(1 - y, c, z, x)

    def seq_peer(step):
        return lax.rem(sq_i + step, seq_n)

    def dp_peer(step):
        return lax.rem(dp_i + step, dp_n)

    def z_peer(step):
        return lax.rem(z + step, nz)

    def hop(src, dst, index, target):
        return pltpu.make_async_remote_copy(
            src_ref=src, dst_ref=dst, send_sem=send_sem.at[index],
            recv_sem=recv_sem.at[index], device_id=target, device_id_type=MESH,
        )

    def start(hops):
        for one in hops:
            one.start()

    def arrived(hops):
        for one in hops:
            one.wait_recv()

    def sent(hops):
        for one in hops:
            one.wait_send()

    def each(count, body):
        def step(index, carry):
            body(index)
            return carry

        lax.fori_loop(0, count, step, 0)

    def flat(count, body):
        for index in range(count):
            body(index)

    def tile_rows(tile):
        if isinstance(tile, int):
            return pl.ds(tile * TILE, TILE)
        return pl.ds(pl.multiple_of(tile * TILE, TILE), TILE)

    load_x = pltpu.make_async_copy(x_any, x_ref, local_sem.at[0])
    load_dy = pltpu.make_async_copy(dy_any, dy_ref, local_sem.at[1])
    keep_act = pltpu.make_async_copy(dy_ref, act_any, local_sem.at[2])
    keep_dx = pltpu.make_async_copy(dx_ref, dx_any, local_sem.at[3])
    load_dy.start()
    load_x.start()

    barrier = pltpu.get_barrier_semaphore()
    for step in range(1, seq_n):
        pl.semaphore_signal(
            barrier, inc=1, device_id=(dp_i, seq_peer(step)), device_id_type=MESH
        )
    for step in range(1, dp_n):
        pl.semaphore_signal(
            barrier, inc=1, device_id=(dp_peer(step), sq_i), device_id_type=MESH
        )

    bkv[y, c, z, x, :, 0 : 2 * width] = wq_ref[:, width:].astype(BF)
    bqo[y, c, z, x, :, 0:width] = wq_ref[:, 0:width].astype(BF)
    bqo[y, c, z, x, :, width:] = wo_ref[...].astype(BF)
    count = nrm_ref.shape[0]
    ntall[...] = jnp.zeros_like(ntall)
    ntall[0:count, 0:blk] = nrm_ref[...]
    bkv[y, c, z, x, :, 2 * width :] = ntall[...].T[0:blk].astype(BF)
    for part in range(nz):
        for group in range(dp_n):
            lo, at = part * part_n + group * LANES, (group * nz + part) * LANES
            bu[y, c, z, x, :, lo : lo + LANES] = wu_ref[:, at : at + LANES].astype(BF)
    bd[y, c, z, x] = wd_ref[...].astype(BF)
    pl.semaphore_wait(barrier, seq_n + dp_n - 2)

    def gather_hops(full, base):
        cut = (full.shape[5] // 2) // LANES * LANES
        one, two = pl.ds(0, cut), pl.ds(cut, full.shape[5] - cut)

        def same(part, index, target):
            return hop(part, part, base + index, target)

        first = [
            same(full.at[y, c, z, x], step - 1, dev(y, c, z_peer(step), x))
            for step in range(1, nz)
        ]
        second = [
            same(full.at[y, c, :, x, :, one], 3, over_x),
            same(full.at[y, c, :, x, :, two], 4, over_y),
        ]
        third = [
            same(full.at[y, c, :, :, :, one], 5, over_y),
            same(full.at[:, c, :, x, :, two], 6, over_x),
        ]
        last = [same(full.at[:, c], 7, twin)]
        return first, second, third, last

    def direct(full, base):
        mine = full.at[y, c, z, x]
        return [
            hop(mine, mine, base + step - 1, dev(y, c, z_peer(step), x)) for step in range(1, nz)
        ]

    def spread_hops(part):
        base = SPREAD + part * 10
        cols = pl.ds(pl.multiple_of(part * part_n, part_n), part_n)
        one = pl.ds(pl.multiple_of(part * part_n, LANES), part_n // 2)
        two = pl.ds(pl.multiple_of(part * part_n + part_n // 2, LANES), part_n // 2)
        d_one, d_two = pl.ds(0, width // 2), pl.ds(width // 2, width // 2)

        def same(place, index, target):
            return hop(place, place, base + index, target)

        return (
            [
                same(bu.at[y, c, :, x, :, one], 0, over_x),
                same(bu.at[y, c, :, x, :, two], 1, over_y),
                same(bd.at[y, c, part, x, :, d_one], 2, over_x),
                same(bd.at[y, c, part, x, :, d_two], 3, over_y),
            ],
            [
                same(bu.at[y, c, :, :, :, one], 4, over_y),
                same(bu.at[:, c, :, x, :, two], 5, over_x),
                same(bd.at[y, c, part, :, :, d_one], 6, over_y),
                same(bd.at[:, c, part, x, :, d_two], 7, over_x),
            ],
            [
                same(bu.at[:, c, :, :, :, cols], 8, twin),
                same(bd.at[:, c, part], 9, twin),
            ],
        )

    def pass_on(part, stage):
        hops = spread_hops(part)
        arrived(hops[stage])
        start(hops[stage + 1])

    hops_kv = gather_hops(bkv, GATHER)
    hops_qo = gather_hops(bqo, GATHER + 8)
    direct_u = direct(bu, GATHER + 16)
    direct_d = direct(bd, GATHER + 19)
    start(hops_kv[0])
    start(hops_qo[0])
    nacc[...] = jnp.zeros_like(nacc)
    arrived(hops_kv[0])
    start(hops_kv[1])
    start(direct_u)
    start(direct_d)
    load_dy.wait()

    def turn_dy(tile):
        rows = tile_rows(tile)
        dyt_s[:, rows] = dy_ref[rows, :].astype(F32).T.astype(BF)

    each(tiles // 2, turn_dy)
    arrived(hops_kv[1])
    start(hops_kv[2])
    arrived(hops_qo[0])
    start(hops_qo[1])
    load_x.wait()
    each(tiles // 2, lambda tile: turn_dy(tile + tiles // 2))

    def first_hat(tile):
        rows = tile_rows(tile)
        dx_ref[rows, :] = centered(x_ref[rows, :].astype(F32))[0]

    each(tiles, first_hat)
    arrived(hops_kv[2])
    start(hops_kv[3])
    arrived(hops_qo[1])
    start(hops_qo[2])
    arrived(direct_u)
    arrived(direct_d)
    for part in range(nz):
        start(spread_hops(part)[0])
    arrived(hops_kv[3])

    norm_cols = bkv[:, :, :, :, :, 2 * width :].reshape(width, LANES).astype(F32)
    nrow[...] = norm_cols.T[0:8]

    def w_qkv(part):
        if part == 0:
            return bqo[:, :, :, :, :, 0:width].reshape(width, width)
        return bkv[:, :, :, :, :, (part - 1) * width : part * width].reshape(width, width)

    def first_norm(rows):
        hat, scale = centered(x_ref[rows, :].astype(F32))
        return hat, scale, (hat * nrow[0:1, :] + nrow[1:2, :]).astype(BF)

    def live_pick(tile):
        block_at = lax.broadcasted_iota(jnp.int32, (blocks, TILE), 0)
        row_at = lax.broadcasted_iota(jnp.int32, (blocks, TILE), 1) + tile * TILE
        pos = sq_i * local_len + lax.rem(row_at, local_len)
        item = row_at // local_len
        length = jnp.zeros((blocks, TILE), jnp.int32)
        for i in range(TILE // local_len):
            at = tile * (TILE // local_len) + i
            length = jnp.where(item == at, len_ref[at], length)
        return jnp.where((row_at // SPAN == block_at) & (pos < length), 1.0, 0.0).astype(BF)

    def kv_tile(tile, pooled):
        rows = tile_rows(tile)
        h1 = (dx_ref[rows, :] * nrow[0:1, :] + nrow[1:2, :]).astype(BF)
        h2_s[rows, :] = h1
        for part in (1, 2):
            qkv[rows, pl.ds(part * width, width)] = mm(h1, w_qkv(part)).astype(BF)

        if tile == 3:
            arrived(hops_qo[2])
            start(hops_qo[3])
        return pooled + mm(live_pick(tile), qkv[rows, width:])

    pooled = jnp.zeros((blocks, 2 * width), F32)
    for index in range(tiles):
        pooled = kv_tile(index, pooled)
    block_col = lax.broadcasted_iota(jnp.int32, (blocks, 1), 0)
    length_col = jnp.zeros((blocks, 1), jnp.int32)
    for i in range(blocks // spans_here):
        length_col = jnp.where(block_col // spans_here == i, len_ref[i], length_col)
    first_pos = sq_i * local_len + lax.rem(block_col, spans_here) * SPAN
    count_col = jnp.clip(length_col - first_pos, 1, SPAN).astype(F32)
    pool_all[sq_i] = (pooled / count_col).astype(BF)
    pool_hops = [
        hop(pool_all.at[sq_i], pool_all.at[sq_i], POOL + step - 1, (dp_i, seq_peer(step)))
        for step in range(1, seq_n)
    ]
    start(pool_hops)
    pass_on(0, 0)
    arrived(hops_qo[3])

    def q_tile(tile):
        rows = tile_rows(tile)
        qkv[rows, 0:width] = mm(h2_s[rows, :], w_qkv(0)).astype(BF)

    flat(tiles, q_tile)
    arrived(pool_hops)

    far_n = seq_n * blocks
    to_row = lax.broadcasted_iota(jnp.int32, (far_n, far_n), 0)
    to_col = lax.broadcasted_iota(jnp.int32, (far_n, far_n), 1)
    item_row, span_row = to_row // spans_all, to_row % spans_all
    wanted = (span_row // spans_here) * blocks + item_row * spans_here + span_row % spans_here
    order = jnp.where(wanted == to_col, 1.0, 0.0).astype(BF)
    pool_far[...] = mm(order, pool_all[...].reshape(far_n, 2 * width)).astype(BF)

    keys_n = SPAN + spans_all
    lane = lax.broadcasted_iota(jnp.int32, (1, LANES), 1)
    score_scale = HEAD_DIM ** (-0.5)
    half_a = jnp.where(lane < HEAD_DIM, 1.0, 0.0)
    half_b = jnp.where(lane >= HEAD_DIM, 1.0, 0.0)
    query_a, query_b = (half_a * score_scale).astype(BF), (half_b * score_scale).astype(BF)
    grad_a, grad_b = half_a.astype(BF), half_b.astype(BF)

    def both(near_rows, far_rows, cols):
        far_cols = pl.ds(cols.start - width, cols.size)
        return jnp.concatenate([qkv[near_rows, cols], pool_far[far_rows, far_cols]], axis=0)

    def cols_of(third, pair):
        return pl.ds(third * width + pair * LANES, LANES)

    def by_head(rows_in, first, second):
        return jnp.concatenate([rows_in * first, rows_in * second], axis=0)

    units = [(sub, pair) for sub in range(spans_here) for pair in range(pairs)]
    items = blocks // spans_here

    def rows_of(item, sub):
        return pl.ds(pl.multiple_of(item * local_len + sub * SPAN, SPAN), SPAN)

    def far_of(item):
        return pl.ds(pl.multiple_of(item * spans_all, spans_all), spans_all)

    def attend(two):
        for at, moves in (
            (0, ((1, 0),)), (1, ((0, 1), (2, 0))), (2, ((3, 0),)), (3, ((1, 1),)),
        ):

            @pl.when(two == at)
            def _(moves=moves):
                for part, stage in moves:
                    pass_on(part, stage)

        key_at = lax.broadcasted_iota(jnp.int32, (keys_n, 2 * SPAN), 0)
        span_at = key_at - SPAN
        spots = [(two * 2 + k, sub) for k in range(2) for sub in range(spans_here)]

        def seen(item, sub):
            mine = sq_i * spans_here + sub
            length = len_ref[item]
            near_ok = (key_at < SPAN) & (mine * SPAN + key_at < length)
            return near_ok | ((key_at >= SPAN) & (span_at * SPAN < length) & (span_at != mine))

        scores = []
        for item, sub in spots:
            rows = rows_of(item, sub)
            for pair in range(pairs):
                kk = both(rows, far_of(item), cols_of(1, pair))
                scores.append(mm(kk, by_head(qkv[rows, cols_of(0, pair)], query_a, query_b), NT))
        for n, (item, sub) in enumerate(spots):
            for pair in range(pairs):
                score = jnp.where(seen(item, sub), scores[n * pairs + pair], neg_fill)
                raised = jnp.exp(score - jnp.max(score, axis=0, keepdims=True))
                share = raised * (1.0 / jnp.sum(raised, axis=0, keepdims=True))
                prob[item * spans_here + sub, pair] = share.astype(BF)
        for item, sub in spots:
            rows = rows_of(item, sub)
            mixed = []
            for pair in range(pairs):
                vv = both(rows, far_of(item), cols_of(2, pair))
                stacked = mm(vv, prob[item * spans_here + sub, pair], TN)
                mixed += [stacked[0:HEAD_DIM, 0:SPAN], stacked[HEAD_DIM:, SPAN:]]
            mix[rows, :] = jnp.concatenate(mixed, axis=0).T.astype(BF)

    each(items // 2, attend)
    for group in (*hops_kv, *hops_qo, direct_u, direct_d, pool_hops):
        sent(group)

    w_out = bqo[:, :, :, :, :, width:].reshape(width, width)
    gelu_in = math.sqrt(2.0 / math.pi)
    gelu_cube = 0.044715

    def second_norm(rows):
        x1 = x_ref[rows, :].astype(F32) + mm(mix[rows, :], w_out)
        hat, scale = centered(x1)
        return x1, hat, scale

    def ffn_open(tile):
        if tile == 2:
            pass_on(2, 1)
        rows = tile_rows(tile)
        x1, hat, _ = second_norm(rows)
        yacc[rows, :] = x1
        dx_ref[rows, :] = jnp.zeros((TILE, width), F32)
        h2 = hat * nrow[2:3, :] + nrow[3:4, :]
        h2_s[rows, :] = h2.astype(BF)
        ht_s[:, rows] = h2.T.astype(BF)

    flat(tiles, ffn_open)

    half_cols = width // 2
    one_p, two_p = pl.ds(0, half_cols), pl.ds(half_cols, half_cols)
    up_rows = nz * blk

    def part_hops(part):
        base = PARTS + part * 8
        slot = part % 2
        return (
            [hop(s1p, r1p.at[slot], base, twin)],
            [
                hop(s1p.at[1 - y, :, :, one_p], r2ap.at[slot], base + 1, over_y),
                hop(s1p.at[:, 1 - x, :, two_p], r2bp.at[slot], base + 2, over_x),
            ],
            [
                hop(s2ap.at[1 - x], r3ap.at[slot], base + 3, over_x),
                hop(s2bp.at[1 - y], r3bp.at[slot], base + 4, over_y),
            ],
            [
                hop(
                    s4p.at[part, z_peer(step)], r4p.at[step - 1, part], base + 4 + step,
                    dev(y, c, z_peer(step), x),
                )
                for step in range(1, nz)
            ],
        )

    def down_cols(group):
        cols = pl.ds(pl.multiple_of(group * LANES, LANES), LANES)
        return gq[:, :, :, :, :, cols].reshape(width, LANES)

    def part_first(part):
        for yy in range(ny):
            for xx in range(nx):
                for zz in range(nz):
                    at = pl.ds(zz * blk, blk)
                    own_p[yy, xx, at] = go[yy, c, zz, xx]
                    s1p[yy, xx, at] = go[yy, 1 - c, zz, xx].astype(BF)
            mine = down_cols(yy * nc + c).T
            other = down_cols(yy * nc + 1 - c).T
            for xx in range(nx):
                own_p[yy, xx, up_rows:] = mine[xx * dblk : (xx + 1) * dblk]
                s1p[yy, xx, up_rows:] = other[xx * dblk : (xx + 1) * dblk].astype(BF)
        start(part_hops(part)[0])

    def part_second(part):
        hops = part_hops(part)
        arrived(hops[0])
        sent(hops[0])

        def add(index):
            yy, xx = index // nx, index % nx
            total = own_p[yy, xx] + r1p[part % 2, yy, xx].astype(F32)
            own_p[yy, xx] = total
            s1p[yy, xx] = total.astype(BF)

        each(ny * nx, add)
        start(hops[1])

    def part_third(part):
        hops = part_hops(part)
        arrived(hops[1])
        sent(hops[1])
        for xx in range(nx):
            total = own_p[y, xx, :, one_p] + r2ap[part % 2, xx].astype(F32)
            own_p[y, xx, :, one_p] = total
            s2ap[xx] = total.astype(BF)
        for yy in range(ny):
            total = own_p[yy, x, :, two_p] + r2bp[part % 2, yy].astype(F32)
            own_p[yy, x, :, two_p] = total
            s2bp[yy] = total.astype(BF)
        kept_p[...] = own_p[y, x]
        start(hops[2])

    def part_fourth(part):
        hops = part_hops(part)
        arrived(hops[2])
        sent(hops[2])
        kept_p[:, one_p] += r3ap[part % 2].astype(F32)
        kept_p[:, two_p] += r3bp[part % 2].astype(F32)
        for zz in range(nz):
            s4p[part, zz] = kept_p[zz * blk : (zz + 1) * blk].astype(BF)
        fin_p[part] = kept_p[pl.ds(pl.multiple_of(z * blk, blk), blk)]
        down = kept_p[up_rows:]
        keep_d[part] = down
        s5d[part] = down.astype(BF)
        start(hops[3])

    down_hops = [
        hop(
            s5d.at[z_peer(step)], r5d.at[step - 1], DOWN + step - 1, dev(y, c, z_peer(step), x)
        )
        for step in range(1, nz)
    ]

    def ffn_part(part, carry):
        cols = pl.ds(pl.multiple_of(part * part_n, part_n), part_n)
        arrived(spread_hops(part)[2])
        w_up = bu[:, :, :, :, :, cols].reshape(width, part_n)
        w_down = bd[:, :, part].reshape(part_n, width)

        def ffn_tile(tile):
            @pl.when((part == 0) & (tile == 1))
            def _():
                pass_on(3, 1)

            @pl.when((part > 0) & (tile == 1))
            def _():
                part_second(part - 1)

            rows = pl.ds(pl.multiple_of(tile * ffn_rows, ffn_rows), ffn_rows)
            for piece in range(ffn_rows // TILE):
                some = tile_rows(tile * (ffn_rows // TILE) + piece)
                up = mm(h2_s[some, :], w_up)
                square = up * up
                bent = jnp.tanh(up * (gelu_in + (gelu_in * gelu_cube) * square))
                half = 0.5 + 0.5 * bent
                act_s[some, :] = (up * half).astype(BF)
                rate = half + (up * (1.0 - bent * bent)) * (
                    0.5 * gelu_in + (1.5 * gelu_in * gelu_cube) * square
                )
                dup_s[some, :] = (mm(dy_ref[some, :], w_down, NT) * rate).astype(BF)
            yacc[rows, :] += mm(act_s[rows, :], w_down)
            dx_ref[rows, :] += mm(dup_s[rows, :], w_up, NT)

        each(rows_all // ffn_rows, ffn_tile)

        @pl.when(part > 1)
        def _():
            part_fourth(part - 2)

        gq[:, :, :, :, :, 0:part_n] = mm(dyt_s[...], act_s[...]).reshape(go.shape)
        go[...] = mm(ht_s[...], dup_s[...]).reshape(go.shape)

        @pl.when(part > 0)
        def _():
            part_third(part - 1)

        part_first(part)
        return carry

    lax.fori_loop(0, nz, ffn_part, 0)

    def ffn_close(tile):
        if tile == 2:
            part_second(nz - 1)
        if tile == 3:
            part_fourth(nz - 2)
        rows = tile_rows(tile)
        _, hat, scale = second_norm(rows)
        dh2 = dx_ref[rows, :]
        nacc[2] += fold_rows(dh2 * hat)
        nacc[3] += fold_rows(dh2)
        dx1 = dy_ref[rows, :].astype(F32) + norm_back(dh2 * nrow[2:3, :], hat, scale)
        dy_ref[rows, :] = yacc[rows, :].astype(BF)
        dx_ref[rows, :] = dx1
        dz = dx1.astype(BF)
        act_s[rows, :] = dz
        ht_s[:, rows] = mix[rows, :].astype(F32).T.astype(BF)
        mix[rows, :] = mm(dz, w_out, NT).astype(BF)

    flat(tiles, ffn_close)
    keep_act.start()
    for part in range(nz):
        for group in spread_hops(part):
            sent(group)
    go[...] = mm(ht_s[...], act_s[...]).reshape(go.shape)

    def reduce_steps(full, cols, s1, r1, s2a, s2b, r2a, r2b, r3a, r3b, s3, r4, fin, base):
        full = full.at[:, :, :, :, :, cols]
        own = full.at[:, c]
        n = s1.shape[4]
        cut = (n // 2) // LANES * LANES
        one, two = pl.ds(0, cut), pl.ds(cut, n - cut)
        hop1 = [hop(s1, r1, base, twin)]
        hop2 = [
            hop(s1.at[1 - y, :, :, :, one], r2a, base + 1, over_y),
            hop(s1.at[:, :, 1 - x, :, two], r2b, base + 2, over_x),
        ]
        hop3 = [
            hop(s2a.at[:, 1 - x], r3a, base + 3, over_x),
            hop(s2b.at[1 - y], r3b, base + 4, over_y),
        ]
        hop4 = [
            hop(
                s3.at[z_peer(step)], r4.at[step - 1], base + 4 + step,
                dev(y, c, z_peer(step), x),
            )
            for step in range(1, nz)
        ]

        def places(index):
            return index // (nz * nx), (index // nx) % nz, index % nx

        def stage1():
            def load(index):
                yy, zz, xx = places(index)
                s1[yy, zz, xx] = full[yy, 1 - c, zz, xx].astype(BF)

            each(ny * nz * nx, load)
            start(hop1)

        def stage2():
            arrived(hop1)
            sent(hop1)

            def add(index):
                yy, zz, xx = places(index)
                total = own[yy, zz, xx] + r1[yy, zz, xx].astype(F32)
                own[yy, zz, xx] = total
                s1[yy, zz, xx] = total.astype(BF)

            each(ny * nz * nx, add)
            start(hop2)

        def stage3():
            arrived(hop2)
            for zz in range(nz):
                for xx in range(nx):
                    total = own[y, zz, xx, :, one] + r2a[zz, xx].astype(F32)
                    own[y, zz, xx, :, one] = total
                    s2a[zz, xx] = total.astype(BF)
            start(hop3[0:1])
            for yy in range(ny):
                for zz in range(nz):
                    total = own[yy, zz, x, :, two] + r2b[yy, zz].astype(F32)
                    own[yy, zz, x, :, two] = total
                    s2b[yy, zz] = total.astype(BF)
            start(hop3[1:2])

        def stage4():
            arrived(hop3)
            for zz in range(nz):
                total = own[y, zz, x, :, one] + r3a[zz].astype(F32)
                own[y, zz, x, :, one] = total
                s3[zz, :, one] = total.astype(BF)
                total = own[y, zz, x, :, two] + r3b[zz].astype(F32)
                own[y, zz, x, :, two] = total
                s3[zz, :, two] = total.astype(BF)
            start(hop4)

        def stage5():
            arrived(hop4)
            total = own[y, z, x]
            for step in range(nz - 1):
                total = total + r4[step].astype(F32)
            fin[:, cols] = total
            sent(hop2)
            sent(hop3)
            sent(hop4)

        return stage1, stage2, stage3, stage4, stage5

    cols_q, cols_kv = pl.ds(0, width), pl.ds(width, 2 * width)
    red_o = reduce_steps(
        go, cols_q, bu.at[:, 0, :, :, :, cols_q], r1o, s2ao, s2bo, r2ao, r2bo, r3ao, r3bo, s3o,
        r4o, fin_o, OUTER,
    )
    red_q = reduce_steps(
        gq, cols_q, bu.at[:, 1, :, :, :, cols_q], r1q, s2aq, s2bq, r2aq, r2bq, r3aq, r3bq,
        s3q, r4q, fin_q, INNER,
    )
    red_kv = reduce_steps(
        gq, cols_kv, bu.at[:, 1, :, :, :, cols_kv], r1k, s2ak, s2bk, r2ak, r2bk, r3ak, r3bk,
        s3k, r4k, fin_q, INNER + 8,
    )
    red_o[0]()

    def last_third():
        part_third(nz - 1)

    def fourth_and_down():
        part_fourth(nz - 1)
        start(down_hops)

    def attend_back(item):
        for at, step in (
            (0, red_o[1]), (1, last_third), (3, fourth_and_down), (4, red_o[2]), (7, red_o[3])
        ):

            @pl.when(item == at)
            def _(step=step):
                step()

        far_rows = far_of(item)
        dshares = []
        for sub, pair in units:
            rows = rows_of(item, sub)
            vv = both(rows, far_rows, cols_of(2, pair))
            dshares.append(mm(vv, by_head(mix[rows, cols_of(0, pair)], grad_a, grad_b), NT))
        far_k, far_v = [0.0] * pairs, [0.0] * pairs
        for (sub, pair), dshare in zip(units, dshares):
            rows, at = rows_of(item, sub), item * spans_here + sub
            share = prob[at, pair]
            dv = mm(share, by_head(mix[rows, cols_of(0, pair)], grad_a, grad_b))
            qkv[rows, cols_of(2, pair)] = dv[0:SPAN].astype(BF)
            far_v[pair] = far_v[pair] + dv[SPAN:]
            share = share.astype(F32)
            inner = jnp.sum(share * dshare, axis=0, keepdims=True)
            prob[at, pair] = (share * (dshare - inner)).astype(BF)
        for sub in range(spans_here):
            rows = rows_of(item, sub)
            dqs = []
            for pair in range(pairs):
                dscore = prob[item * spans_here + sub, pair]
                stacked = mm(both(rows, far_rows, cols_of(1, pair)), dscore, TN)
                dqs += [stacked[0:HEAD_DIM, 0:SPAN], stacked[HEAD_DIM:, SPAN:]]
                dk = mm(dscore, by_head(qkv[rows, cols_of(0, pair)], query_a, query_b))
                qkv[rows, cols_of(1, pair)] = dk[0:SPAN].astype(BF)
                far_k[pair] = far_k[pair] + dk[SPAN:]
            dq = jnp.concatenate(dqs, axis=0).T * score_scale
            qkv[rows, 0:width] = dq.astype(BF)
        for pair in range(pairs):
            pool_grad[far_rows, cols_of(0, pair)] = far_k[pair]
            pool_grad[far_rows, cols_of(1, pair)] = far_v[pair]

    each(items, attend_back)

    back_row = lax.broadcasted_iota(jnp.int32, (far_n, far_n), 0)
    back_col = lax.broadcasted_iota(jnp.int32, (far_n, far_n), 1)
    owner, place = back_row // blocks, back_row % blocks
    source = (place // spans_here) * spans_all + owner * spans_here + place % spans_here
    reorder = jnp.where(source == back_col, 1.0, 0.0).astype(BF)
    pool_send[...] = (
        mm(reorder, pool_grad[...].astype(BF)).astype(BF).reshape(seq_n, blocks, 2 * width)
    )
    back_hops = [
        hop(
            pool_send.at[seq_peer(step)], pool_recv.at[step - 1], POOLBACK + step - 1,
            (dp_i, seq_peer(step)),
        )
        for step in range(1, seq_n)
    ]
    start(back_hops)

    live_sum[...] = jnp.zeros_like(live_sum)

    def turn_h1(tile):
        rows = tile_rows(tile)
        _, _, h1 = first_norm(rows)
        ht_s[:, rows] = h1.astype(F32).T.astype(BF)
        live_sum[...] += mm(live_pick(tile), h1)

    each(tiles, turn_h1)
    for part in range(3):
        cols = pl.ds(part * width, width)
        gq[:, :, :, :, :, cols] = mm(ht_s[...], qkv[:, cols]).reshape(
            ny, nc, nz, nx, blk, width
        )
        if part == 0:
            red_q[0]()
    red_q[1]()
    arrived(back_hops)
    pool_total = pool_send[sq_i].astype(F32)
    for step in range(seq_n - 1):
        pool_total = pool_total + pool_recv[step].astype(F32)
    far = pool_total / count_col
    far_hi = far.astype(BF)
    far_lo = (far - far_hi.astype(F32)).astype(BF)
    near = live_sum[...]
    near_hi = near.astype(BF)
    near_lo = (near - near_hi.astype(F32)).astype(BF)
    left = jnp.concatenate([near_hi, near_lo, near_hi], axis=0)
    right = jnp.concatenate([far_hi, far_hi, far_lo], axis=0)
    for part in range(2):
        cols = pl.ds((part + 1) * width, width)
        gq[:, :, :, :, :, cols] += mm(left, right[:, part * width : (part + 1) * width], TN).reshape(
            ny, nc, nz, nx, blk, width
        )
    red_kv[0]()
    far_two = jnp.concatenate([far_hi, far_lo], axis=0)
    both_far = mm(far_two[:, 0:width], w_qkv(1), NT) + mm(far_two[:, width:], w_qkv(2), NT)
    spread_w[...] = both_far[0:blocks] + both_far[blocks:]

    def last_tile(tile):
        @pl.when(tile == 1)
        def _():
            red_kv[1]()

        @pl.when(tile == 2)
        def _():
            red_q[2]()

        rows = tile_rows(tile)
        hat, scale, _ = first_norm(rows)
        extra = []
        for part in range(per_tile):
            block = tile * per_tile + part
            pos = (
                sq_i * local_len
                + lax.rem(block, spans_here) * SPAN
                + lax.broadcasted_iota(jnp.int32, (SPAN, 1), 0)
            )
            live = jnp.where(pos < len_ref[block // spans_here], 1.0, 0.0)
            extra.append(live * spread_w[pl.ds(block, 1), :])
        dh1 = jnp.concatenate(extra, axis=0)
        for part in range(3):
            dh1 = dh1 + mm(qkv[rows, pl.ds(part * width, width)], w_qkv(part), NT)
        nacc[0] += fold_rows(dh1 * hat)
        nacc[1] += fold_rows(dh1)
        dx_ref[rows, :] += norm_back(dh1 * nrow[0:1, :], hat, scale)

    each(tiles, last_tile)
    keep_dx.start()
    norm_rows = [jnp.sum(nacc[k], axis=0, keepdims=True) for k in range(4)]
    norm_rows.append(jnp.zeros((4, width), F32))
    norm_seq[sq_i] = jnp.concatenate(norm_rows, axis=0)
    norm_hops = [
        hop(norm_seq.at[sq_i], norm_seq.at[sq_i], NORM_SEQ + step - 1, (dp_i, seq_peer(step)))
        for step in range(1, seq_n)
    ]
    norm_hops_dp = [
        hop(norm_dp.at[dp_i], norm_dp.at[dp_i], NORM_DP + step - 1, (dp_peer(step), sq_i))
        for step in range(1, dp_n)
    ]
    start(norm_hops)
    red_kv[2]()
    red_q[3]()
    for part in range(nz):
        arrived(part_hops(part)[3])
        total = fin_p[part]
        for step in range(nz - 1):
            total = total + r4p[step, part].astype(F32)
        for group in range(dp_n):
            at = (group * nz + part) * LANES
            fin_u[:, at : at + LANES] = total[:, group * LANES : (group + 1) * LANES]
    arrived(down_hops)
    total = keep_d[z]
    for step in range(nz - 1):
        total = total + r5d[step].astype(F32)
    fin_d[...] = total
    red_o[4]()

    arrived(norm_hops)
    total = norm_seq[0]
    for k in range(1, seq_n):
        total = total + norm_seq[k]
    norm_dp[dp_i] = total
    start(norm_hops_dp)
    red_kv[3]()
    red_q[4]()

    def partial(values_in):
        squares = fold_rows(values_in * values_in)
        return sum(
            squares[:, k * LANES : (k + 1) * LANES] for k in range(squares.shape[1] // LANES)
        )

    early = partial(fin_u[...]) + partial(fin_d[...]) + partial(fin_o[...])
    red_kv[4]()
    psq[sq_i] = early + partial(fin_q[...])
    seq_hops = [
        hop(psq.at[sq_i], psq.at[sq_i], SQUARE_SEQ + step - 1, (dp_i, seq_peer(step)))
        for step in range(1, seq_n)
    ]
    start(seq_hops)
    sent(back_hops)
    for part in range(nz):
        sent(part_hops(part)[3])
    sent(down_hops)
    sent(norm_hops)
    arrived(norm_hops_dp)
    sent(norm_hops_dp)
    total = norm_dp[0]
    for k in range(1, dp_n):
        total = total + norm_dp[k]
    norm_sum[...] = total
    arrived(seq_hops)
    total = psq[0]
    for k in range(1, seq_n):
        total = total + psq[k]
    psd[dp_i] = total
    dp_hops = [
        hop(psd.at[dp_i], psd.at[dp_i], SQUARE_DP + step - 1, (dp_peer(step), sq_i))
        for step in range(1, dp_n)
    ]
    start(dp_hops)
    arrived(dp_hops)
    total = psd[0]
    for k in range(1, dp_n):
        total = total + psd[k]
    total_ref[...] = total
    sent(seq_hops)
    sent(dp_hops)
    keep_act.wait()
    keep_dx.wait()


def update_kernel(
    act_in, dx_in, total_ref, gq_ref, go_ref, gu_ref, gd_ref, gn_ref,
    wq_ref, wo_ref, wu_ref, wd_ref, wn_ref, fq_ref, fo_ref, fu_ref, fd_ref, fn_ref,
    sq_ref, so_ref, su_ref, sd_ref, sn_ref,
    act_out, dx_out, norm_ref, nq, nfq, nsq, no, nfo, nso, nu, nfu, nsu, nd, nfd, nsd,
    nn, nfn, nsn, act_s, dx_s, sems_in, sems_out,
):
    pieces = 2
    piece = act_s.shape[0] // pieces
    moves = []
    for k in range(pieces):
        rows = pl.ds(k * piece, piece)
        for n, (src, mid, dst) in enumerate(
            ((dx_in, dx_s, dx_out), (act_in, act_s, act_out))
        ):
            moves.append((
                pltpu.make_async_copy(src.at[rows], mid.at[rows], sems_in.at[n * pieces + k]),
                pltpu.make_async_copy(mid.at[rows], dst.at[rows], sems_out.at[n * pieces + k]),
            ))
    for inward, _ in moves:
        inward.start()
    norm_grads = gn_ref[...]
    total = jnp.sum(total_ref[...]) + jnp.sum(norm_grads * norm_grads)
    total = jnp.full((1, 1), total, F32)
    grad_norm = jnp.sqrt(total)
    factor = clip_bound / jnp.maximum(grad_norm, clip_bound)
    norm_ref[...] = grad_norm

    def update(weight, grad_in, first, second, outs, rate, decay):
        new = adamw_update(weight, grad_in, first, second, factor, rate, decay)
        for out, value in zip(outs, new):
            out[...] = value

    for inward, outward in moves:
        inward.wait()
        outward.start()
    for w, g, m, s, outs in (
        (wq_ref, gq_ref, fq_ref, sq_ref, (nq, nfq, nsq)),
        (wo_ref, go_ref, fo_ref, so_ref, (no, nfo, nso)),
        (wu_ref, gu_ref, fu_ref, su_ref, (nu, nfu, nsu)),
        (wd_ref, gd_ref, fd_ref, sd_ref, (nd, nfd, nsd)),
    ):
        update(w[...], g[...], m[...], s[...], outs, rate_matrix, decay_coef)
    count, cols = wn_ref.shape
    width = norm_grads.shape[1]
    place = (lax.axis_index("dp") * lax.axis_size("seq") + lax.axis_index("seq")) * cols
    turned = pltpu.roll(norm_grads, lax.rem(width - place, width), 1)
    update(
        wn_ref[...], turned[0:count, 0:cols], fn_ref[...], sn_ref[...], (nn, nfn, nsn),
        rate_norm, 0.0,
    )
    for _, outward in moves:
        outward.wait()


def fused_device(
    tokens, cotangent, lengths, w_qkv, w_out, w_up, w_down, norm_params,
    first_qkv, first_out, first_up, first_down, first_norm,
    second_qkv, second_out, second_up, second_down, second_norm,
):
    item_count, local_len, width = tokens.shape
    rows_all = item_count * local_len
    dp_n, seq_n = lax.axis_size("dp"), lax.axis_size("seq")
    nc = 2
    ny = dp_n // nc
    nx = ny
    nz = seq_n // nx
    blk, width3 = w_qkv.shape
    ff = w_up.shape[1]
    dblk = w_down.shape[0]
    blocks = rows_all // SPAN
    far_n = seq_n * blocks
    keys_n = SPAN + local_len // SPAN * seq_n
    part_n = ff // nz
    up_rows = nz * blk
    half = width // 2

    def bufs(b, n):
        cut = (n // 2) // LANES * LANES
        rest = n - cut
        taken = [pltpu.VMEM((nz, nx, b, cut), BF), pltpu.VMEM((ny, nz, b, rest), BF)]
        return [
            *taken,
            pltpu.VMEM((nz, b, n), BF),
            pltpu.VMEM((ny, nz, nx, b, n), BF),
            *taken,
            pltpu.VMEM((nz, b, cut), BF),
            pltpu.VMEM((nz, b, rest), BF),
            pltpu.VMEM((nz - 1, b, n), BF),
        ]

    whole = pl.BlockSpec(memory_space=pltpu.VMEM)
    outside = pl.BlockSpec(memory_space=pl.ANY)
    part_rows = up_rows + dblk
    outs = pl.pallas_call(
        layer_kernel,
        out_shape=[
            jax.ShapeDtypeStruct((rows_all, width), BF),
            jax.ShapeDtypeStruct((rows_all, width), F32),
            jax.ShapeDtypeStruct(w_qkv.shape, F32),
            jax.ShapeDtypeStruct(w_out.shape, F32),
            jax.ShapeDtypeStruct(w_up.shape, F32),
            jax.ShapeDtypeStruct(w_down.shape, F32),
            jax.ShapeDtypeStruct((8, width), F32),
            jax.ShapeDtypeStruct((8, LANES), F32),
        ],
        in_specs=[pl.BlockSpec(memory_space=pltpu.SMEM), outside, outside] + [whole] * 5,
        out_specs=[outside, outside] + [whole] * 6,
        scratch_shapes=[
            pltpu.VMEM((ny, nc, nz, nx, blk, 2 * width + LANES), BF),
            pltpu.VMEM((ny, nc, nz, nx, blk, 2 * width), BF),
            pltpu.VMEM((ny, nc, nz, nx, blk, ff), BF),
            pltpu.VMEM((ny, nc, nz, nx, dblk, width), BF),
            pltpu.VMEM((rows_all, width3), BF),
            pltpu.VMEM((rows_all, width), BF),
            pltpu.VMEM((blocks, width // LANES, keys_n, 2 * SPAN), BF),
            pltpu.VMEM((ny, nc, nz, nx, blk, width3), F32),
            pltpu.VMEM((ny, nc, nz, nx, blk, width), F32),
            pltpu.VMEM((rows_all, width), F32),
            pltpu.VMEM((rows_all, width), BF),
            pltpu.VMEM((width, rows_all), BF),
            pltpu.VMEM((width, rows_all), BF),
            pltpu.VMEM((rows_all, part_n), BF),
            pltpu.VMEM((rows_all, part_n), BF),
            pltpu.VMEM((ny, nx, part_rows, width), F32),
            pltpu.VMEM((part_rows, width), F32),
            pltpu.VMEM((ny, nx, part_rows, width), BF),
            pltpu.VMEM((2, ny, nx, part_rows, width), BF),
            pltpu.VMEM((nx, part_rows, half), BF),
            pltpu.VMEM((ny, part_rows, half), BF),
            pltpu.VMEM((2, nx, part_rows, half), BF),
            pltpu.VMEM((2, ny, part_rows, half), BF),
            pltpu.VMEM((2, part_rows, half), BF),
            pltpu.VMEM((2, part_rows, half), BF),
            pltpu.VMEM((nz, nz, blk, width), BF),
            pltpu.VMEM((nz - 1, nz, blk, width), BF),
            pltpu.VMEM((nz, blk, width), F32),
            pltpu.VMEM((nz, dblk, width), F32),
            pltpu.VMEM((nz, dblk, width), BF),
            pltpu.VMEM((nz - 1, dblk, width), BF),
            *bufs(blk, width),
            *bufs(blk, 2 * width),
            *bufs(blk, width),
            pltpu.VMEM((seq_n, blocks, 2 * width), BF),
            pltpu.VMEM((far_n, 2 * width), BF),
            pltpu.VMEM((far_n, 2 * width), F32),
            pltpu.VMEM((seq_n, blocks, 2 * width), BF),
            pltpu.VMEM((seq_n - 1, blocks, 2 * width), BF),
            pltpu.VMEM((blocks, width), F32),
            pltpu.VMEM((blocks, width), F32),
            pltpu.VMEM((8, width), F32),
            pltpu.VMEM((4, 8, width), F32),
            pltpu.VMEM((LANES, LANES), F32),
            pltpu.VMEM((seq_n, 8, width), F32),
            pltpu.VMEM((dp_n, 8, width), F32),
            pltpu.VMEM((seq_n, 8, LANES), F32),
            pltpu.VMEM((dp_n, 8, LANES), F32),
            pltpu.VMEM((rows_all, width), BF),
            pltpu.VMEM((rows_all, width), BF),
            pltpu.VMEM((rows_all, width), F32),
            pltpu.SemaphoreType.DMA((COPIES,)),
            pltpu.SemaphoreType.DMA((COPIES,)),
            pltpu.SemaphoreType.DMA((4,)),
        ],
        compiler_params=pltpu.CompilerParams(
            collective_id=0, has_side_effects=True, vmem_limit_bytes=64 * 1024 * 1024 - 65536
        ),
    )(
        lengths,
        tokens.reshape(rows_all, width),
        cotangent.reshape(rows_all, width),
        w_qkv, w_out, w_up, w_down, norm_params,
    )
    weights = (w_qkv, w_out, w_up, w_down, norm_params)
    new = pl.pallas_call(
        update_kernel,
        out_shape=[
            jax.ShapeDtypeStruct((rows_all, width), BF),
            jax.ShapeDtypeStruct((rows_all, width), F32),
            jax.ShapeDtypeStruct((1, 1), F32),
            *(jax.ShapeDtypeStruct(w.shape, F32) for w in weights for _ in range(3)),
        ],
        in_specs=[outside, outside] + [whole] * 21,
        out_specs=[outside, outside] + [whole] * 16,
        scratch_shapes=[
            pltpu.VMEM((rows_all, width), BF),
            pltpu.VMEM((rows_all, width), F32),
            pltpu.SemaphoreType.DMA((4,)),
            pltpu.SemaphoreType.DMA((4,)),
        ],
        compiler_params=pltpu.CompilerParams(vmem_limit_bytes=64 * 1024 * 1024 - 65536),
    )(
        outs[0], outs[1], outs[7], *outs[2:7], *weights,
        first_qkv, first_out, first_up, first_down, first_norm,
        second_qkv, second_out, second_up, second_down, second_norm,
    )
    return (
        new[0].reshape(tokens.shape), new[1].reshape(tokens.shape), new[2].reshape(()),
        *new[3:],
    )


def solution(mesh):
    placed = (
        P("dp", "seq", None),
        P("dp", "seq", None),
        P("dp"),
        P(("dp", "seq"), None),
        P(("dp", "seq"), None),
        P(("dp", "seq"), None),
        P(("dp", "seq"), None),
        P(None, ("dp", "seq")),
        P(("dp", "seq"), None),
        P(("dp", "seq"), None),
        P(("dp", "seq"), None),
        P(("dp", "seq"), None),
        P(None, ("dp", "seq")),
        P(("dp", "seq"), None),
        P(("dp", "seq"), None),
        P(("dp", "seq"), None),
        P(("dp", "seq"), None),
        P(None, ("dp", "seq")),
    )
    dp_n, seq_n = mesh.shape["dp"], mesh.shape["seq"]
    fits = dp_n == 4 and seq_n % 2 == 0 and WIDTH // (dp_n * seq_n) == 16
    return jax.shard_map(
        fused_device if fits else generic_device,
        mesh=mesh,
        in_specs=placed,
        out_specs=(
            P("dp", "seq", None),
            P("dp", "seq", None),
            P(),
            P(("dp", "seq"), None),
            P(("dp", "seq"), None),
            P(("dp", "seq"), None),
            P(("dp", "seq"), None),
            P(("dp", "seq"), None),
            P(("dp", "seq"), None),
            P(("dp", "seq"), None),
            P(("dp", "seq"), None),
            P(("dp", "seq"), None),
            P(("dp", "seq"), None),
            P(("dp", "seq"), None),
            P(("dp", "seq"), None),
            P(None, ("dp", "seq")),
            P(None, ("dp", "seq")),
            P(None, ("dp", "seq")),
        ),
        check_vma=False,
    )
```
